128 devices in a mesh: lat: 4 (over z_hi, core), lon: 32 (over x, y, z_lo).
Axes of the slice: x: 4, y: 4, z: 4 (z_hi: 2, z_lo: 2; z = z_hi * 2 + z_lo), core: 2. Of those that a mesh axis runs over, the one named last changes fastest.
Arguments:
- latent: bfloat16 [48, 768, 2, 512], P('lat', 'lon'), may hold values from -8 to 8
- grad_fields: bfloat16 [48, 768, 13, 80], P('lat', 'lon'), may hold values from -6 to 6
- region_ids: int32 [48, 768], P('lat', 'lon'), may hold values from 0 to 2
- level_ids: int32 [13], replicated, may hold values from 0 to 36
- w_qkv: bfloat16 [512, 1536], replicated, may hold values from -0.25 to 0.25
- w_proj: bfloat16 [512, 512], replicated, may hold values from -0.25 to 0.25
- gain: float32 [512], replicated, may hold values from 0.5 to 1.5
- level_table: bfloat16 [37, 512], replicated, may hold values from -6 to 6
- w_key: bfloat16 [512, 512], replicated, may hold values from -0.25 to 0.25
- w_value: bfloat16 [512, 512], replicated, may hold values from -0.25 to 0.25
- w_out: bfloat16 [512, 80], replicated, may hold values from -0.25 to 0.25
Outputs:
- d_latent: bfloat16 [48, 768, 2, 512], P('lat', 'lon')
- grad_qkv: float32 [512, 1536], replicated
- grad_proj: float32 [512, 512], replicated
- grad_gain: float32 [512], replicated
- grad_table: float32 [37, 512], replicated
- grad_key: float32 [512, 512], replicated
- grad_value: float32 [512, 512], replicated
- grad_out: float32 [512, 80], replicated
The draws below stay inside these ranges and needn't reach their ends.
All inputs are finite; a program needn't handle non-finite values.
Results may differ from the reference program's by a relative error of at most 0.024.
The reference program's roundings to bfloat16 on the way count: a program that leaves them out, or rounds other values in their place, can miss the bound.
Values may be sent and summed in bfloat16 or wider, within the bound.
No kernel may reach another device: no remote copies, remote signals or barrier semaphores. Data moves between devices by JAX's collectives and lax.ppermute only.
A program may use at most 128 MiB of HBM per device.

```python
import jax
import jax.numpy as jnp
from jax import lax

D = 512
HEADS = 8
WH = 6
WW = 12
LEVELS = 13
LV = 2
LEVTAB = 37
SH = 3
SW = 6
PIX = 80
NH = 48
NW = 768


def draw_latent(key, part):
    key = jax.random.fold_in(key, 11)
    values = jax.random.normal(key, (NH, NW, LV, D), jnp.float32)
    return jnp.clip(values, -8.0, 8.0).astype(jnp.bfloat16)


def set_ends(values, own_key, low, top_value):
    place = [jax.random.randint(jax.random.fold_in(own_key, axis), (), 0, length) for axis, length in enumerate(values.shape)]
    main_axis = values.shape.index(max(values.shape))
    next_to = place[:main_axis] + [(place[main_axis] + 1) % values.shape[main_axis]] + place[main_axis + 1:]
    return values.at[tuple(place)].set(low).at[tuple(next_to)].set(top_value)


def steps_of(stream_key, dims, cuts, low, top_value):
    factor_of, own = 1.0, jax.random.fold_in(stream_key, 6)
    for axis_at, shards_of in cuts:
        draws = jnp.exp(jax.random.uniform(jax.random.fold_in(own, axis_at), (shards_of,), jnp.float32, low / len(cuts), top_value / len(cuts)))
        factor_of = factor_of * jnp.repeat(draws, dims[axis_at] // shards_of).reshape([-1 if axis == axis_at else 1 for axis in range(len(dims))])
    return factor_of


def gaussian(key, shape, spread, most, split=(), kind=jnp.bfloat16):
    drawn = jax.random.normal(key, shape, jnp.float32) * spread
    if len(split) > 0:
        drawn = steps_of(key, shape, split, -0.22, 0.18) * drawn
    return jnp.clip(drawn, min=-most, max=most).astype(kind)


def setup_inputs(seed: int = 0) -> dict:
    keys = jax.random.split(jax.random.key(seed), 12)
    return {
        "latent": draw_latent(jax.random.fold_in(keys[11], 71), 0),
        "grad_fields": gaussian(keys[1], (NH, NW, LEVELS, PIX), 1.0, 6.0, ((0, 4), (1, 32))),
        "region_ids": set_ends(jax.random.randint(keys[2], (NH, NW), 0, 3), jax.random.fold_in(keys[2], 1), 0, 2).astype(jnp.int32),
        "level_ids": set_ends(jax.random.randint(keys[3], (LEVELS,), 0, LEVTAB), jax.random.fold_in(keys[3], 1), 0, LEVTAB - 1).astype(jnp.int32),
        "w_qkv": gaussian(keys[4], (D, 3 * D), D ** -0.5, 0.25),
        "w_proj": gaussian(keys[5], (D, D), D ** -0.5, 0.25),
        "gain": jnp.clip(1.0 + 0.1 * jax.random.normal(keys[6], (D,), jnp.float32), 0.5, 1.5),
        "level_table": gaussian(keys[7], (LEVTAB, D), 1.0, 6.0),
        "w_key": gaussian(keys[8], (D, D), D ** -0.5, 0.25),
        "w_value": gaussian(keys[9], (D, D), D ** -0.5, 0.25),
        "w_out": gaussian(keys[10], (D, PIX), D ** -0.5, 0.25),
    }


EPS = 1e-05
MASKED = -1e+30

def widen(value):
    return lax.optimization_barrier(value).astype(jnp.float32)

def to_windows(lattice):
    height, breadth, depth, features = lattice.shape
    blocks = lattice.reshape(height // WH, WH, breadth // WW, WW, depth, features)
    return blocks.transpose(0, 2, 1, 3, 4, 5).reshape(-1, WH * WW * depth, features)

def from_windows(windowed, height, breadth):
    features = windowed.shape[-1]
    blocks = windowed.reshape(height // WH, breadth // WW, WH, WW, LV, features)
    return blocks.transpose(0, 2, 1, 3, 4, 5).reshape(height, breadth, LV, features)

def region_mask(labels):
    height, breadth = labels.shape
    blocks = labels.reshape(height // WH, WH, breadth // WW, WW).transpose(0, 2, 1, 3)
    blocks = blocks.reshape(-1, WH * WW)
    tokens_ids = jnp.broadcast_to(blocks[:, :, None], blocks.shape + (LV,)).reshape(blocks.shape[0], -1)
    return tokens_ids[:, :, None] == tokens_ids[:, None, :]

def level_select(level_ids, level_table):
    onehot = (level_ids[:, None] == jnp.arange(level_table.shape[0], dtype=jnp.int32)[None, :]).astype(jnp.float32)
    queries = lax.optimization_barrier(jnp.sum(onehot[:, :, None] * level_table.astype(jnp.float32)[None], axis=1)).astype(jnp.bfloat16)
    return (queries, onehot)

def window_forward(tokens, allowed, w_qkv, w_proj, gain):
    windows, length, features = tokens.shape
    head_size = features // HEADS
    scale = head_size ** (-0.5)
    packed = jnp.dot(tokens.reshape(-1, features), w_qkv, preferred_element_type=jnp.float32)
    packed = packed.astype(jnp.bfloat16).reshape(windows, length, 3, HEADS, head_size)
    query_part = widen(packed[:, :, 0])
    key_part = widen(packed[:, :, 1])
    value_part = widen(packed[:, :, 2])
    scores = jnp.einsum('nihe,njhe->nhij', query_part, key_part) * scale
    scores = jnp.where(allowed[:, None], scores, MASKED)
    largest = lax.optimization_barrier(jnp.max(scores, axis=-1, keepdims=True))
    powers = jnp.exp(scores - largest)
    weights = powers / lax.optimization_barrier(jnp.sum(powers, axis=-1, keepdims=True))
    rounded = weights.astype(jnp.bfloat16)
    attended = jnp.einsum('nhij,njhe->nihe', widen(rounded), value_part).astype(jnp.bfloat16)
    attended = attended.reshape(windows * length, features)
    projected = jnp.dot(attended, w_proj, preferred_element_type=jnp.float32)
    centered = projected - lax.optimization_barrier(jnp.mean(projected, axis=-1, keepdims=True))
    inverse = lax.rsqrt(lax.optimization_barrier(jnp.mean(centered * centered, axis=-1, keepdims=True)) + EPS)
    normed = centered * inverse
    branch = normed * gain
    return (branch.reshape(windows, length, features), (packed, weights, rounded, attended, normed, inverse))

def window_backward(d_branch, tokens, stored, w_qkv, w_proj, gain):
    packed, weights, rounded, attended, normed, inverse = stored
    windows, length, features = tokens.shape
    head_size = features // HEADS
    scale = head_size ** (-0.5)
    d_flat = d_branch.reshape(-1, features)
    grad_gain = lax.optimization_barrier(jnp.sum(d_flat * normed, axis=0))
    d_normed = d_flat * gain
    d_projected = inverse * (d_normed - lax.optimization_barrier(jnp.mean(d_normed, axis=-1, keepdims=True)) - normed * lax.optimization_barrier(jnp.mean(d_normed * normed, axis=-1, keepdims=True)))
    d_projected = d_projected.astype(jnp.bfloat16)
    grad_proj = jnp.dot(attended.T, d_projected, preferred_element_type=jnp.float32)
    d_attended = jnp.dot(d_projected, w_proj.T, preferred_element_type=jnp.float32).astype(jnp.bfloat16)
    d_attended = widen(d_attended.reshape(windows, length, HEADS, head_size))
    query_part = widen(packed[:, :, 0])
    key_part = widen(packed[:, :, 1])
    value_part = widen(packed[:, :, 2])
    d_weights = jnp.einsum('nihe,njhe->nhij', d_attended, value_part)
    d_values = jnp.einsum('nhij,nihe->njhe', widen(rounded), d_attended).astype(jnp.bfloat16)
    d_scores = weights * (d_weights - lax.optimization_barrier(jnp.sum(weights * d_weights, axis=-1, keepdims=True))) * scale
    d_scores = widen(d_scores.astype(jnp.bfloat16))
    d_queries = jnp.einsum('nhij,njhe->nihe', d_scores, key_part).astype(jnp.bfloat16)
    d_keys = jnp.einsum('nhij,nihe->njhe', d_scores, query_part).astype(jnp.bfloat16)
    d_packed = jnp.stack([d_queries, d_keys, d_values], axis=2).reshape(windows * length, 3 * features)
    flat_tokens = tokens.reshape(-1, features)
    grad_qkv = jnp.dot(flat_tokens.T, d_packed, preferred_element_type=jnp.float32)
    d_tokens = jnp.dot(d_packed, w_qkv.T, preferred_element_type=jnp.float32).reshape(windows, length, features)
    return (d_tokens, (grad_qkv, grad_proj, grad_gain))

def decoder_backward(mixed, fields, queries, w_key, w_value, w_out):
    spots, depth, features = mixed.shape
    head_size = features // HEADS
    scale = head_size ** (-0.5)
    flat = mixed.reshape(-1, features)
    keys_dec = jnp.dot(flat, w_key, preferred_element_type=jnp.float32).astype(jnp.bfloat16)
    values_dec = jnp.dot(flat, w_value, preferred_element_type=jnp.float32).astype(jnp.bfloat16)
    keys_wide = widen(keys_dec.reshape(spots, depth, HEADS, head_size))
    values_wide = widen(values_dec.reshape(spots, depth, HEADS, head_size))
    query_heads = widen(queries.reshape(-1, HEADS, head_size))
    scores = jnp.einsum('phe,tlhe->tphl', query_heads, keys_wide) * scale
    largest = lax.optimization_barrier(jnp.max(scores, axis=-1, keepdims=True))
    powers = jnp.exp(scores - largest)
    weights = powers / lax.optimization_barrier(jnp.sum(powers, axis=-1, keepdims=True))
    rounded = widen(weights.astype(jnp.bfloat16))
    outputs = jnp.einsum('tphl,tlhe->tphe', rounded, values_wide).astype(jnp.bfloat16).reshape(-1, features)
    flat_fields = fields.reshape(-1, fields.shape[-1])
    grad_out = jnp.dot(outputs.T, flat_fields, preferred_element_type=jnp.float32)
    d_outputs = jnp.dot(flat_fields, w_out.T, preferred_element_type=jnp.float32).astype(jnp.bfloat16)
    d_outputs = widen(d_outputs.reshape(spots, -1, HEADS, head_size))
    d_weights = jnp.einsum('tphe,tlhe->tphl', d_outputs, values_wide)
    d_values = jnp.einsum('tphl,tphe->tlhe', rounded, d_outputs).astype(jnp.bfloat16)
    d_scores = weights * (d_weights - lax.optimization_barrier(jnp.sum(weights * d_weights, axis=-1, keepdims=True))) * scale
    d_scores = widen(d_scores.astype(jnp.bfloat16))
    d_query = jnp.einsum('tphl,tlhe->phe', d_scores, keys_wide).reshape(-1, features)
    d_keys = jnp.einsum('tphl,phe->tlhe', d_scores, query_heads).astype(jnp.bfloat16)
    d_keys_flat = d_keys.reshape(-1, features)
    d_values_flat = d_values.reshape(-1, features)
    d_mixed = (jnp.dot(d_keys_flat, w_key.T, preferred_element_type=jnp.float32) + jnp.dot(d_values_flat, w_value.T, preferred_element_type=jnp.float32)).astype(jnp.bfloat16)
    grad_key = jnp.dot(flat.T, d_keys_flat, preferred_element_type=jnp.float32)
    grad_value = jnp.dot(flat.T, d_values_flat, preferred_element_type=jnp.float32)
    return (d_mixed.reshape(spots, depth, features), (d_query, grad_key, grad_value, grad_out))

def tile_backward(tokens_tile, fields_tile, labels_tile, queries, w_qkv, w_proj, gain, w_key, w_value, w_out):
    height, breadth = (tokens_tile.shape[0], tokens_tile.shape[1])
    allowed = region_mask(labels_tile)
    windows = to_windows(tokens_tile)
    branch, stored = window_forward(windows, allowed, w_qkv, w_proj, gain)
    mixed = (tokens_tile.astype(jnp.float32) + from_windows(branch, height, breadth)).astype(jnp.bfloat16)
    d_mixed, dec_grads = decoder_backward(mixed.reshape(-1, LV, D), fields_tile.reshape(-1, LEVELS, PIX), queries, w_key, w_value, w_out)
    d_wide = widen(d_mixed.reshape(height, breadth, LV, D))
    d_tokens, swin_grads = window_backward(to_windows(d_wide), windows, stored, w_qkv, w_proj, gain)
    d_total = d_wide + from_windows(d_tokens, height, breadth)
    return (d_total, swin_grads + dec_grads)

def reference(latent, grad_fields, region_ids, level_ids, w_qkv, w_proj, gain, level_table, w_key, w_value, w_out):
    shifted = jnp.roll(latent, (-SH, -SW), axis=(0, 1))
    fields = jnp.roll(grad_fields, (-SH, -SW), axis=(0, 1))
    queries, onehot = level_select(level_ids, level_table)
    bands = NH // WH
    band_tokens = shifted.reshape(bands, WH, NW, LV, D)
    band_fields = fields.reshape(bands, WH, NW, LEVELS, PIX)
    band_labels = region_ids.reshape(bands, WH, NW)

    def one_band(totals, items):
        tokens_band, fields_band, labels_band = items
        d_total, grads = tile_backward(tokens_band, fields_band, labels_band, queries, w_qkv, w_proj, gain, w_key, w_value, w_out)
        return (tuple((left + right for left, right in zip(totals, grads))), d_total)
    initial = (jnp.zeros((D, 3 * D), jnp.float32), jnp.zeros((D, D), jnp.float32), jnp.zeros((D,), jnp.float32), jnp.zeros((LEVELS, D), jnp.float32), jnp.zeros((D, D), jnp.float32), jnp.zeros((D, D), jnp.float32), jnp.zeros((D, PIX), jnp.float32))
    totals, d_bands = lax.scan(one_band, initial, (band_tokens, band_fields, band_labels))
    d_latent = jnp.roll(d_bands.reshape(NH, NW, LV, D), (SH, SW), axis=(0, 1)).astype(jnp.bfloat16)
    grad_qkv, grad_proj, grad_gain, d_query, grad_key, grad_value, grad_out = totals
    grad_table = lax.optimization_barrier(jnp.sum(onehot[:, :, None] * d_query[:, None, :], axis=0))
    return (d_latent, grad_qkv, grad_proj, grad_gain, grad_table, grad_key, grad_value, grad_out)
```

```python
import functools
import jax
import jax.numpy as jnp
from jax import lax
from jax.experimental import pallas as pl
from jax.experimental.pallas import tpu as pltpu

HEADS = 8
WH = 6
WW = 12
LV = 2
SH = 3
SW = 6
EPS = 1e-05
MASKED = -1e30
F32 = jnp.float32
BF16 = jnp.bfloat16


def dot_nn(a, b):
    return lax.dot_general(a, b, (((1,), (0,)), ((), ())), preferred_element_type=F32)


def dot_nt(a, b):
    return lax.dot_general(a, b, (((1,), (1,)), ((), ())), preferred_element_type=F32)


def dot_tn(a, b):
    return lax.dot_general(a, b, (((0,), (0,)), ((), ())), preferred_element_type=F32)


def swap_rows(a):
    rows, lanes = a.shape
    blocks = a.reshape(rows // 8, 8, lanes)
    later = pltpu.roll(blocks, 7, 1)
    earlier = pltpu.roll(blocks, 1, 1)
    even = lax.broadcasted_iota(jnp.int32, blocks.shape, 1) % 2 == 0
    return jnp.where(even, later, earlier).reshape(rows, lanes)


def section_kernel(
    core_ref, x_ref, f_ref, idc_ref, idr_ref, q_ref, wqkv_ref, wproj_ref, gain_ref, wkey_ref, wval_ref, wout_ref,
    out_ref, grads_ref,
    xw32, xw, pk, probs, at, nrm, inv, mix32, mixb, kk, vv, uu, ww, cc, ds, gg, dkd, dvd, dm32, dp32, dpb, dat, dpk, hs,
):
    n_win = 4
    tok = 144
    rows = 576
    core = core_ref[0, 0]

    def put(half_no, block, matrix):
        for c in range(matrix.shape[1] // 128):
            at_row = 512 * (block + c)
            piece = matrix[:, 128 * c:128 * c + 128].astype(BF16)
            grads_ref[half_no ^ core, at_row:at_row + 512, :] = piece

    lane = lax.broadcasted_iota(jnp.int32, (1, 128), 1)
    half = ((lane < 64).astype(BF16), (lane >= 64).astype(BF16))
    low = lax.broadcasted_iota(jnp.int32, (tok, 128), 1) < 64
    gain = gain_ref[...]

    for h in range(12):
        piece = x_ref[48 * h:48 * h + 48, :].astype(F32)
        for b in range(2):
            xw32[(h // 6) * 2 + b, 24 * (h % 6):24 * (h % 6) + 24, :] = piece[24 * b:24 * b + 24]
    for w in range(n_win):
        xw[w] = xw32[w].astype(BF16)
    flat_x = xw[...].reshape(rows, 512)
    for n in range(6):
        part = dot_nn(flat_x, wqkv_ref[:, 256 * n:256 * n + 256]).astype(BF16)
        pk[:, :, 256 * n:256 * n + 256] = part.reshape(n_win, tok, 256)

    def attend(w, carry):
        bias = jnp.where(idc_ref[w] == idr_ref[w], 0.0, MASKED)
        for hp in range(4):
            q = pk[w, :, 128 * hp:128 * hp + 128]
            k = pk[w, :, 512 + 128 * hp:512 + 128 * hp + 128]
            v = pk[w, :, 1024 + 128 * hp:1024 + 128 * hp + 128]
            outs = []
            for e in range(2):
                s = dot_nt(q * half[e], k) * 0.125 + bias
                p = jnp.exp(s - jnp.max(s, axis=-1, keepdims=True))
                p = p / jnp.sum(p, axis=-1, keepdims=True)
                probs[w, 2 * hp + e] = p
                outs.append(dot_nn(p.astype(BF16), v))
            at[w, :, 128 * hp:128 * hp + 128] = jnp.where(low, outs[0], outs[1]).astype(BF16)
        return carry

    lax.fori_loop(0, n_win, attend, 0)

    flat_at = at[...].reshape(rows, 512)
    nrm[...] = dot_nn(flat_at, wproj_ref[...]).reshape(n_win, tok, 512)
    for w in range(n_win):
        for i in range(6):
            at_row = 48 * (6 * (w // 2) + i) + 24 * (w % 2)
            p = nrm[w, 24 * i:24 * i + 24, :]
            c = p - jnp.mean(p, axis=-1, keepdims=True)
            r = lax.rsqrt(jnp.mean(c * c, axis=-1, keepdims=True) + EPS)
            n = c * r
            nrm[w, 24 * i:24 * i + 24, :] = n
            inv[w, 24 * i:24 * i + 24, :] = jnp.broadcast_to(r, (24, 128))
            mix32[at_row:at_row + 24, :] = xw32[w, 24 * i:24 * i + 24, :] + n * gain
    mixb[...] = mix32[...].astype(BF16)

    mixed = mixb[...]
    for hp in range(4):
        cols = slice(128 * hp, 128 * hp + 128)
        for w_ref, pair in ((wkey_ref, kk), (wval_ref, vv)):
            part = dot_nn(mixed, w_ref[:, cols]).astype(BF16)
            other = swap_rows(part.astype(F32))
            pair[hp, :, 0:128] = part
            pair[hp, :, 128:256] = (-other).astype(BF16)

    row16 = lax.broadcasted_iota(jnp.int32, (16, 128), 0)
    lane16 = lax.broadcasted_iota(jnp.int32, (16, 128), 1)
    own = (row16 // 2 == lane16 % 8).astype(F32)[None]
    zero64 = jnp.zeros((64, 128), BF16)
    for hp in range(4):
        cols = slice(128 * hp, 128 * hp + 128)
        q = q_ref[:, cols] * jnp.asarray(0.125, BF16)
        q_e, q_o = q * half[0], q * half[1]
        rhs = jnp.concatenate(
            [jnp.concatenate([q_e, q_e], axis=1), jnp.concatenate([q_o, q_o], axis=1)], axis=0
        )
        diff = dot_nt(kk[hp], rhs)
        wo = wout_ref[cols, :]
        top = jnp.concatenate(
            [jnp.concatenate([wo[:64], zero64], axis=0), jnp.concatenate([zero64, wo[64:]], axis=0)], axis=1
        )
        u = dot_nn(vv[hp], jnp.concatenate([top, top], axis=0)).astype(BF16)
        for e in range(2):
            d = diff[:, 128 * e:128 * e + 128].reshape(36, 16, 128)
            small = jnp.exp(-jnp.abs(d))
            big = 1.0 / (1.0 + small)
            small = small * big
            weight = jnp.where(d >= 0, big, small)
            ww[2 * hp + e] = (weight * own).astype(BF16).reshape(rows, 128)
            cc[2 * hp + e] = (small * big * (own * 0.125)).reshape(rows, 128)
            uu[2 * hp + e] = u[:, 128 * e:128 * e + 128]

    def group(h, carry):
        line = f_ref[h].astype(F32)
        for o in range(3):
            g16 = pl.ds(pl.multiple_of(48 * h + 16 * o, 16), 16)
            f = line[:, 8 * o:8 * o + 8, :].reshape(104, 128)
            f = jnp.concatenate([f, jnp.zeros((24, 128), F32)], axis=0).astype(BF16)
            dw = dot_nt(uu[:, g16, :].reshape(128, 128), f)
            d = (dw * cc[:, g16, :].reshape(128, 128)).astype(BF16)
            ds[:, g16, :] = d.reshape(8, 16, 128)
            g = dot_nn(ww[:, g16, :].reshape(128, 128), f).astype(BF16)
            gg[:, g16, :] = g.reshape(8, 16, 128)
        return carry

    lax.fori_loop(0, 12, group, 0)

    fold_row = lax.broadcasted_iota(jnp.int32, (128, 128), 0)
    fold_lane = lax.broadcasted_iota(jnp.int32, (128, 128), 1)
    fold = (fold_row // 8 == fold_lane - 80).astype(BF16)
    for hp in range(4):
        cols = slice(128 * hp, 128 * hp + 128)
        q = q_ref[:, cols]
        d = jnp.concatenate([ds[2 * hp], ds[2 * hp + 1]], axis=1)
        g = jnp.concatenate([gg[2 * hp], gg[2 * hp + 1]], axis=1)
        dkd[:, cols] = dot_nn(d, jnp.concatenate([q * half[0], q * half[1]], axis=0)).astype(BF16)
        wo = wout_ref[cols, :]
        top = jnp.concatenate(
            [jnp.concatenate([wo[:64], zero64], axis=0), jnp.concatenate([zero64, wo[64:]], axis=0)], axis=1
        )
        dvd[:, cols] = dot_nt(g, top).astype(BF16)
        dq = dot_tn(kk[hp, :, 0:128], d)
        dq = jnp.concatenate([dq[:64, :128], dq[64:, 128:]], axis=0)
        go = dot_tn(vv[hp, :, 0:128], g)
        go = jnp.concatenate([go[:64, :128], go[64:, 128:]], axis=0)
        dq_hi = dq.astype(BF16)
        dq_lo = (dq - dq_hi.astype(F32)).astype(BF16)
        hs[:, cols] = go + dot_nn(dq_hi, fold) + dot_nn(dq_lo, fold)

    d_mix = dot_nt(dkd[...], wkey_ref[...]) + dot_nt(dvd[...], wval_ref[...])
    dm32[...] = d_mix.astype(BF16).astype(F32)
    put(1, 4, dot_tn(mixed, dkd[...]))
    put(1, 8, dot_tn(mixed, dvd[...]))

    total_gain = jnp.zeros((8, 512), F32)
    for w in range(n_win):
        for i in range(6):
            at_row = 48 * (6 * (w // 2) + i) + 24 * (w % 2)
            g = dm32[at_row:at_row + 24, :]
            n = nrm[w, 24 * i:24 * i + 24, :]
            total_gain = total_gain + jnp.sum((g * n).reshape(3, 8, 512), axis=0)
            gn = g * gain
            m1 = jnp.mean(gn, axis=-1, keepdims=True)
            m2 = jnp.mean(gn * n, axis=-1, keepdims=True)
            r = inv[w, 24 * i:24 * i + 24, 0:1]
            dp32[w, 24 * i:24 * i + 24, :] = r * (gn - m1 - n * m2)
    row_gain = jnp.broadcast_to(jnp.sum(total_gain, axis=0, keepdims=True), (128, 512))
    for hp in range(4):
        cols = slice(128 * hp, 128 * hp + 128)
        column = row_gain[:, cols].T
        lanes = lax.broadcasted_iota(jnp.int32, (128, 128), 1)
        tail = jnp.where(lanes == 96, column, hs[:, cols]).astype(BF16)
        at_row = 6144 + 128 * (hp % 2)
        grads_ref[(hp // 2) ^ core, at_row:at_row + 128, :] = tail
    for half_no in range(2):
        grads_ref[half_no, 6400:6656, :] = jnp.zeros((256, 128), BF16)
    for w in range(n_win):
        dpb[w] = dp32[w].astype(BF16)
    flat_dp = dpb[...].reshape(rows, 512)
    put(1, 0, dot_tn(flat_at, flat_dp))
    dat[...] = dot_nt(flat_dp, wproj_ref[...]).astype(BF16).reshape(n_win, tok, 512)

    def unattend(w, carry):
        for hp in range(4):
            q = pk[w, :, 128 * hp:128 * hp + 128]
            k = pk[w, :, 512 + 128 * hp:512 + 128 * hp + 128]
            v = pk[w, :, 1024 + 128 * hp:1024 + 128 * hp + 128]
            da = dat[w, :, 128 * hp:128 * hp + 128]
            dqs, dks, dvs = [], [], []
            for e in range(2):
                p = probs[w, 2 * hp + e]
                dvs.append(dot_tn(p.astype(BF16), da))
                dw = dot_nt(da * half[e], v)
                s = p * (dw - jnp.sum(p * dw, axis=-1, keepdims=True)) * 0.125
                s = s.astype(BF16)
                dqs.append(dot_nn(s, k))
                dks.append(dot_tn(s, q))
            for at_col, pair in ((0, dqs), (512, dks), (1024, dvs)):
                merged = jnp.where(low, pair[0], pair[1]).astype(BF16)
                dpk[w, :, at_col + 128 * hp:at_col + 128 * hp + 128] = merged
        return carry

    lax.fori_loop(0, n_win, unattend, 0)

    flat_d = dpk[...].reshape(rows, 1536)
    for n in range(3):
        put(0, 4 * n, dot_tn(flat_x, flat_d[:, 512 * n:512 * n + 512]))
    dp32[...] = dot_nt(flat_d, wqkv_ref[...]).reshape(n_win, tok, 512)
    for h in range(12):
        parts = []
        for b in range(2):
            at_row = 48 * h + 24 * b
            parts.append(
                dp32[(h // 6) * 2 + b, 24 * (h % 6):24 * (h % 6) + 24, :] + dm32[at_row:at_row + 24, :]
            )
        out_ref[48 * h:48 * h + 48, :] = jnp.concatenate(parts, axis=0).astype(BF16)


def section(core, x, fields, ids, q128, w_qkv, w_proj, gain, w_key, w_value, w_out):
    vm = lambda shape, kind: pltpu.VMEM(shape, kind)
    scratch = [
        vm((4, 144, 512), F32), vm((4, 144, 512), BF16), vm((4, 144, 1536), BF16), vm((4, 8, 144, 144), F32),
        vm((4, 144, 512), BF16), vm((4, 144, 512), F32), vm((4, 144, 128), F32), vm((576, 512), F32),
        vm((576, 512), BF16), vm((4, 576, 256), BF16), vm((4, 576, 256), BF16), vm((8, 576, 128), BF16),
        vm((8, 576, 128), BF16), vm((8, 576, 128), F32), vm((8, 576, 128), BF16), vm((8, 576, 128), BF16),
        vm((576, 512), BF16), vm((576, 512), BF16), vm((576, 512), F32), vm((4, 144, 512), F32),
        vm((4, 144, 512), BF16), vm((4, 144, 512), BF16), vm((4, 144, 1536), BF16), vm((128, 512), F32),
    ]
    return pl.pallas_call(
        section_kernel,
        out_shape=(jax.ShapeDtypeStruct((576, 512), BF16), jax.ShapeDtypeStruct((2, 6656, 128), BF16)),
        in_specs=[pl.BlockSpec(memory_space=pltpu.SMEM)] + [pl.BlockSpec(memory_space=pltpu.VMEM)] * 11,
        out_specs=[pl.BlockSpec(memory_space=pltpu.VMEM)] * 2,
        scratch_shapes=scratch,
        compiler_params=pltpu.CompilerParams(vmem_limit_bytes=56 * 1024 * 1024),
        cost_estimate=pl.CostEstimate(flops=15_000_000_000, bytes_accessed=12_000_000, transcendentals=2_000_000),
        name="section",
    )(core, x, fields, ids[:, :, None], ids[:, None, :], q128, w_qkv, w_proj, gain[None], w_key, w_value, w_out)


from jax.sharding import Mesh, PartitionSpec as P

LAT = ("z_hi", "core")
LON = ("x", "y", "z_lo")
CHIPS = ("z_hi", "x", "y", "z_lo")


def neighbours(axes, by):
    count = 1
    for axis in axes:
        count *= lax.axis_size(axis)
    return [(i, (i + by) % count) for i in range(count)]


def corner_pairs(by):
    n_lat, n_lon = 4, 32
    return [
        (a * n_lon + b, ((a + by) % n_lat) * n_lon + (b + by) % n_lon) for a in range(n_lat) for b in range(n_lon)
    ]


def fetch(tile, lat_axis, lon_axis):
    h, w = tile.shape[lat_axis], tile.shape[lon_axis]
    first = lax.slice_in_dim(tile, 0, SH, axis=lat_axis)
    rest = lax.slice_in_dim(tile, SH, h, axis=lat_axis)
    below = lax.ppermute(lax.slice_in_dim(first, SW, w, axis=lon_axis), LAT, neighbours(LAT, -1))
    right = lax.ppermute(lax.slice_in_dim(rest, 0, SW, axis=lon_axis), LON, neighbours(LON, -1))
    corner = lax.ppermute(lax.slice_in_dim(first, 0, SW, axis=lon_axis), LAT + LON, corner_pairs(-1))
    inner = lax.slice_in_dim(rest, SW, w, axis=lon_axis)
    return lax.concatenate(
        [lax.concatenate([inner, right], lon_axis), lax.concatenate([below, corner], lon_axis)], lat_axis
    )


def send_back(tile):
    h, w = tile.shape[0], tile.shape[1]
    above = lax.ppermute(tile[h - SH:, :w - SW], LAT, neighbours(LAT, 1))
    left = lax.ppermute(tile[:h - SH, w - SW:], LON, neighbours(LON, 1))
    corner = lax.ppermute(tile[h - SH:, w - SW:], LAT + LON, corner_pairs(1))
    top = jnp.concatenate([corner, above], axis=1)
    bottom = jnp.concatenate([left, tile[:h - SH, :w - SW]], axis=1)
    return jnp.concatenate([top, bottom], axis=0)


def sum_all(grads, core):
    swap = [(0, 1), (1, 0)]
    other = lax.ppermute(grads[1], "core", swap)
    mine = (grads[0].astype(F32) + other.astype(F32)).astype(BF16)
    pieces = lax.all_to_all(mine.reshape(64, 104, 128), CHIPS, split_axis=0, concat_axis=0, tiled=True)
    piece = jnp.sum(pieces.astype(F32), axis=0).astype(BF16)
    spread = jnp.broadcast_to(piece[None], (64, 104, 128))
    mine = lax.all_to_all(spread, CHIPS, split_axis=0, concat_axis=0, tiled=True).reshape(6656, 128)
    other = lax.ppermute(mine, "core", swap)
    first = core == 0
    return jnp.where(first, mine, other), jnp.where(first, other, mine)


def matrix(blocks):
    return blocks.reshape(-1, 512, 128).transpose(1, 0, 2).reshape(512, -1).astype(F32)


def shards(
    latent, grad_fields, region_ids, level_ids, w_qkv, w_proj, gain, level_table, w_key, w_value, w_out
):
    core = lax.axis_index("core")
    tokens = fetch(latent, 0, 1)
    fields = fetch(grad_fields.transpose(0, 2, 1, 3), 0, 2)
    x = tokens.reshape(576, 512)
    f = jnp.pad(fields, ((0, 0), (0, 0), (0, 0), (0, 48)))
    ids = region_ids.reshape(2, 6, 2, 12).transpose(0, 2, 1, 3).reshape(4, 72)
    ids = jnp.repeat(ids, 2, axis=1)
    onehot = (level_ids[:, None] == jnp.arange(37, dtype=jnp.int32)[None, :]).astype(F32)
    q = jnp.sum(onehot[:, :, None] * level_table.astype(F32)[None], axis=1).astype(BF16)
    q128 = jnp.pad(jnp.repeat(q, 8, axis=0), ((0, 24), (0, 0)))
    out, grads = section(
        core.reshape(1, 1), x, f, ids, q128, w_qkv, w_proj, gain, w_key, w_value, jnp.pad(w_out, ((0, 0), (0, 48)))
    )
    d_latent = send_back(out.reshape(12, 24, 2, 512))
    lower, upper = sum_all(grads, core)
    tail = jnp.concatenate([lower[6144:6400], upper[6144:6400]], axis=0).astype(F32)
    d_query = tail[:, 80:93].T
    grad_table = jnp.sum(onehot[:, :, None] * d_query[:, None, :], axis=0)
    return (
        d_latent, matrix(lower[:6144]), matrix(upper[:2048]), tail[:, 96], grad_table, matrix(upper[2048:4096]),
        matrix(upper[4096:6144]), tail[:, :80],
    )


def solution(mesh):
    fine = Mesh(mesh.devices.reshape(2, 2, 4, 4, 2), LAT + LON)
    tile = P(LAT, LON, None, None)
    return jax.shard_map(
        shards,
        mesh=fine,
        in_specs=(tile, tile, P(LAT, LON)) + (P(),) * 8,
        out_specs=(tile,) + (P(),) * 7,
        check_vma=False,
    )
```

```python
import functools
import jax
import jax.numpy as jnp
from jax import lax
from jax.experimental import pallas as pl
from jax.experimental.pallas import tpu as pltpu

HEADS = 8
WH = 6
WW = 12
LV = 2
SH = 3
SW = 6
EPS = 1e-05
MASKED = -1e30
F32 = jnp.float32
BF16 = jnp.bfloat16


def dot_nn(a, b):
    return lax.dot_general(a, b, (((1,), (0,)), ((), ())), preferred_element_type=F32)


def dot_nt(a, b):
    return lax.dot_general(a, b, (((1,), (1,)), ((), ())), preferred_element_type=F32)


def dot_tn(a, b):
    return lax.dot_general(a, b, (((0,), (0,)), ((), ())), preferred_element_type=F32)


def swap_rows(a):
    rows, lanes = a.shape
    blocks = a.reshape(rows // 8, 8, lanes)
    later = pltpu.roll(blocks, 7, 1)
    earlier = pltpu.roll(blocks, 1, 1)
    even = lax.broadcasted_iota(jnp.int32, blocks.shape, 1) % 2 == 0
    return jnp.where(even, later, earlier).reshape(rows, lanes)


def nine_tiles(levels):
    lane = lax.broadcasted_iota(jnp.int32, levels.shape[1:], 1)
    tiles = [levels[p] for p in range(9)]
    for m in range(4):
        extra = levels[9 + m]
        tiles[2 * m] = jnp.where(lane < 80, tiles[2 * m], pltpu.roll(extra, 80, 1))
        tiles[2 * m + 1] = jnp.where(lane < 80, tiles[2 * m + 1], pltpu.roll(extra, 32, 1))
    return jnp.stack(tiles, axis=0)


def all_levels(tiles):
    lane = lax.broadcasted_iota(jnp.int32, tiles.shape[1:], 1)
    levels = [tiles[p] for p in range(9)]
    for m in range(4):
        levels.append(
            jnp.where(lane < 48, pltpu.roll(tiles[2 * m], 48, 1), pltpu.roll(tiles[2 * m + 1], 96, 1))
        )
    return jnp.stack(levels, axis=0)[:, :, :80]


def pack_kernel(x_ref, f_ref, below_ref, right_ref, corner_ref, wide):
    for c in range(4):
        cols = slice(128 * c, 128 * c + 128)
        below_ref[144 * c:144 * c + 144, :] = x_ref[0:144, cols]
        for h in range(3):
            corner_ref[16 * (3 * c + h):16 * (3 * c + h) + 16, :] = x_ref[48 * h:48 * h + 16, cols]
        for h in range(9):
            right_ref[16 * (9 * c + h):16 * (9 * c + h) + 16, :] = x_ref[48 * (h + 3):48 * (h + 3) + 16, cols]
    lines, sides = [], []
    for h in range(12):
        wide[h, :, :, 0:80] = f_ref[h].astype(F32)
        if h < 3:
            lines.append(nine_tiles(wide[h]).reshape(216, 128))
        sides.append(nine_tiles(wide[h, :, 0:8, :]).reshape(72, 128))
    below_ref[576:1224, :] = jnp.concatenate(lines, axis=0).astype(BF16)
    right_ref[576:1224, :] = jnp.concatenate(sides[3:], axis=0).astype(BF16)
    corner_ref[192:408, :] = jnp.concatenate(sides[:3], axis=0).astype(BF16)


def pack(x, fields):
    vmem = pl.BlockSpec(memory_space=pltpu.VMEM)
    return pl.pallas_call(
        pack_kernel,
        out_shape=tuple(jax.ShapeDtypeStruct((rows, 128), BF16) for rows in (1224, 1224, 408)),
        in_specs=[vmem, vmem],
        out_specs=[vmem] * 3,
        scratch_shapes=[pltpu.VMEM((12, 13, 24, 128), F32)],
        compiler_params=pltpu.CompilerParams(vmem_limit_bytes=16 * 1024 * 1024),
        cost_estimate=pl.CostEstimate(flops=2_000_000, bytes_accessed=3_000_000, transcendentals=0),
        name="pack",
    )(x, fields)


def section_kernel(
    core_ref, level_ref, x_ref, below_ref, right_ref, corner_ref, ids_ref, table_ref, gain_ref, wout_ref,
    wqkv_hbm, wproj_hbm, wkey_hbm, wval_hbm, f_hbm,
    out_hbm, keep_hbm, send_hbm,
    xw32, xw, pk, probs, at, nrm, inv, mix32, mixb, kk, vv, uu, ww, cc, ds, gg, dkd, dvd, dm32, dp32, dpb, dat, dpk, hs, at_t, x_t, hot, q32, qs, wo128, f_below, f_right, f_corner,
    wqkv_ref, wproj_ref, wkey_ref, wval_ref, f_ref, out_ref, grads_ref, in_sem, out_sem,
):
    n_win = 4
    tok = 144
    rows = 576
    core = core_ref[0, 0]
    loads = [
        pltpu.make_async_copy(source, target, in_sem.at[n])
        for n, (source, target) in enumerate(
            (
                (wqkv_hbm, wqkv_ref), (wproj_hbm, wproj_ref), (wkey_hbm, wkey_ref), (wval_hbm, wval_ref),
                (f_hbm, f_ref),
            )
        )
    ]
    for load in loads:
        load.start()

    def put(half_no, block, matrix):
        for c in range(matrix.shape[1] // 128):
            at_row = 512 * (block + c)
            piece = matrix[:, 128 * c:128 * c + 128].astype(BF16)
            grads_ref[half_no ^ core, at_row:at_row + 512, :] = piece

    lane = lax.broadcasted_iota(jnp.int32, (1, 128), 1)
    half = ((lane < 64).astype(BF16), (lane >= 64).astype(BF16))
    eighth = (half[0] * jnp.asarray(0.125, BF16), half[1] * jnp.asarray(0.125, BF16))
    low = lax.broadcasted_iota(jnp.int32, (tok, 128), 1) < 64
    gain = gain_ref[...]

    wide = table_ref[...].astype(F32)
    table_row = lax.broadcasted_iota(jnp.int32, wide.shape, 0)
    for p in range(13):
        q32[8 * p:8 * p + 8, :] = jnp.broadcast_to(
            jnp.sum(jnp.where(table_row == level_ref[p], wide, 0.0), axis=0, keepdims=True), (8, 512)
        )
    q32[104:128, :] = jnp.zeros((24, 512), F32)
    qs[...] = q32[...].astype(BF16)
    wo128[...] = jnp.zeros((512, 128), BF16)
    wo128[:, 0:80] = wout_ref[...].T

    ids = ids_ref[...].astype(F32)
    token = lax.broadcasted_iota(jnp.int32, (tok, 24), 0)
    spot = lax.broadcasted_iota(jnp.int32, (tok, 24), 1)
    tok12 = lax.broadcasted_iota(jnp.int32, (tok, 12), 0)
    row12 = lax.broadcasted_iota(jnp.int32, (tok, 12), 1)
    kind = lax.broadcasted_iota(jnp.int32, (tok, 128), 1).astype(F32)
    for w in range(n_win):
        pick = (tok12 // 24 + 6 * (w // 2) == row12).astype(F32)
        line = dot_nn(pick, ids)
        own_id = jnp.sum(
            jnp.where(spot == 12 * (w % 2) + (token % 24) // 2, line, 0.0), axis=1, keepdims=True
        )
        hot[w] = (own_id == kind).astype(BF16)

    f_below[...] = below_ref[576:1224, :].astype(F32).reshape(3, 9, 24, 128)
    f_right[...] = right_ref[576:1224, :].astype(F32).reshape(9, 9, 8, 128)
    f_corner[...] = corner_ref[192:408, :].astype(F32).reshape(3, 9, 8, 128)
    row8 = lax.broadcasted_iota(jnp.int32, (8, 128), 0)
    for h in range(12):
        for c in range(4):
            cols = slice(128 * c, 128 * c + 128)
            if h < 9:
                main = x_ref[48 * (h + 3):48 * (h + 3) + 48, cols]
                side = right_ref[16 * (9 * c + h):16 * (9 * c + h) + 16, :]
            else:
                main = below_ref[144 * c + 48 * (h - 9):144 * c + 48 * (h - 9) + 48, :]
                side = corner_ref[16 * (3 * c + h - 9):16 * (3 * c + h - 9) + 16, :]
            line = jnp.concatenate([main.astype(F32), side.astype(F32)], axis=0)
            turned = [pltpu.roll(line[8 * n:8 * n + 8], 4, 0) for n in range(1, 8)]
            piece = [jnp.where(row8 < 4, turned[n], turned[n + 1]) for n in range(6)]
            for b in range(2):
                xw32[(h // 6) * 2 + b, 24 * (h % 6):24 * (h % 6) + 24, cols] = jnp.concatenate(
                    piece[3 * b:3 * b + 3], axis=0
                )
    for w in range(n_win):
        xw[w] = xw32[w].astype(BF16)
    flat_x = xw[...].reshape(rows, 512)
    loads[0].wait()
    x_t[...] = flat_x.T
    for n in range(6):
        part = dot_nn(flat_x, wqkv_ref[:, 256 * n:256 * n + 256]).astype(BF16)
        pk[:, :, 256 * n:256 * n + 256] = part.reshape(n_win, tok, 256)

    def attend(w, carry):
        same = dot_nt(hot[w], hot[w])
        bias = (same - 1.0) * -MASKED
        for hp in range(4):
            cols = slice(128 * hp, 128 * hp + 128)
            q = pk[w, :, 128 * hp:128 * hp + 128]
            k = pk[w, :, 512 + 128 * hp:512 + 128 * hp + 128]
            v_t = pk[w, :, 1024 + 128 * hp:1024 + 128 * hp + 128].T
            outs = []
            both = dot_nt(jnp.concatenate([k * eighth[0], k * eighth[1]], axis=0), q)
            for e in range(2):
                s = both[tok * e:tok * e + tok] + bias
                p = jnp.exp(s - jnp.max(s, axis=0, keepdims=True))
                p = p * (1.0 / jnp.sum(p, axis=0, keepdims=True))
                probs[w, 2 * hp + e] = p
                outs.append(dot_nn(v_t[64 * e:64 * e + 64], p.astype(BF16)))
            o_t = jnp.concatenate(outs, axis=0).astype(BF16)
            at_t[w, cols, :] = o_t
            at[w, :, cols] = o_t.T
        return carry

    lax.fori_loop(0, n_win, attend, 0)

    flat_at = at[...].reshape(rows, 512)
    loads[1].wait()
    nrm[...] = dot_nn(flat_at, wproj_ref[...]).reshape(n_win, tok, 512)
    for w in range(n_win):
        for i in range(6):
            at_row = 48 * (6 * (w // 2) + i) + 24 * (w % 2)
            p = nrm[w, 24 * i:24 * i + 24, :]
            c = p - jnp.mean(p, axis=-1, keepdims=True)
            r = lax.rsqrt(jnp.mean(c * c, axis=-1, keepdims=True) + EPS)
            n = c * r
            nrm[w, 24 * i:24 * i + 24, :] = n
            inv[w, 24 * i:24 * i + 24, :] = jnp.broadcast_to(r, (24, 128))
            mix32[at_row:at_row + 24, :] = xw32[w, 24 * i:24 * i + 24, :] + n * gain
    mixb[...] = mix32[...].astype(BF16)

    mixed = mixb[...]
    for load in loads[2:]:
        load.wait()
    for hp in range(4):
        cols = slice(128 * hp, 128 * hp + 128)
        for w_ref, pair in ((wkey_ref, kk), (wval_ref, vv)):
            part = dot_nn(mixed, w_ref[:, cols]).astype(BF16)
            other = swap_rows(part.astype(F32))
            pair[hp, :, 0:128] = part
            pair[hp, :, 128:256] = (-other).astype(BF16)

    row16 = lax.broadcasted_iota(jnp.int32, (16, 128), 0)
    lane16 = lax.broadcasted_iota(jnp.int32, (16, 128), 1)
    own = (row16 // 2 == lane16 % 8).astype(F32)[None]
    zero64 = jnp.zeros((64, 128), BF16)
    for hp in range(4):
        cols = slice(128 * hp, 128 * hp + 128)
        q = qs[:, cols] * jnp.asarray(0.125, BF16)
        q_e, q_o = q * half[0], q * half[1]
        rhs = jnp.concatenate(
            [jnp.concatenate([q_e, q_e], axis=1), jnp.concatenate([q_o, q_o], axis=1)], axis=0
        )
        diff = dot_nt(kk[hp], rhs)
        wo = wo128[cols, :]
        top = jnp.concatenate(
            [jnp.concatenate([wo[:64], zero64], axis=0), jnp.concatenate([zero64, wo[64:]], axis=0)], axis=1
        )
        u = dot_nn(vv[hp], jnp.concatenate([top, top], axis=0)).astype(BF16)
        for e in range(2):
            d = diff[:, 128 * e:128 * e + 128].reshape(36, 16, 128)
            small = jnp.exp(-jnp.abs(d))
            big = 1.0 / (1.0 + small)
            small = small * big
            weight = jnp.where(d >= 0, big, small)
            ww[2 * hp + e] = (weight * own).astype(BF16).reshape(rows, 128)
            cc[2 * hp + e] = (small * big * (own * 0.125)).reshape(rows, 128)
            uu[2 * hp + e] = u[:, 128 * e:128 * e + 128]

    gg[...] = jnp.zeros((8, rows, 128), BF16)

    edge = lax.broadcasted_iota(jnp.int32, (13, 8, 80), 1) < 2

    def groups(h, tiles):
        turned = [pltpu.roll(tile, 2, 1) for tile in tiles]
        for o in range(3):
            g16 = pl.ds(pl.multiple_of(48 * h + 16 * o, 16), 16)
            f = jnp.where(edge, turned[o], turned[o + 1]).reshape(104, 80)
            f = jnp.concatenate([f, jnp.zeros((24, 80), F32)], axis=0).astype(BF16)
            dw = dot_nt(uu[:, g16, 0:80].reshape(128, 80), f)
            d = (dw * cc[:, g16, :].reshape(128, 128)).astype(BF16)
            ds[:, g16, :] = d.reshape(8, 16, 128)
            g = dot_nn(ww[:, g16, :].reshape(128, 128), f).astype(BF16)
            gg[:, g16, 0:80] = g.reshape(8, 16, 80)

    def near(h, carry):
        own = f_ref[h + 3].astype(F32)
        groups(h, [own[:, 0:8], own[:, 8:16], own[:, 16:24], all_levels(f_right[h])])
        return carry

    def far(h, carry):
        own = all_levels(f_below[h])
        groups(h + 9, [own[:, 0:8], own[:, 8:16], own[:, 16:24], all_levels(f_corner[h])])
        return carry

    lax.fori_loop(0, 9, near, 0, unroll=9)
    lax.fori_loop(0, 3, far, 0, unroll=3)

    fold_row = lax.broadcasted_iota(jnp.int32, (128, 128), 0)
    fold_lane = lax.broadcasted_iota(jnp.int32, (128, 128), 1)
    fold = (fold_row // 8 == fold_lane - 80).astype(BF16)
    for hp in range(4):
        cols = slice(128 * hp, 128 * hp + 128)
        q = qs[:, cols]
        d = jnp.concatenate([ds[2 * hp], ds[2 * hp + 1]], axis=1)
        g = jnp.concatenate([gg[2 * hp], gg[2 * hp + 1]], axis=1)
        dkd[:, cols] = dot_nn(d, jnp.concatenate([q * half[0], q * half[1]], axis=0)).astype(BF16)
        wo = wo128[cols, :]
        top = jnp.concatenate(
            [jnp.concatenate([wo[:64], zero64], axis=0), jnp.concatenate([zero64, wo[64:]], axis=0)], axis=1
        )
        dvd[:, cols] = dot_nt(g, top).astype(BF16)
        dq = dot_tn(kk[hp, :, 0:128], d)
        dq = jnp.concatenate([dq[:64, :128], dq[64:, 128:]], axis=0)
        go = dot_tn(vv[hp, :, 0:128], g)
        go = jnp.concatenate([go[:64, :128], go[64:, 128:]], axis=0)
        dq_hi = dq.astype(BF16)
        dq_lo = (dq - dq_hi.astype(F32)).astype(BF16)
        hs[:, cols] = go + dot_nn(dq_hi, fold) + dot_nn(dq_lo, fold)

    d_mix = dot_nt(dkd[...], wkey_ref[...]) + dot_nt(dvd[...], wval_ref[...])
    dm32[...] = d_mix.astype(BF16).astype(F32)
    mixed_t = mixed.T
    put(1, 4, dot_nn(mixed_t, dkd[...]))
    put(1, 8, dot_nn(mixed_t, dvd[...]))

    total_gain = jnp.zeros((8, 512), F32)
    for w in range(n_win):
        for i in range(6):
            at_row = 48 * (6 * (w // 2) + i) + 24 * (w % 2)
            g = dm32[at_row:at_row + 24, :]
            n = nrm[w, 24 * i:24 * i + 24, :]
            total_gain = total_gain + jnp.sum((g * n).reshape(3, 8, 512), axis=0)
            gn = g * gain
            m1 = jnp.mean(gn, axis=-1, keepdims=True)
            m2 = jnp.mean(gn * n, axis=-1, keepdims=True)
            r = inv[w, 24 * i:24 * i + 24, 0:1]
            dp32[w, 24 * i:24 * i + 24, :] = r * (gn - m1 - n * m2)
    row_gain = jnp.broadcast_to(jnp.sum(total_gain, axis=0, keepdims=True), (128, 512))
    for hp in range(4):
        cols = slice(128 * hp, 128 * hp + 128)
        column = row_gain[:, cols].T
        lanes = lax.broadcasted_iota(jnp.int32, (128, 128), 1)
        tail = jnp.where(lanes == 96, column, hs[:, cols]).astype(BF16)
        at_row = 6144 + 128 * (hp % 2)
        grads_ref[(hp // 2) ^ core, at_row:at_row + 128, :] = tail
    for half_no in range(2):
        grads_ref[half_no, 6400:6656, :] = jnp.zeros((256, 128), BF16)
    for w in range(n_win):
        dpb[w] = dp32[w].astype(BF16)
    flat_dp = dpb[...].reshape(rows, 512)
    total = dot_nn(at_t[0], dpb[0])
    for w in range(1, n_win):
        total = total + dot_nn(at_t[w], dpb[w])
    put(1, 0, total)
    dat[...] = dot_nt(flat_dp, wproj_ref[...]).astype(BF16).reshape(n_win, tok, 512)

    early_keep = pltpu.make_async_copy(grads_ref.at[0], keep_hbm, out_sem.at[0])
    early_send = pltpu.make_async_copy(grads_ref.at[1], send_hbm, out_sem.at[1])
    late_keep = pltpu.make_async_copy(grads_ref.at[0], keep_hbm, out_sem.at[2])
    late_send = pltpu.make_async_copy(grads_ref.at[1], send_hbm, out_sem.at[3])

    @pl.when(core == 1)
    def _():
        early_keep.start()

    @pl.when(core == 0)
    def _():
        early_send.start()

    def unattend(w, carry):
        for hp in range(4):
            cols = slice(128 * hp, 128 * hp + 128)
            q = pk[w, :, 128 * hp:128 * hp + 128]
            k_t = pk[w, :, 512 + 128 * hp:512 + 128 * hp + 128].T
            v = pk[w, :, 1024 + 128 * hp:1024 + 128 * hp + 128]
            da = dat[w, :, cols]
            both = dot_nt(jnp.concatenate([v * eighth[0], v * eighth[1]], axis=0), da)
            ps, ss, dqs = [], [], []
            for e in range(2):
                p = probs[w, 2 * hp + e]
                dw = both[tok * e:tok * e + tok]
                s = (p * (dw - jnp.sum(p * dw, axis=0, keepdims=True))).astype(BF16)
                ps.append(p.astype(BF16))
                ss.append(s)
                dqs.append(dot_nn(k_t[64 * e:64 * e + 64], s))
            dv = dot_nn(jnp.concatenate(ps, axis=0), da)
            dk = dot_nn(jnp.concatenate(ss, axis=0), q)
            dpk[w, :, cols] = jnp.concatenate(dqs, axis=0).astype(BF16).T
            dpk[w, :, 512 + 128 * hp:512 + 128 * hp + 128] = jnp.where(low, dk[:tok], dk[tok:]).astype(BF16)
            dpk[w, :, 1024 + 128 * hp:1024 + 128 * hp + 128] = jnp.where(low, dv[:tok], dv[tok:]).astype(BF16)
        return carry

    lax.fori_loop(0, n_win, unattend, 0)

    flat_d = dpk[...].reshape(rows, 1536)
    for n in range(3):
        put(0, 4 * n, dot_nn(x_t[...], flat_d[:, 512 * n:512 * n + 512]))

    @pl.when(core == 0)
    def _():
        late_keep.start()

    @pl.when(core == 1)
    def _():
        late_send.start()

    dp32[...] = dot_nt(flat_d, wqkv_ref[...]).reshape(n_win, tok, 512)
    for h in range(12):
        parts = []
        for b in range(2):
            at_row = 48 * h + 24 * b
            parts.append(
                dp32[(h // 6) * 2 + b, 24 * (h % 6):24 * (h % 6) + 24, :] + dm32[at_row:at_row + 24, :]
            )
        out_ref[48 * h:48 * h + 48, :] = jnp.concatenate(parts, axis=0).astype(BF16)
    result = pltpu.make_async_copy(out_ref, out_hbm, out_sem.at[4])
    result.start()

    @pl.when(core == 0)
    def _():
        early_send.wait()
        late_keep.wait()

    @pl.when(core == 1)
    def _():
        early_keep.wait()
        late_send.wait()

    result.wait()


def section(core, level_ids, x, fields, halo, ids, table, w_qkv, w_proj, gain, w_key, w_value, w_out):
    vm = lambda shape, kind: pltpu.VMEM(shape, kind)
    scratch = [
        vm((4, 144, 512), F32), vm((4, 144, 512), BF16), vm((4, 144, 1536), BF16), vm((4, 8, 144, 144), F32),
        vm((4, 144, 512), BF16), vm((4, 144, 512), F32), vm((4, 144, 128), F32), vm((576, 512), F32),
        vm((576, 512), BF16), vm((4, 576, 256), BF16), vm((4, 576, 256), BF16), vm((8, 576, 128), BF16),
        vm((8, 576, 128), BF16), vm((8, 576, 128), F32), vm((8, 576, 128), BF16), vm((8, 576, 128), BF16),
        vm((576, 512), BF16), vm((576, 512), BF16), vm((576, 512), F32), vm((4, 144, 512), F32),
        vm((4, 144, 512), BF16), vm((4, 144, 512), BF16), vm((4, 144, 1536), BF16), vm((128, 512), F32),
        vm((4, 512, 144), BF16), vm((512, 576), BF16), vm((4, 144, 128), BF16), vm((128, 512), F32),
        vm((128, 512), BF16), vm((512, 128), BF16), vm((3, 9, 24, 128), F32), vm((9, 9, 8, 128), F32),
        vm((3, 9, 8, 128), F32),
        vm((512, 1536), BF16), vm((512, 512), BF16), vm((512, 512), BF16), vm((512, 512), BF16),
        vm((12, 13, 24, 80), BF16), vm((576, 512), BF16), vm((2, 6656, 128), BF16),
        pltpu.SemaphoreType.DMA((5,)), pltpu.SemaphoreType.DMA((5,)),
    ]
    smem, vmem = pl.BlockSpec(memory_space=pltpu.SMEM), pl.BlockSpec(memory_space=pltpu.VMEM)
    hbm = pl.BlockSpec(memory_space=pl.ANY)
    half = jax.ShapeDtypeStruct((6656, 128), BF16)
    return pl.pallas_call(
        section_kernel,
        out_shape=(jax.ShapeDtypeStruct((576, 512), BF16), half, half),
        in_specs=[smem, smem] + [vmem] * 8 + [hbm] * 5,
        out_specs=[hbm] * 3,
        scratch_shapes=scratch,
        compiler_params=pltpu.CompilerParams(vmem_limit_bytes=58 * 1024 * 1024),
        cost_estimate=pl.CostEstimate(flops=15_000_000_000, bytes_accessed=12_000_000, transcendentals=2_000_000),
        name="section",
    )(core, level_ids, x, *halo, ids, table, gain[None], w_out, w_qkv, w_proj, w_key, w_value, fields)


from jax.sharding import Mesh, PartitionSpec as P

LAT = ("z_hi", "core")
LON = ("x", "y", "z_lo")
CHIPS = ("z_hi", "x", "y", "z_lo")


def neighbours(axes, by):
    count = 1
    for axis in axes:
        count *= lax.axis_size(axis)
    return [(i, (i + by) % count) for i in range(count)]


def corner_pairs(by):
    n_lat, n_lon = 4, 32
    return [
        (a * n_lon + b, ((a + by) % n_lat) * n_lon + (b + by) % n_lon) for a in range(n_lat) for b in range(n_lon)
    ]


def fetch(tokens, fields):
    below, right, corner = pack(tokens, fields)
    return (
        lax.ppermute(below, LAT, neighbours(LAT, -1)),
        lax.ppermute(right, LON, neighbours(LON, -1)),
        lax.ppermute(corner, LAT + LON, corner_pairs(-1)),
    )


def send_back(tile):
    h, w = tile.shape[0], tile.shape[1]
    above = lax.ppermute(tile[h - SH:, :w - SW], LAT, neighbours(LAT, 1))
    left = lax.ppermute(tile[:h - SH, w - SW:], LON, neighbours(LON, 1))
    corner = lax.ppermute(tile[h - SH:, w - SW:], LAT + LON, corner_pairs(1))
    return above, left, corner


def place_back(tile, above, left, corner):
    h, w = tile.shape[0], tile.shape[1]
    top = jnp.concatenate([corner, above], axis=1)
    bottom = jnp.concatenate([left, tile[:h - SH, :w - SW]], axis=1)
    return jnp.concatenate([top, bottom], axis=0)


def sum_all(keep, send, tile, sent):
    swap = [(0, 1), (1, 0)]
    other = lax.ppermute(send, "core", swap)
    mine = (keep.astype(F32) + other.astype(F32)).astype(BF16)
    pieces = lax.all_to_all(mine.reshape(64, 104, 128), CHIPS, split_axis=0, concat_axis=0, tiled=True)
    piece = jnp.sum(pieces.astype(F32), axis=0).astype(BF16)
    piece, sent = lax.optimization_barrier((piece, sent))
    spread = jnp.broadcast_to(piece[None], (64, 104, 128))
    mine = lax.all_to_all(spread, CHIPS, split_axis=0, concat_axis=0, tiled=True).reshape(6656, 128)
    mine, d_latent = lax.optimization_barrier((mine, place_back(tile, *sent)))
    other = lax.ppermute(mine, "core", swap)
    return mine, other, d_latent


def unpack_kernel(core_ref, level_ref, mine_ref, other_ref, qkv_ref, proj_ref, key_ref, value_ref, out_ref, gain_ref, table_ref, tail_ref):
    first = core_ref[0, 0] == 0

    def pick(half_no, at_row, count):
        mine, other = mine_ref[at_row:at_row + count, :], other_ref[at_row:at_row + count, :]
        chosen = jnp.where(first, mine, other) if half_no == 0 else jnp.where(first, other, mine)
        return chosen.astype(F32)

    for block in range(12):
        qkv_ref[:, 128 * block:128 * block + 128] = pick(0, 512 * block, 512)
    for n, ref in enumerate((proj_ref, key_ref, value_ref)):
        for c in range(4):
            ref[:, 128 * c:128 * c + 128] = pick(1, 512 * (4 * n + c), 512)
    for hp in range(4):
        tail_ref[:, 128 * hp:128 * hp + 128] = pick(hp // 2, 6144 + 128 * (hp % 2), 128).T
    out_ref[...] = tail_ref[0:80, :]
    gain_ref[...] = tail_ref[96:97, :]
    row = lax.broadcasted_iota(jnp.int32, (37, 512), 0)
    table = jnp.zeros((37, 512), F32)
    for p in range(13):
        table = table + jnp.where(row == level_ref[p], tail_ref[80 + p:81 + p, :], 0.0)
    table_ref[...] = table


def unpack(core, level_ids, mine, other):
    shape = lambda *dims: jax.ShapeDtypeStruct(dims, F32)
    smem, vmem = pl.BlockSpec(memory_space=pltpu.SMEM), pl.BlockSpec(memory_space=pltpu.VMEM)
    return pl.pallas_call(
        unpack_kernel,
        out_shape=(
            shape(512, 1536), shape(512, 512), shape(512, 512), shape(512, 512), shape(80, 512), shape(1, 512),
            shape(37, 512),
        ),
        in_specs=[smem, smem, vmem, vmem],
        out_specs=[vmem] * 7,
        scratch_shapes=[pltpu.VMEM((128, 512), F32)],
        compiler_params=pltpu.CompilerParams(vmem_limit_bytes=24 * 1024 * 1024),
        cost_estimate=pl.CostEstimate(flops=3_000_000, bytes_accessed=10_000_000, transcendentals=0),
        name="unpack",
    )(core, level_ids, mine, other)


def shards(
    latent, grad_fields, region_ids, level_ids, w_qkv, w_proj, gain, level_table, w_key, w_value, w_out
):
    core = lax.axis_index("core")
    tokens = latent.reshape(576, 512)
    fields = grad_fields.transpose(0, 2, 1, 3)
    out, keep, send = section(
        core.reshape(1, 1), level_ids, tokens, fields, fetch(tokens, fields), region_ids, level_table, w_qkv, w_proj,
        gain, w_key, w_value, w_out.T,
    )
    tile = out.reshape(12, 24, 2, 512)
    mine, other, d_latent = sum_all(keep, send, tile, send_back(tile))
    grad_qkv, grad_proj, grad_key, grad_value, out_t, grad_gain, table = unpack(core.reshape(1, 1), level_ids, mine, other)
    return d_latent, grad_qkv, grad_proj, grad_gain[0], table, grad_key, grad_value, out_t.T


def solution(mesh):
    fine = Mesh(mesh.devices.reshape(2, 2, 4, 4, 2), LAT + LON)
    tile = P(LAT, LON, None, None)
    return jax.shard_map(
        shards,
        mesh=fine,
        in_specs=(tile, tile, P(LAT, LON)) + (P(),) * 8,
        out_specs=(tile,) + (P(),) * 7,
        check_vma=False,
    )
```

```python
import functools
import jax
import jax.numpy as jnp
from jax import lax
from jax.experimental import pallas as pl
from jax.experimental.pallas import tpu as pltpu

HEADS = 8
WH = 6
WW = 12
LV = 2
SH = 3
SW = 6
EPS = 1e-05
MASKED = -1e30
F32 = jnp.float32
BF16 = jnp.bfloat16


def dot_nn(a, b):
    return lax.dot_general(a, b, (((1,), (0,)), ((), ())), preferred_element_type=F32)


def dot_nt(a, b):
    return lax.dot_general(a, b, (((1,), (1,)), ((), ())), preferred_element_type=F32)


def dot_tn(a, b):
    return lax.dot_general(a, b, (((0,), (0,)), ((), ())), preferred_element_type=F32)


def swap_rows(a):
    rows, lanes = a.shape
    blocks = a.reshape(rows // 8, 8, lanes)
    later = pltpu.roll(blocks, 7, 1)
    earlier = pltpu.roll(blocks, 1, 1)
    even = lax.broadcasted_iota(jnp.int32, blocks.shape, 1) % 2 == 0
    return jnp.where(even, later, earlier).reshape(rows, lanes)


def nine_tiles(levels):
    lane = lax.broadcasted_iota(jnp.int32, levels.shape[1:], 1)
    tiles = [levels[p] for p in range(9)]
    for m in range(4):
        extra = levels[9 + m]
        tiles[2 * m] = jnp.where(lane < 80, tiles[2 * m], pltpu.roll(extra, 80, 1))
        tiles[2 * m + 1] = jnp.where(lane < 80, tiles[2 * m + 1], pltpu.roll(extra, 32, 1))
    return jnp.stack(tiles, axis=0)


def all_levels(tiles):
    lane = lax.broadcasted_iota(jnp.int32, tiles.shape[1:], 1)
    levels = [tiles[p] for p in range(9)]
    for m in range(4):
        levels.append(
            jnp.where(lane < 48, pltpu.roll(tiles[2 * m], 48, 1), pltpu.roll(tiles[2 * m + 1], 96, 1))
        )
    return jnp.stack(levels, axis=0)[:, :, :80]


def row_of_tile():
    return lax.broadcasted_iota(jnp.int32, (8, 128), 0)


def side_tiles(line, levels):
    row = row_of_tile()
    tiles = [line[0:8, 128 * c:128 * c + 128] for c in range(4)]
    for m in range(2):
        left, right = (line[8:16, 128 * c:128 * c + 128] for c in (2 * m, 2 * m + 1))
        tiles.append(jnp.where(row < 4, left, pltpu.roll(right, 4, 0)))
    places = []
    for m in range(2):
        for i in range(3):
            places.append(jnp.where(row < 6, levels[4 * m + i], pltpu.roll(levels[4 * m + 3], 6 - 2 * i, 0)))
    return tiles, places + [levels[8]]


def side_levels(places):
    row = row_of_tile()
    out = []
    for m in range(2):
        first, second, third = places[3 * m:3 * m + 3]
        last = jnp.where(
            row < 2, pltpu.roll(first, 2, 0), jnp.where(row < 4, pltpu.roll(second, 4, 0), pltpu.roll(third, 6, 0))
        )
        out += [first, second, third, last]
    return jnp.stack(out + [places[6]], axis=0)


def pack_kernel(x_ref, f_ref, below_ref, right_ref, corner_ref, wide):
    row = row_of_tile()
    full, halves, lines, sides = [], [], [], ([], [])
    for h in range(12):
        wide[h, :, :, 0:80] = f_ref[h].astype(F32)
        line = x_ref[48 * h:48 * h + 48, :].astype(F32)
        tiles, places = side_tiles(line[0:16], nine_tiles(wide[h, :, 0:8, :]))
        sides[0].append(tiles)
        sides[1].append(places)
        if h < 3:
            for c in range(4):
                full += [line[8 * n:8 * n + 8, 128 * c:128 * c + 128] for n in range(2, 6)]
            for m in range(2):
                left, right = (line[8:16, 128 * c:128 * c + 128] for c in (2 * m, 2 * m + 1))
                halves.append(jnp.where(row < 4, pltpu.roll(right, 4, 0), left))
            levels = nine_tiles(wide[h])
            for k in range(9):
                lines += [levels[k, 8:16], levels[k, 16:24]]
            for q in range(2):
                four = [pltpu.roll(levels[4 * q + i, 0:8], (8 - 2 * i) % 8, 0) for i in range(4)]
                low = jnp.where(row < 2, four[3], four[2])
                lines.append(jnp.where(row < 4, low, jnp.where(row < 6, four[1], four[0])))
            lines.append(levels[8, 0:8])
    below_ref[...] = jnp.concatenate(full + halves + lines, axis=0).astype(BF16)
    right_ref[...] = jnp.concatenate(sum(sides[0][3:], []) + sum(sides[1][3:], []), axis=0).astype(BF16)
    corner_ref[...] = jnp.concatenate(sum(sides[0][:3], []) + sum(sides[1][:3], []), axis=0).astype(BF16)


def pack(x, fields):
    vmem = pl.BlockSpec(memory_space=pltpu.VMEM)
    return pl.pallas_call(
        pack_kernel,
        out_shape=tuple(jax.ShapeDtypeStruct((rows, 128), BF16) for rows in (936, 936, 312)),
        in_specs=[vmem, vmem],
        out_specs=[vmem] * 3,
        scratch_shapes=[pltpu.VMEM((12, 13, 24, 128), F32)],
        compiler_params=pltpu.CompilerParams(vmem_limit_bytes=16 * 1024 * 1024),
        cost_estimate=pl.CostEstimate(flops=2_000_000, bytes_accessed=3_000_000, transcendentals=0),
        name="pack",
    )(x, fields)


def section_kernel(
    core_ref, level_ref, x_ref, below_ref, right_ref, corner_ref, ids_ref, table_ref, gain_ref, wout_ref,
    wqkv_hbm, wproj_hbm, wkey_hbm, wval_hbm, f_hbm,
    out_hbm, keep_hbm, send_hbm,
    xw32, xw, pk, probs, at, nrm, inv, mix32, mixb, kk, vv, uu, ww, cc, ds, gg, dkd, dvd, dm32, dp32, dpb, dat, dpk, hs, at_t, x_t, hot, q32, qs, wo128, f_below, f_right, f_corner,
    wqkv_ref, wproj_ref, wkey_ref, wval_ref, f_ref, out_ref, grads_ref, in_sem, out_sem,
):
    n_win = 4
    tok = 144
    rows = 576
    core = core_ref[0, 0]
    loads = [
        pltpu.make_async_copy(source, target, in_sem.at[n])
        for n, (source, target) in enumerate(
            (
                (wqkv_hbm, wqkv_ref), (wproj_hbm, wproj_ref), (wkey_hbm, wkey_ref), (wval_hbm, wval_ref),
                (f_hbm, f_ref),
            )
        )
    ]
    for load in loads:
        load.start()

    def put(half_no, block, matrix):
        for c in range(matrix.shape[1] // 128):
            at_row = 512 * (block + c)
            piece = matrix[:, 128 * c:128 * c + 128].astype(BF16)
            grads_ref[half_no ^ core, at_row:at_row + 512, :] = piece

    lane = lax.broadcasted_iota(jnp.int32, (1, 128), 1)
    half = ((lane < 64).astype(BF16), (lane >= 64).astype(BF16))
    eighth = (half[0] * jnp.asarray(0.125, BF16), half[1] * jnp.asarray(0.125, BF16))
    low = lax.broadcasted_iota(jnp.int32, (tok, 128), 1) < 64
    gain = gain_ref[...]

    wide = table_ref[...].astype(F32)
    table_row = lax.broadcasted_iota(jnp.int32, wide.shape, 0)
    for p in range(13):
        q32[8 * p:8 * p + 8, :] = jnp.broadcast_to(
            jnp.sum(jnp.where(table_row == level_ref[p], wide, 0.0), axis=0, keepdims=True), (8, 512)
        )
    q32[104:128, :] = jnp.zeros((24, 512), F32)
    qs[...] = q32[...].astype(BF16)
    wo128[...] = jnp.zeros((512, 128), BF16)
    wo128[:, 0:80] = wout_ref[...].T

    ids = ids_ref[...].astype(F32)
    token = lax.broadcasted_iota(jnp.int32, (tok, 24), 0)
    spot = lax.broadcasted_iota(jnp.int32, (tok, 24), 1)
    tok12 = lax.broadcasted_iota(jnp.int32, (tok, 12), 0)
    row12 = lax.broadcasted_iota(jnp.int32, (tok, 12), 1)
    kind = lax.broadcasted_iota(jnp.int32, (tok, 128), 1).astype(F32)
    for w in range(n_win):
        pick = (tok12 // 24 + 6 * (w // 2) == row12).astype(F32)
        line = dot_nn(pick, ids)
        own_id = jnp.sum(
            jnp.where(spot == 12 * (w % 2) + (token % 24) // 2, line, 0.0), axis=1, keepdims=True
        )
        hot[w] = (own_id == kind).astype(BF16)

    row8 = row_of_tile()
    below = below_ref[...].astype(F32).reshape(117, 8, 128)
    right = right_ref[...].astype(F32).reshape(117, 8, 128)
    corner = corner_ref[...].astype(F32).reshape(39, 8, 128)
    for h in range(9):
        f_right[h] = side_levels([right[54 + 7 * h + n] for n in range(7)])
    for h in range(3):
        f_corner[h] = side_levels([corner[18 + 7 * h + n] for n in range(7)])
        for k in range(9):
            at_tile = 54 + 21 * h
            f_below[h, k, 0:8, :] = pltpu.roll(below[at_tile + 18 + k // 4], 2 * (k % 4), 0)
            f_below[h, k, 8:16, :] = below[at_tile + 2 * k]
            f_below[h, k, 16:24, :] = below[at_tile + 2 * k + 1]
    for h in range(12):
        side = right[6 * h:6 * h + 6] if h < 9 else corner[6 * (h - 9):6 * (h - 9) + 6]
        for c in range(4):
            cols = slice(128 * c, 128 * c + 128)
            if h < 9:
                main = x_ref[48 * (h + 3):48 * (h + 3) + 48, cols].astype(F32)
                line = [main[8 * n:8 * n + 8] for n in range(1, 6)]
            else:
                half_tile = below[48 + 2 * (h - 9) + c // 2]
                line = [half_tile if c % 2 == 0 else pltpu.roll(half_tile, 4, 0)]
                line += [below[16 * (h - 9) + 4 * c + n] for n in range(4)]
            half_tile = side[4 + c // 2]
            line += [side[c], half_tile if c % 2 == 0 else pltpu.roll(half_tile, 4, 0)]
            turned = [pltpu.roll(tile, 4, 0) for tile in line]
            piece = [jnp.where(row8 < 4, turned[n], turned[n + 1]) for n in range(6)]
            for b in range(2):
                xw32[(h // 6) * 2 + b, 24 * (h % 6):24 * (h % 6) + 24, cols] = jnp.concatenate(
                    piece[3 * b:3 * b + 3], axis=0
                )
    for w in range(n_win):
        xw[w] = xw32[w].astype(BF16)
    flat_x = xw[...].reshape(rows, 512)
    loads[0].wait()
    x_t[...] = flat_x.T
    for n in range(6):
        part = dot_nn(flat_x, wqkv_ref[:, 256 * n:256 * n + 256]).astype(BF16)
        pk[:, :, 256 * n:256 * n + 256] = part.reshape(n_win, tok, 256)

    def attend(w, carry):
        same = dot_nt(hot[w], hot[w])
        bias = (same - 1.0) * -MASKED
        for hp in range(4):
            cols = slice(128 * hp, 128 * hp + 128)
            q = pk[w, :, 128 * hp:128 * hp + 128]
            k = pk[w, :, 512 + 128 * hp:512 + 128 * hp + 128]
            v_t = pk[w, :, 1024 + 128 * hp:1024 + 128 * hp + 128].T
            outs = []
            both = dot_nt(jnp.concatenate([k * eighth[0], k * eighth[1]], axis=0), q)
            for e in range(2):
                s = both[tok * e:tok * e + tok] + bias
                p = jnp.exp(s - jnp.max(s, axis=0, keepdims=True))
                p = p * (1.0 / jnp.sum(p, axis=0, keepdims=True))
                probs[w, 2 * hp + e] = p
                outs.append(dot_nn(v_t[64 * e:64 * e + 64], p.astype(BF16)))
            o_t = jnp.concatenate(outs, axis=0).astype(BF16)
            at_t[w, cols, :] = o_t
            at[w, :, cols] = o_t.T
        return carry

    lax.fori_loop(0, n_win, attend, 0)

    flat_at = at[...].reshape(rows, 512)
    loads[1].wait()
    nrm[...] = dot_nn(flat_at, wproj_ref[...]).reshape(n_win, tok, 512)
    for w in range(n_win):
        for i in range(6):
            at_row = 48 * (6 * (w // 2) + i) + 24 * (w % 2)
            p = nrm[w, 24 * i:24 * i + 24, :]
            c = p - jnp.mean(p, axis=-1, keepdims=True)
            r = lax.rsqrt(jnp.mean(c * c, axis=-1, keepdims=True) + EPS)
            n = c * r
            nrm[w, 24 * i:24 * i + 24, :] = n
            inv[w, 24 * i:24 * i + 24, :] = jnp.broadcast_to(r, (24, 128))
            mix32[at_row:at_row + 24, :] = xw32[w, 24 * i:24 * i + 24, :] + n * gain
    mixb[...] = mix32[...].astype(BF16)

    mixed = mixb[...]
    for load in loads[2:]:
        load.wait()
    for hp in range(4):
        cols = slice(128 * hp, 128 * hp + 128)
        for w_ref, pair in ((wkey_ref, kk), (wval_ref, vv)):
            part = dot_nn(mixed, w_ref[:, cols]).astype(BF16)
            other = swap_rows(part.astype(F32))
            pair[hp, :, 0:128] = part
            pair[hp, :, 128:256] = (-other).astype(BF16)

    row16 = lax.broadcasted_iota(jnp.int32, (16, 128), 0)
    lane16 = lax.broadcasted_iota(jnp.int32, (16, 128), 1)
    own = (row16 // 2 == lane16 % 8).astype(F32)[None]
    zero64 = jnp.zeros((64, 128), BF16)
    for hp in range(4):
        cols = slice(128 * hp, 128 * hp + 128)
        q = qs[:, cols] * jnp.asarray(0.125, BF16)
        q_e, q_o = q * half[0], q * half[1]
        rhs = jnp.concatenate(
            [jnp.concatenate([q_e, q_e], axis=1), jnp.concatenate([q_o, q_o], axis=1)], axis=0
        )
        diff = dot_nt(kk[hp], rhs)
        wo = wo128[cols, :]
        top = jnp.concatenate(
            [jnp.concatenate([wo[:64], zero64], axis=0), jnp.concatenate([zero64, wo[64:]], axis=0)], axis=1
        )
        u = dot_nn(vv[hp], jnp.concatenate([top, top], axis=0)).astype(BF16)
        for e in range(2):
            d = diff[:, 128 * e:128 * e + 128].reshape(36, 16, 128)
            small = jnp.exp(-jnp.abs(d))
            big = 1.0 / (1.0 + small)
            small = small * big
            weight = jnp.where(d >= 0, big, small)
            ww[2 * hp + e] = (weight * own).astype(BF16).reshape(rows, 128)
            cc[2 * hp + e] = (small * big * (own * 0.125)).reshape(rows, 128)
            uu[2 * hp + e] = u[:, 128 * e:128 * e + 128]

    gg[...] = jnp.zeros((8, rows, 128), BF16)

    edge = lax.broadcasted_iota(jnp.int32, (13, 8, 80), 1) < 2

    def groups(h, tiles):
        turned = [pltpu.roll(tile, 2, 1) for tile in tiles]
        for o in range(3):
            g16 = pl.ds(pl.multiple_of(48 * h + 16 * o, 16), 16)
            f = jnp.where(edge, turned[o], turned[o + 1]).reshape(104, 80)
            f = jnp.concatenate([f, jnp.zeros((24, 80), F32)], axis=0).astype(BF16)
            dw = dot_nt(uu[:, g16, 0:80].reshape(128, 80), f)
            d = (dw * cc[:, g16, :].reshape(128, 128)).astype(BF16)
            ds[:, g16, :] = d.reshape(8, 16, 128)
            g = dot_nn(ww[:, g16, :].reshape(128, 128), f).astype(BF16)
            gg[:, g16, 0:80] = g.reshape(8, 16, 80)

    def near(h, carry):
        own = f_ref[h + 3].astype(F32)
        groups(h, [own[:, 0:8], own[:, 8:16], own[:, 16:24], all_levels(f_right[h])])
        return carry

    def far(h, carry):
        own = all_levels(f_below[h])
        groups(h + 9, [own[:, 0:8], own[:, 8:16], own[:, 16:24], all_levels(f_corner[h])])
        return carry

    lax.fori_loop(0, 9, near, 0, unroll=9)
    lax.fori_loop(0, 3, far, 0, unroll=3)

    fold_row = lax.broadcasted_iota(jnp.int32, (128, 128), 0)
    fold_lane = lax.broadcasted_iota(jnp.int32, (128, 128), 1)
    fold = (fold_row // 8 == fold_lane - 80).astype(BF16)
    for hp in range(4):
        cols = slice(128 * hp, 128 * hp + 128)
        q = qs[:, cols]
        d = jnp.concatenate([ds[2 * hp], ds[2 * hp + 1]], axis=1)
        g = jnp.concatenate([gg[2 * hp], gg[2 * hp + 1]], axis=1)
        dkd[:, cols] = dot_nn(d, jnp.concatenate([q * half[0], q * half[1]], axis=0)).astype(BF16)
        wo = wo128[cols, :]
        top = jnp.concatenate(
            [jnp.concatenate([wo[:64], zero64], axis=0), jnp.concatenate([zero64, wo[64:]], axis=0)], axis=1
        )
        dvd[:, cols] = dot_nt(g, top).astype(BF16)
        dq = dot_tn(kk[hp, :, 0:128], d)
        dq = jnp.concatenate([dq[:64, :128], dq[64:, 128:]], axis=0)
        go = dot_tn(vv[hp, :, 0:128], g)
        go = jnp.concatenate([go[:64, :128], go[64:, 128:]], axis=0)
        dq_hi = dq.astype(BF16)
        dq_lo = (dq - dq_hi.astype(F32)).astype(BF16)
        hs[:, cols] = go + dot_nn(dq_hi, fold) + dot_nn(dq_lo, fold)

    d_mix = dot_nt(dkd[...], wkey_ref[...]) + dot_nt(dvd[...], wval_ref[...])
    dm32[...] = d_mix.astype(BF16).astype(F32)
    mixed_t = mixed.T
    put(1, 4, dot_nn(mixed_t, dkd[...]))
    put(1, 8, dot_nn(mixed_t, dvd[...]))

    total_gain = jnp.zeros((8, 512), F32)
    for w in range(n_win):
        for i in range(6):
            at_row = 48 * (6 * (w // 2) + i) + 24 * (w % 2)
            g = dm32[at_row:at_row + 24, :]
            n = nrm[w, 24 * i:24 * i + 24, :]
            total_gain = total_gain + jnp.sum((g * n).reshape(3, 8, 512), axis=0)
            gn = g * gain
            m1 = jnp.mean(gn, axis=-1, keepdims=True)
            m2 = jnp.mean(gn * n, axis=-1, keepdims=True)
            r = inv[w, 24 * i:24 * i + 24, 0:1]
            dp32[w, 24 * i:24 * i + 24, :] = r * (gn - m1 - n * m2)
    row_gain = jnp.broadcast_to(jnp.sum(total_gain, axis=0, keepdims=True), (128, 512))
    for hp in range(4):
        cols = slice(128 * hp, 128 * hp + 128)
        column = row_gain[:, cols].T
        lanes = lax.broadcasted_iota(jnp.int32, (128, 128), 1)
        tail = jnp.where(lanes == 96, column, hs[:, cols]).astype(BF16)
        at_row = 6144 + 128 * (hp % 2)
        grads_ref[(hp // 2) ^ core, at_row:at_row + 128, :] = tail
    for half_no in range(2):
        grads_ref[half_no, 6400:6656, :] = jnp.zeros((256, 128), BF16)
    for w in range(n_win):
        dpb[w] = dp32[w].astype(BF16)
    flat_dp = dpb[...].reshape(rows, 512)
    total = dot_nn(at_t[0], dpb[0])
    for w in range(1, n_win):
        total = total + dot_nn(at_t[w], dpb[w])
    put(1, 0, total)
    dat[...] = dot_nt(flat_dp, wproj_ref[...]).astype(BF16).reshape(n_win, tok, 512)

    early_keep = pltpu.make_async_copy(grads_ref.at[0], keep_hbm, out_sem.at[0])
    early_send = pltpu.make_async_copy(grads_ref.at[1], send_hbm, out_sem.at[1])
    late_keep = pltpu.make_async_copy(grads_ref.at[0], keep_hbm, out_sem.at[2])
    late_send = pltpu.make_async_copy(grads_ref.at[1], send_hbm, out_sem.at[3])

    @pl.when(core == 1)
    def _():
        early_keep.start()

    @pl.when(core == 0)
    def _():
        early_send.start()

    def unattend(w, carry):
        for hp in range(4):
            cols = slice(128 * hp, 128 * hp + 128)
            q = pk[w, :, 128 * hp:128 * hp + 128]
            k_t = pk[w, :, 512 + 128 * hp:512 + 128 * hp + 128].T
            v = pk[w, :, 1024 + 128 * hp:1024 + 128 * hp + 128]
            da = dat[w, :, cols]
            both = dot_nt(jnp.concatenate([v * eighth[0], v * eighth[1]], axis=0), da)
            ps, ss, dqs = [], [], []
            for e in range(2):
                p = probs[w, 2 * hp + e]
                dw = both[tok * e:tok * e + tok]
                s = (p * (dw - jnp.sum(p * dw, axis=0, keepdims=True))).astype(BF16)
                ps.append(p.astype(BF16))
                ss.append(s)
                dqs.append(dot_nn(k_t[64 * e:64 * e + 64], s))
            dv = dot_nn(jnp.concatenate(ps, axis=0), da)
            dk = dot_nn(jnp.concatenate(ss, axis=0), q)
            dpk[w, :, cols] = jnp.concatenate(dqs, axis=0).astype(BF16).T
            dpk[w, :, 512 + 128 * hp:512 + 128 * hp + 128] = jnp.where(low, dk[:tok], dk[tok:]).astype(BF16)
            dpk[w, :, 1024 + 128 * hp:1024 + 128 * hp + 128] = jnp.where(low, dv[:tok], dv[tok:]).astype(BF16)
        return carry

    lax.fori_loop(0, n_win, unattend, 0)

    flat_d = dpk[...].reshape(rows, 1536)
    for n in range(3):
        put(0, 4 * n, dot_nn(x_t[...], flat_d[:, 512 * n:512 * n + 512]))

    @pl.when(core == 0)
    def _():
        late_keep.start()

    @pl.when(core == 1)
    def _():
        late_send.start()

    dp32[...] = dot_nt(flat_d, wqkv_ref[...]).reshape(n_win, tok, 512)
    for h in range(12):
        parts = []
        for b in range(2):
            at_row = 48 * h + 24 * b
            parts.append(
                dp32[(h // 6) * 2 + b, 24 * (h % 6):24 * (h % 6) + 24, :] + dm32[at_row:at_row + 24, :]
            )
        out_ref[48 * h:48 * h + 48, :] = jnp.concatenate(parts, axis=0).astype(BF16)
    result = pltpu.make_async_copy(out_ref, out_hbm, out_sem.at[4])
    result.start()

    @pl.when(core == 0)
    def _():
        early_send.wait()
        late_keep.wait()

    @pl.when(core == 1)
    def _():
        early_keep.wait()
        late_send.wait()

    result.wait()


def section(core, level_ids, x, fields, halo, ids, table, w_qkv, w_proj, gain, w_key, w_value, w_out):
    vm = lambda shape, kind: pltpu.VMEM(shape, kind)
    scratch = [
        vm((4, 144, 512), F32), vm((4, 144, 512), BF16), vm((4, 144, 1536), BF16), vm((4, 8, 144, 144), F32),
        vm((4, 144, 512), BF16), vm((4, 144, 512), F32), vm((4, 144, 128), F32), vm((576, 512), F32),
        vm((576, 512), BF16), vm((4, 576, 256), BF16), vm((4, 576, 256), BF16), vm((8, 576, 128), BF16),
        vm((8, 576, 128), BF16), vm((8, 576, 128), F32), vm((8, 576, 128), BF16), vm((8, 576, 128), BF16),
        vm((576, 512), BF16), vm((576, 512), BF16), vm((576, 512), F32), vm((4, 144, 512), F32),
        vm((4, 144, 512), BF16), vm((4, 144, 512), BF16), vm((4, 144, 1536), BF16), vm((128, 512), F32),
        vm((4, 512, 144), BF16), vm((512, 576), BF16), vm((4, 144, 128), BF16), vm((128, 512), F32),
        vm((128, 512), BF16), vm((512, 128), BF16), vm((3, 9, 24, 128), F32), vm((9, 9, 8, 128), F32),
        vm((3, 9, 8, 128), F32),
        vm((512, 1536), BF16), vm((512, 512), BF16), vm((512, 512), BF16), vm((512, 512), BF16),
        vm((12, 13, 24, 80), BF16), vm((576, 512), BF16), vm((2, 6656, 128), BF16),
        pltpu.SemaphoreType.DMA((5,)), pltpu.SemaphoreType.DMA((5,)),
    ]
    smem, vmem = pl.BlockSpec(memory_space=pltpu.SMEM), pl.BlockSpec(memory_space=pltpu.VMEM)
    hbm = pl.BlockSpec(memory_space=pl.ANY)
    half = jax.ShapeDtypeStruct((6656, 128), BF16)
    return pl.pallas_call(
        section_kernel,
        out_shape=(jax.ShapeDtypeStruct((576, 512), BF16), half, half),
        in_specs=[smem, smem] + [vmem] * 8 + [hbm] * 5,
        out_specs=[hbm] * 3,
        scratch_shapes=scratch,
        compiler_params=pltpu.CompilerParams(vmem_limit_bytes=58 * 1024 * 1024),
        cost_estimate=pl.CostEstimate(flops=15_000_000_000, bytes_accessed=12_000_000, transcendentals=2_000_000),
        name="section",
    )(core, level_ids, x, *halo, ids, table, gain[None], w_out, w_qkv, w_proj, w_key, w_value, fields)


from jax.sharding import Mesh, PartitionSpec as P

LAT = ("z_hi", "core")
LON = ("x", "y", "z_lo")
CHIPS = ("z_hi", "x", "y", "z_lo")


def neighbours(axes, by):
    count = 1
    for axis in axes:
        count *= lax.axis_size(axis)
    return [(i, (i + by) % count) for i in range(count)]


def corner_pairs(by):
    n_lat, n_lon = 4, 32
    return [
        (a * n_lon + b, ((a + by) % n_lat) * n_lon + (b + by) % n_lon) for a in range(n_lat) for b in range(n_lon)
    ]


def fetch(tokens, fields):
    below, right, corner = pack(tokens, fields)
    return (
        lax.ppermute(below, LAT, neighbours(LAT, -1)),
        lax.ppermute(right, LON, neighbours(LON, -1)),
        lax.ppermute(corner, LAT + LON, corner_pairs(-1)),
    )


def send_back(tile):
    h, w = tile.shape[0], tile.shape[1]
    above = lax.ppermute(tile[h - SH:, :w - SW], LAT, neighbours(LAT, 1))
    left = lax.ppermute(tile[:h - SH, w - SW:], LON, neighbours(LON, 1))
    corner = lax.ppermute(tile[h - SH:, w - SW:], LAT + LON, corner_pairs(1))
    return above, left, corner


def place_back(tile, above, left, corner):
    h, w = tile.shape[0], tile.shape[1]
    top = jnp.concatenate([corner, above], axis=1)
    bottom = jnp.concatenate([left, tile[:h - SH, :w - SW]], axis=1)
    return jnp.concatenate([top, bottom], axis=0)


def sum_all(keep, send, tile, sent):
    swap = [(0, 1), (1, 0)]
    other = lax.ppermute(send, "core", swap)
    mine = (keep.astype(F32) + other.astype(F32)).astype(BF16)
    pieces = lax.all_to_all(mine.reshape(64, 104, 128), CHIPS, split_axis=0, concat_axis=0, tiled=True)
    piece = jnp.sum(pieces.astype(F32), axis=0).astype(BF16)
    piece, sent = lax.optimization_barrier((piece, sent))
    spread = jnp.broadcast_to(piece[None], (64, 104, 128))
    mine = lax.all_to_all(spread, CHIPS, split_axis=0, concat_axis=0, tiled=True).reshape(6656, 128)
    mine, d_latent = lax.optimization_barrier((mine, place_back(tile, *sent)))
    other = lax.ppermute(mine, "core", swap)
    return mine, other, d_latent


def spread_half(is_first, half_ref, targets, stage, sem):
    qkv_hbm, squares = targets[0], targets[1:]

    def copies(n, act):
        cols = slice(512 * n, 512 * n + 512)

        @pl.when(is_first)
        def _():
            act(pltpu.make_async_copy(stage.at[:, cols], qkv_hbm.at[:, cols], sem.at[n]))

        @pl.when(jnp.logical_not(is_first))
        def _():
            act(pltpu.make_async_copy(stage.at[:, cols], squares[n], sem.at[n]))

    for n in range(3):
        for block in range(4 * n, 4 * n + 4):
            stage[:, 128 * block:128 * block + 128] = half_ref[512 * block:512 * block + 512, :].astype(F32)
        copies(n, lambda copy: copy.start())
    return lambda: [copies(n, lambda copy: copy.wait()) for n in range(3)]


def unpack_mine_kernel(core_ref, mine_ref, qkv_hbm, proj_hbm, key_hbm, value_hbm, stage, sem):
    finish = spread_half(core_ref[0, 0] == 0, mine_ref, (qkv_hbm, proj_hbm, key_hbm, value_hbm), stage, sem)
    finish()


def unpack_other_kernel(
    core_ref, level_ref, mine_hbm, other_ref, qkv_in, proj_in, key_in, value_in,
    qkv_hbm, proj_hbm, key_hbm, value_hbm, out_ref, gain_ref, table_ref, stage, tail_ref, mine_ref, sem, mine_sem,
):
    first = core_ref[0, 0] == 0
    fetch_tail = pltpu.make_async_copy(mine_hbm.at[6144:6400], mine_ref, mine_sem)
    fetch_tail.start()
    finish = spread_half(
        jnp.logical_not(first), other_ref, (qkv_hbm, proj_hbm, key_hbm, value_hbm), stage, sem
    )
    fetch_tail.wait()
    for hp in range(4):
        at_row = 128 * (hp % 2)
        mine, other = mine_ref[at_row:at_row + 128, :], other_ref[6144 + at_row:6144 + at_row + 128, :]
        chosen = jnp.where(first, mine, other) if hp < 2 else jnp.where(first, other, mine)
        tail_ref[:, 128 * hp:128 * hp + 128] = chosen.astype(F32).T
    out_ref[...] = tail_ref[0:80, :]
    gain_ref[...] = tail_ref[96:97, :]
    row = lax.broadcasted_iota(jnp.int32, (37, 512), 0)
    table = jnp.zeros((37, 512), F32)
    for p in range(13):
        table = table + jnp.where(row == level_ref[p], tail_ref[80 + p:81 + p, :], 0.0)
    table_ref[...] = table
    finish()


def unpack(core, level_ids, mine, other):
    shape = lambda *dims: jax.ShapeDtypeStruct(dims, F32)
    smem, vmem = pl.BlockSpec(memory_space=pltpu.SMEM), pl.BlockSpec(memory_space=pltpu.VMEM)
    hbm = pl.BlockSpec(memory_space=pl.ANY)
    matrices = (shape(512, 1536), shape(512, 512), shape(512, 512), shape(512, 512))
    cost = pl.CostEstimate(flops=3_000_000, bytes_accessed=6_000_000, transcendentals=0)
    params = pltpu.CompilerParams(vmem_limit_bytes=24 * 1024 * 1024)
    sem, stage = pltpu.SemaphoreType.DMA((3,)), pltpu.VMEM((512, 1536), F32)
    halves = pl.pallas_call(
        unpack_mine_kernel,
        out_shape=matrices,
        in_specs=[smem, vmem],
        out_specs=[hbm] * 4,
        scratch_shapes=[stage, sem],
        compiler_params=params,
        cost_estimate=cost,
        name="unpack_mine",
    )(core, mine)
    return pl.pallas_call(
        unpack_other_kernel,
        out_shape=matrices + (shape(80, 512), shape(1, 512), shape(37, 512)),
        in_specs=[smem, smem, hbm, vmem] + [hbm] * 4,
        out_specs=[hbm] * 4 + [vmem] * 3,
        scratch_shapes=[
            stage, pltpu.VMEM((128, 512), F32), pltpu.VMEM((256, 128), BF16), sem, pltpu.SemaphoreType.DMA,
        ],
        input_output_aliases={4: 0, 5: 1, 6: 2, 7: 3},
        compiler_params=params,
        cost_estimate=cost,
        name="unpack_other",
    )(core, level_ids, mine, other, *halves)


def shards(
    latent, grad_fields, region_ids, level_ids, w_qkv, w_proj, gain, level_table, w_key, w_value, w_out
):
    core = lax.axis_index("core")
    tokens = latent.reshape(576, 512)
    fields = grad_fields.transpose(0, 2, 1, 3)
    out, keep, send = section(
        core.reshape(1, 1), level_ids, tokens, fields, fetch(tokens, fields), region_ids, level_table, w_qkv, w_proj,
        gain, w_key, w_value, w_out.T,
    )
    tile = out.reshape(12, 24, 2, 512)
    mine, other, d_latent = sum_all(keep, send, tile, send_back(tile))
    grad_qkv, grad_proj, grad_key, grad_value, out_t, grad_gain, table = unpack(core.reshape(1, 1), level_ids, mine, other)
    return d_latent, grad_qkv, grad_proj, grad_gain[0], table, grad_key, grad_value, out_t.T


def solution(mesh):
    fine = Mesh(mesh.devices.reshape(2, 2, 4, 4, 2), LAT + LON)
    tile = P(LAT, LON, None, None)
    return jax.shard_map(
        shards,
        mesh=fine,
        in_specs=(tile, tile, P(LAT, LON)) + (P(),) * 8,
        out_specs=(tile,) + (P(),) * 7,
        check_vma=False,
    )
```

```python
import functools
import jax
import jax.numpy as jnp
from jax import lax
from jax.experimental import pallas as pl
from jax.experimental.pallas import tpu as pltpu

HEADS = 8
WH = 6
WW = 12
LV = 2
SH = 3
SW = 6
EPS = 1e-05
MASKED = -1e30
F32 = jnp.float32
BF16 = jnp.bfloat16


def dot_nn(a, b):
    return lax.dot_general(a, b, (((1,), (0,)), ((), ())), preferred_element_type=F32)


def dot_nt(a, b):
    return lax.dot_general(a, b, (((1,), (1,)), ((), ())), preferred_element_type=F32)


def dot_tn(a, b):
    return lax.dot_general(a, b, (((0,), (0,)), ((), ())), preferred_element_type=F32)


def swap_rows(a):
    rows, lanes = a.shape
    blocks = a.reshape(rows // 8, 8, lanes)
    later = pltpu.roll(blocks, 7, 1)
    earlier = pltpu.roll(blocks, 1, 1)
    even = lax.broadcasted_iota(jnp.int32, blocks.shape, 1) % 2 == 0
    return jnp.where(even, later, earlier).reshape(rows, lanes)


def nine_tiles(levels):
    lane = lax.broadcasted_iota(jnp.int32, levels.shape[1:], 1)
    tiles = [levels[p] for p in range(9)]
    for m in range(4):
        extra = levels[9 + m]
        tiles[2 * m] = jnp.where(lane < 80, tiles[2 * m], pltpu.roll(extra, 80, 1))
        tiles[2 * m + 1] = jnp.where(lane < 80, tiles[2 * m + 1], pltpu.roll(extra, 32, 1))
    return jnp.stack(tiles, axis=0)


def all_levels(tiles):
    lane = lax.broadcasted_iota(jnp.int32, tiles.shape[1:], 1)
    levels = [tiles[p] for p in range(9)]
    for m in range(4):
        levels.append(
            jnp.where(lane < 48, pltpu.roll(tiles[2 * m], 48, 1), pltpu.roll(tiles[2 * m + 1], 96, 1))
        )
    return jnp.stack(levels, axis=0)[:, :, :80]


def row_of_tile():
    return lax.broadcasted_iota(jnp.int32, (8, 128), 0)


def side_tiles(line, levels):
    row = row_of_tile()
    tiles = [line[0:8, 128 * c:128 * c + 128] for c in range(4)]
    for m in range(2):
        left, right = (line[8:16, 128 * c:128 * c + 128] for c in (2 * m, 2 * m + 1))
        tiles.append(jnp.where(row < 4, left, pltpu.roll(right, 4, 0)))
    places = []
    for m in range(2):
        for i in range(3):
            places.append(jnp.where(row < 6, levels[4 * m + i], pltpu.roll(levels[4 * m + 3], 6 - 2 * i, 0)))
    return tiles, places + [levels[8]]


def side_levels(places):
    row = row_of_tile()
    out = []
    for m in range(2):
        first, second, third = places[3 * m:3 * m + 3]
        last = jnp.where(
            row < 2, pltpu.roll(first, 2, 0), jnp.where(row < 4, pltpu.roll(second, 4, 0), pltpu.roll(third, 6, 0))
        )
        out += [first, second, third, last]
    return jnp.stack(out + [places[6]], axis=0)


def pack_kernel(x_ref, f_ref, below_ref, right_ref, corner_ref, wide):
    row = row_of_tile()
    full, halves, lines, sides = [], [], [], ([], [])
    for h in range(12):
        wide[h, :, :, 0:80] = f_ref[h].astype(F32)
        line = x_ref[48 * h:48 * h + 48, :].astype(F32)
        tiles, places = side_tiles(line[0:16], nine_tiles(wide[h, :, 0:8, :]))
        sides[0].append(tiles)
        sides[1].append(places)
        if h < 3:
            for c in range(4):
                full += [line[8 * n:8 * n + 8, 128 * c:128 * c + 128] for n in range(2, 6)]
            for m in range(2):
                left, right = (line[8:16, 128 * c:128 * c + 128] for c in (2 * m, 2 * m + 1))
                halves.append(jnp.where(row < 4, pltpu.roll(right, 4, 0), left))
            levels = nine_tiles(wide[h])
            for k in range(9):
                lines += [levels[k, 8:16], levels[k, 16:24]]
            for q in range(2):
                four = [pltpu.roll(levels[4 * q + i, 0:8], (8 - 2 * i) % 8, 0) for i in range(4)]
                low = jnp.where(row < 2, four[3], four[2])
                lines.append(jnp.where(row < 4, low, jnp.where(row < 6, four[1], four[0])))
            lines.append(levels[8, 0:8])
    below_ref[...] = jnp.concatenate(full + halves + lines, axis=0).astype(BF16)
    right_ref[...] = jnp.concatenate(sum(sides[0][3:], []) + sum(sides[1][3:], []), axis=0).astype(BF16)
    corner_ref[...] = jnp.concatenate(sum(sides[0][:3], []) + sum(sides[1][:3], []), axis=0).astype(BF16)


def pack(x, fields):
    vmem = pl.BlockSpec(memory_space=pltpu.VMEM)
    return pl.pallas_call(
        pack_kernel,
        out_shape=tuple(jax.ShapeDtypeStruct((rows, 128), BF16) for rows in (936, 936, 312)),
        in_specs=[vmem, vmem],
        out_specs=[vmem] * 3,
        scratch_shapes=[pltpu.VMEM((12, 13, 24, 128), F32)],
        compiler_params=pltpu.CompilerParams(vmem_limit_bytes=16 * 1024 * 1024),
        cost_estimate=pl.CostEstimate(flops=2_000_000, bytes_accessed=3_000_000, transcendentals=0),
        name="pack",
    )(x, fields)


def section_kernel(
    core_ref, level_ref, x_ref, below_ref, right_ref, corner_ref, ids_ref, table_ref, gain_ref, wout_ref,
    wqkv_hbm, wproj_hbm, wkey_hbm, wval_hbm, f_hbm,
    out_hbm, keep_hbm, send_hbm,
    xw32, xw, pk, probs, at, nrm, inv, mix32, mixb, kk, vv, uu, ww, cc, ds, gg, dkd, dvd, dm32, dp32, dpb, dat, dpk, hs, at_t, x_t, hot, q32, qs, wo128, f_below, f_right, f_corner,
    wqkv_ref, wproj_ref, wkey_ref, wval_ref, f_ref, out_ref, grads_ref, in_sem, out_sem,
):
    n_win = 4
    tok = 144
    rows = 576
    core = core_ref[0, 0]
    loads = [
        pltpu.make_async_copy(source, target, in_sem.at[n])
        for n, (source, target) in enumerate(
            (
                (wqkv_hbm, wqkv_ref), (wproj_hbm, wproj_ref), (wkey_hbm, wkey_ref), (wval_hbm, wval_ref),
                (f_hbm, f_ref),
            )
        )
    ]
    for load in loads:
        load.start()

    def put(half_no, block, matrix):
        for c in range(matrix.shape[1] // 128):
            at_row = 512 * (block + c)
            piece = matrix[:, 128 * c:128 * c + 128].astype(BF16)
            grads_ref[half_no ^ core, at_row:at_row + 512, :] = piece

    lane = lax.broadcasted_iota(jnp.int32, (1, 128), 1)
    half = ((lane < 64).astype(BF16), (lane >= 64).astype(BF16))
    eighth = (half[0] * jnp.asarray(0.125, BF16), half[1] * jnp.asarray(0.125, BF16))
    low = lax.broadcasted_iota(jnp.int32, (tok, 128), 1) < 64
    gain = gain_ref[...]

    wide = table_ref[...].astype(F32)
    table_row = lax.broadcasted_iota(jnp.int32, wide.shape, 0)
    for p in range(13):
        q32[8 * p:8 * p + 8, :] = jnp.broadcast_to(
            jnp.sum(jnp.where(table_row == level_ref[p], wide, 0.0), axis=0, keepdims=True), (8, 512)
        )
    q32[104:128, :] = jnp.zeros((24, 512), F32)
    qs[...] = q32[...].astype(BF16)
    wo128[...] = jnp.zeros((512, 128), BF16)
    wo128[:, 0:80] = wout_ref[...].T

    ids = ids_ref[...].astype(F32)
    token = lax.broadcasted_iota(jnp.int32, (tok, 24), 0)
    spot = lax.broadcasted_iota(jnp.int32, (tok, 24), 1)
    tok12 = lax.broadcasted_iota(jnp.int32, (tok, 12), 0)
    row12 = lax.broadcasted_iota(jnp.int32, (tok, 12), 1)
    kind = lax.broadcasted_iota(jnp.int32, (tok, 128), 1).astype(F32)
    for w in range(n_win):
        pick = (tok12 // 24 + 6 * (w // 2) == row12).astype(F32)
        line = dot_nn(pick, ids)
        own_id = jnp.sum(
            jnp.where(spot == 12 * (w % 2) + (token % 24) // 2, line, 0.0), axis=1, keepdims=True
        )
        hot[w] = (own_id == kind).astype(BF16)

    row8 = row_of_tile()
    below = below_ref[...].astype(F32).reshape(117, 8, 128)
    right = right_ref[...].astype(F32).reshape(117, 8, 128)
    corner = corner_ref[...].astype(F32).reshape(39, 8, 128)
    for h in range(9):
        f_right[h] = side_levels([right[54 + 7 * h + n] for n in range(7)])
    for h in range(3):
        f_corner[h] = side_levels([corner[18 + 7 * h + n] for n in range(7)])
        for k in range(9):
            at_tile = 54 + 21 * h
            f_below[h, k, 0:8, :] = pltpu.roll(below[at_tile + 18 + k // 4], 2 * (k % 4), 0)
            f_below[h, k, 8:16, :] = below[at_tile + 2 * k]
            f_below[h, k, 16:24, :] = below[at_tile + 2 * k + 1]
    for h in range(12):
        side = right[6 * h:6 * h + 6] if h < 9 else corner[6 * (h - 9):6 * (h - 9) + 6]
        for c in range(4):
            cols = slice(128 * c, 128 * c + 128)
            if h < 9:
                main = x_ref[48 * (h + 3):48 * (h + 3) + 48, cols].astype(F32)
                line = [main[8 * n:8 * n + 8] for n in range(1, 6)]
            else:
                half_tile = below[48 + 2 * (h - 9) + c // 2]
                line = [half_tile if c % 2 == 0 else pltpu.roll(half_tile, 4, 0)]
                line += [below[16 * (h - 9) + 4 * c + n] for n in range(4)]
            half_tile = side[4 + c // 2]
            line += [side[c], half_tile if c % 2 == 0 else pltpu.roll(half_tile, 4, 0)]
            turned = [pltpu.roll(tile, 4, 0) for tile in line]
            piece = [jnp.where(row8 < 4, turned[n], turned[n + 1]) for n in range(6)]
            for b in range(2):
                xw32[(h // 6) * 2 + b, 24 * (h % 6):24 * (h % 6) + 24, cols] = jnp.concatenate(
                    piece[3 * b:3 * b + 3], axis=0
                )
    for w in range(n_win):
        xw[w] = xw32[w].astype(BF16)
    flat_x = xw[...].reshape(rows, 512)
    loads[0].wait()
    x_t[...] = flat_x.T
    for n in range(6):
        part = dot_nn(flat_x, wqkv_ref[:, 256 * n:256 * n + 256]).astype(BF16)
        pk[:, :, 256 * n:256 * n + 256] = part.reshape(n_win, tok, 256)

    def attend(w, carry):
        same = dot_nt(hot[w], hot[w])
        bias = (same - 1.0) * -MASKED
        for hp in range(4):
            cols = slice(128 * hp, 128 * hp + 128)
            q = pk[w, :, 128 * hp:128 * hp + 128]
            k = pk[w, :, 512 + 128 * hp:512 + 128 * hp + 128]
            v_t = pk[w, :, 1024 + 128 * hp:1024 + 128 * hp + 128].T
            outs = []
            both = dot_nt(jnp.concatenate([k * eighth[0], k * eighth[1]], axis=0), q)
            for e in range(2):
                s = both[tok * e:tok * e + tok] + bias
                p = jnp.exp(s - jnp.max(s, axis=0, keepdims=True))
                p = p * (1.0 / jnp.sum(p, axis=0, keepdims=True))
                probs[w, 2 * hp + e] = p
                outs.append(dot_nn(v_t[64 * e:64 * e + 64], p.astype(BF16)))
            o_t = jnp.concatenate(outs, axis=0).astype(BF16)
            at_t[w, cols, :] = o_t
            at[w, :, cols] = o_t.T
        return carry

    lax.fori_loop(0, n_win, attend, 0)

    flat_at = at[...].reshape(rows, 512)
    loads[1].wait()
    nrm[...] = dot_nn(flat_at, wproj_ref[...]).reshape(n_win, tok, 512)
    for w in range(n_win):
        for i in range(6):
            at_row = 48 * (6 * (w // 2) + i) + 24 * (w % 2)
            p = nrm[w, 24 * i:24 * i + 24, :]
            c = p - jnp.mean(p, axis=-1, keepdims=True)
            r = lax.rsqrt(jnp.mean(c * c, axis=-1, keepdims=True) + EPS)
            n = c * r
            nrm[w, 24 * i:24 * i + 24, :] = n
            inv[w, 24 * i:24 * i + 24, :] = jnp.broadcast_to(r, (24, 128))
            mix32[at_row:at_row + 24, :] = xw32[w, 24 * i:24 * i + 24, :] + n * gain
    mixb[...] = mix32[...].astype(BF16)

    mixed = mixb[...]
    for load in loads[2:]:
        load.wait()
    for hp in range(4):
        cols = slice(128 * hp, 128 * hp + 128)
        for w_ref, pair in ((wkey_ref, kk), (wval_ref, vv)):
            part = dot_nn(mixed, w_ref[:, cols]).astype(BF16)
            other = swap_rows(part.astype(F32))
            pair[hp, :, 0:128] = part
            pair[hp, :, 128:256] = (-other).astype(BF16)

    row16 = lax.broadcasted_iota(jnp.int32, (16, 128), 0)
    lane16 = lax.broadcasted_iota(jnp.int32, (16, 128), 1)
    own = (row16 // 2 == lane16 % 8).astype(F32)[None]
    zero64 = jnp.zeros((64, 128), BF16)
    for hp in range(4):
        cols = slice(128 * hp, 128 * hp + 128)
        q = qs[:, cols] * jnp.asarray(0.125, BF16)
        q_e, q_o = q * half[0], q * half[1]
        rhs = jnp.concatenate(
            [jnp.concatenate([q_e, q_e], axis=1), jnp.concatenate([q_o, q_o], axis=1)], axis=0
        )
        diff = dot_nt(kk[hp], rhs)
        wo = wo128[cols, :]
        top = jnp.concatenate(
            [jnp.concatenate([wo[:64], zero64], axis=0), jnp.concatenate([zero64, wo[64:]], axis=0)], axis=1
        )
        u = dot_nn(vv[hp], jnp.concatenate([top, top], axis=0)).astype(BF16)
        for e in range(2):
            d = diff[:, 128 * e:128 * e + 128].reshape(36, 16, 128)
            small = jnp.exp(-jnp.abs(d))
            big = 1.0 / (1.0 + small)
            small = small * big
            weight = jnp.where(d >= 0, big, small)
            ww[2 * hp + e] = (weight * own).astype(BF16).reshape(rows, 128)
            cc[2 * hp + e] = (small * big * (own * 0.125)).reshape(rows, 128)
            uu[2 * hp + e] = u[:, 128 * e:128 * e + 128]

    gg[...] = jnp.zeros((8, rows, 128), BF16)

    edge = lax.broadcasted_iota(jnp.int32, (13, 8, 80), 1) < 2

    def groups(h, tiles):
        turned = [pltpu.roll(tile, 2, 1) for tile in tiles]
        for o in range(3):
            g16 = pl.ds(pl.multiple_of(48 * h + 16 * o, 16), 16)
            f = jnp.where(edge, turned[o], turned[o + 1]).reshape(104, 80)
            f = jnp.concatenate([f, jnp.zeros((24, 80), F32)], axis=0).astype(BF16)
            dw = dot_nt(uu[:, g16, 0:80].reshape(128, 80), f)
            d = (dw * cc[:, g16, :].reshape(128, 128)).astype(BF16)
            ds[:, g16, :] = d.reshape(8, 16, 128)
            g = dot_nn(ww[:, g16, :].reshape(128, 128), f).astype(BF16)
            gg[:, g16, 0:80] = g.reshape(8, 16, 80)

    def near(h, carry):
        own = f_ref[h + 3].astype(F32)
        groups(h, [own[:, 0:8], own[:, 8:16], own[:, 16:24], all_levels(f_right[h])])
        return carry

    def far(h, carry):
        own = all_levels(f_below[h])
        groups(h + 9, [own[:, 0:8], own[:, 8:16], own[:, 16:24], all_levels(f_corner[h])])
        return carry

    lax.fori_loop(0, 9, near, 0, unroll=9)
    lax.fori_loop(0, 3, far, 0, unroll=3)

    fold_row = lax.broadcasted_iota(jnp.int32, (128, 128), 0)
    fold_lane = lax.broadcasted_iota(jnp.int32, (128, 128), 1)
    fold = (fold_row // 8 == fold_lane - 80).astype(BF16)
    for hp in range(4):
        cols = slice(128 * hp, 128 * hp + 128)
        q = qs[:, cols]
        d = jnp.concatenate([ds[2 * hp], ds[2 * hp + 1]], axis=1)
        g = jnp.concatenate([gg[2 * hp], gg[2 * hp + 1]], axis=1)
        dkd[:, cols] = dot_nn(d, jnp.concatenate([q * half[0], q * half[1]], axis=0)).astype(BF16)
        wo = wo128[cols, :]
        top = jnp.concatenate(
            [jnp.concatenate([wo[:64], zero64], axis=0), jnp.concatenate([zero64, wo[64:]], axis=0)], axis=1
        )
        dvd[:, cols] = dot_nt(g, top).astype(BF16)
        dq = dot_tn(kk[hp, :, 0:128], d)
        dq = jnp.concatenate([dq[:64, :128], dq[64:, 128:]], axis=0)
        go = dot_tn(vv[hp, :, 0:128], g)
        go = jnp.concatenate([go[:64, :128], go[64:, 128:]], axis=0)
        dq_hi = dq.astype(BF16)
        dq_lo = (dq - dq_hi.astype(F32)).astype(BF16)
        hs[:, cols] = go + dot_nn(dq_hi, fold) + dot_nn(dq_lo, fold)

    d_mix = dot_nt(dkd[...], wkey_ref[...]) + dot_nt(dvd[...], wval_ref[...])
    dm32[...] = d_mix.astype(BF16).astype(F32)
    mixed_t = mixed.T
    put(1, 4, dot_nn(mixed_t, dkd[...]))
    put(1, 8, dot_nn(mixed_t, dvd[...]))

    total_gain = jnp.zeros((8, 512), F32)
    for w in range(n_win):
        for i in range(6):
            at_row = 48 * (6 * (w // 2) + i) + 24 * (w % 2)
            g = dm32[at_row:at_row + 24, :]
            n = nrm[w, 24 * i:24 * i + 24, :]
            total_gain = total_gain + jnp.sum((g * n).reshape(3, 8, 512), axis=0)
            gn = g * gain
            m1 = jnp.mean(gn, axis=-1, keepdims=True)
            m2 = jnp.mean(gn * n, axis=-1, keepdims=True)
            r = inv[w, 24 * i:24 * i + 24, 0:1]
            dp32[w, 24 * i:24 * i + 24, :] = r * (gn - m1 - n * m2)
    row_gain = jnp.broadcast_to(jnp.sum(total_gain, axis=0, keepdims=True), (128, 512))
    for hp in range(4):
        cols = slice(128 * hp, 128 * hp + 128)
        column = row_gain[:, cols].T
        lanes = lax.broadcasted_iota(jnp.int32, (128, 128), 1)
        tail = jnp.where(lanes == 96, column, hs[:, cols]).astype(BF16)
        at_row = 6144 + 128 * (hp % 2)
        grads_ref[(hp // 2) ^ core, at_row:at_row + 128, :] = tail
    for half_no in range(2):
        grads_ref[half_no, 6400:6656, :] = jnp.zeros((256, 128), BF16)
    for w in range(n_win):
        dpb[w] = dp32[w].astype(BF16)
    flat_dp = dpb[...].reshape(rows, 512)
    total = dot_nn(at_t[0], dpb[0])
    for w in range(1, n_win):
        total = total + dot_nn(at_t[w], dpb[w])
    put(1, 0, total)
    dat[...] = dot_nt(flat_dp, wproj_ref[...]).astype(BF16).reshape(n_win, tok, 512)

    early_keep = pltpu.make_async_copy(grads_ref.at[0], keep_hbm, out_sem.at[0])
    early_send = pltpu.make_async_copy(grads_ref.at[1], send_hbm, out_sem.at[1])
    late_keep = pltpu.make_async_copy(grads_ref.at[0], keep_hbm, out_sem.at[2])
    late_send = pltpu.make_async_copy(grads_ref.at[1], send_hbm, out_sem.at[3])

    @pl.when(core == 1)
    def _():
        early_keep.start()

    @pl.when(core == 0)
    def _():
        early_send.start()

    def unattend(w, carry):
        for hp in range(4):
            cols = slice(128 * hp, 128 * hp + 128)
            q = pk[w, :, 128 * hp:128 * hp + 128]
            k_t = pk[w, :, 512 + 128 * hp:512 + 128 * hp + 128].T
            v = pk[w, :, 1024 + 128 * hp:1024 + 128 * hp + 128]
            da = dat[w, :, cols]
            both = dot_nt(jnp.concatenate([v * eighth[0], v * eighth[1]], axis=0), da)
            ps, ss, dqs = [], [], []
            for e in range(2):
                p = probs[w, 2 * hp + e]
                dw = both[tok * e:tok * e + tok]
                s = (p * (dw - jnp.sum(p * dw, axis=0, keepdims=True))).astype(BF16)
                ps.append(p.astype(BF16))
                ss.append(s)
                dqs.append(dot_nn(k_t[64 * e:64 * e + 64], s))
            dv = dot_nn(jnp.concatenate(ps, axis=0), da)
            dk = dot_nn(jnp.concatenate(ss, axis=0), q)
            dpk[w, :, cols] = jnp.concatenate(dqs, axis=0).astype(BF16).T
            dpk[w, :, 512 + 128 * hp:512 + 128 * hp + 128] = jnp.where(low, dk[:tok], dk[tok:]).astype(BF16)
            dpk[w, :, 1024 + 128 * hp:1024 + 128 * hp + 128] = jnp.where(low, dv[:tok], dv[tok:]).astype(BF16)
        return carry

    lax.fori_loop(0, n_win, unattend, 0)

    flat_d = dpk[...].reshape(rows, 1536)
    for n in range(3):
        put(0, 4 * n, dot_nn(x_t[...], flat_d[:, 512 * n:512 * n + 512]))

    @pl.when(core == 0)
    def _():
        late_keep.start()

    @pl.when(core == 1)
    def _():
        late_send.start()

    dp32[...] = dot_nt(flat_d, wqkv_ref[...]).reshape(n_win, tok, 512)
    for h in range(12):
        parts = []
        for b in range(2):
            at_row = 48 * h + 24 * b
            parts.append(
                dp32[(h // 6) * 2 + b, 24 * (h % 6):24 * (h % 6) + 24, :] + dm32[at_row:at_row + 24, :]
            )
        out_ref[48 * h:48 * h + 48, :] = jnp.concatenate(parts, axis=0).astype(BF16)
    result = pltpu.make_async_copy(out_ref, out_hbm, out_sem.at[4])
    result.start()

    @pl.when(core == 0)
    def _():
        early_send.wait()
        late_keep.wait()

    @pl.when(core == 1)
    def _():
        early_keep.wait()
        late_send.wait()

    result.wait()


def section(core, level_ids, x, fields, halo, ids, table, w_qkv, w_proj, gain, w_key, w_value, w_out):
    vm = lambda shape, kind: pltpu.VMEM(shape, kind)
    scratch = [
        vm((4, 144, 512), F32), vm((4, 144, 512), BF16), vm((4, 144, 1536), BF16), vm((4, 8, 144, 144), F32),
        vm((4, 144, 512), BF16), vm((4, 144, 512), F32), vm((4, 144, 128), F32), vm((576, 512), F32),
        vm((576, 512), BF16), vm((4, 576, 256), BF16), vm((4, 576, 256), BF16), vm((8, 576, 128), BF16),
        vm((8, 576, 128), BF16), vm((8, 576, 128), F32), vm((8, 576, 128), BF16), vm((8, 576, 128), BF16),
        vm((576, 512), BF16), vm((576, 512), BF16), vm((576, 512), F32), vm((4, 144, 512), F32),
        vm((4, 144, 512), BF16), vm((4, 144, 512), BF16), vm((4, 144, 1536), BF16), vm((128, 512), F32),
        vm((4, 512, 144), BF16), vm((512, 576), BF16), vm((4, 144, 128), BF16), vm((128, 512), F32),
        vm((128, 512), BF16), vm((512, 128), BF16), vm((3, 9, 24, 128), F32), vm((9, 9, 8, 128), F32),
        vm((3, 9, 8, 128), F32),
        vm((512, 1536), BF16), vm((512, 512), BF16), vm((512, 512), BF16), vm((512, 512), BF16),
        vm((12, 13, 24, 80), BF16), vm((576, 512), BF16), vm((2, 6656, 128), BF16),
        pltpu.SemaphoreType.DMA((5,)), pltpu.SemaphoreType.DMA((5,)),
    ]
    smem, vmem = pl.BlockSpec(memory_space=pltpu.SMEM), pl.BlockSpec(memory_space=pltpu.VMEM)
    hbm = pl.BlockSpec(memory_space=pl.ANY)
    half = jax.ShapeDtypeStruct((6656, 128), BF16)
    return pl.pallas_call(
        section_kernel,
        out_shape=(jax.ShapeDtypeStruct((576, 512), BF16), half, half),
        in_specs=[smem, smem] + [vmem] * 8 + [hbm] * 5,
        out_specs=[hbm] * 3,
        scratch_shapes=scratch,
        compiler_params=pltpu.CompilerParams(vmem_limit_bytes=52 * 1024 * 1024),
        cost_estimate=pl.CostEstimate(flops=15_000_000_000, bytes_accessed=12_000_000, transcendentals=2_000_000),
        name="section",
    )(core, level_ids, x, *halo, ids, table, gain[None], w_out, w_qkv, w_proj, w_key, w_value, fields)


from jax.sharding import Mesh, PartitionSpec as P

LAT = ("z_hi", "core")
LON = ("x", "y", "z_lo")
CHIPS = ("z_hi", "x", "y", "z_lo")


def neighbours(axes, by):
    count = 1
    for axis in axes:
        count *= lax.axis_size(axis)
    return [(i, (i + by) % count) for i in range(count)]


def corner_pairs(by):
    n_lat, n_lon = 4, 32
    return [
        (a * n_lon + b, ((a + by) % n_lat) * n_lon + (b + by) % n_lon) for a in range(n_lat) for b in range(n_lon)
    ]


def fetch(tokens, fields):
    below, right, corner = pack(tokens, fields)
    return (
        lax.ppermute(below, LAT, neighbours(LAT, -1)),
        lax.ppermute(right, LON, neighbours(LON, -1)),
        lax.ppermute(corner, LAT + LON, corner_pairs(-1)),
    )


def send_back(tile):
    h, w = tile.shape[0], tile.shape[1]
    above = lax.ppermute(tile[h - SH:, :w - SW], LAT, neighbours(LAT, 1))
    left = lax.ppermute(tile[:h - SH, w - SW:], LON, neighbours(LON, 1))
    corner = lax.ppermute(tile[h - SH:, w - SW:], LAT + LON, corner_pairs(1))
    return above, left, corner


def place_back(tile, above, left, corner):
    h, w = tile.shape[0], tile.shape[1]
    top = jnp.concatenate([corner, above], axis=1)
    bottom = jnp.concatenate([left, tile[:h - SH, :w - SW]], axis=1)
    return jnp.concatenate([top, bottom], axis=0)


def sum_all(keep, send, tile, sent):
    swap = [(0, 1), (1, 0)]
    other = lax.ppermute(send, "core", swap)
    mine = (keep.astype(F32) + other.astype(F32)).astype(BF16)
    pieces = lax.all_to_all(mine.reshape(64, 104, 128), CHIPS, split_axis=0, concat_axis=0, tiled=True)
    piece = jnp.sum(pieces.astype(F32), axis=0).astype(BF16)
    spread = jnp.broadcast_to(piece[None], (64, 104, 128))
    mine = lax.all_to_all(spread, CHIPS, split_axis=0, concat_axis=0, tiled=True).reshape(6656, 128)
    mine, d_latent = lax.optimization_barrier((mine, place_back(tile, *sent)))
    other = lax.ppermute(mine, "core", swap)
    return mine, other, d_latent


def spread_half(is_first, half_ref, targets, stage, sem):
    qkv_hbm, squares = targets[0], targets[1:]

    def copies(n, act):
        cols = slice(512 * n, 512 * n + 512)

        @pl.when(is_first)
        def _():
            act(pltpu.make_async_copy(stage.at[:, cols], qkv_hbm.at[:, cols], sem.at[n]))

        @pl.when(jnp.logical_not(is_first))
        def _():
            act(pltpu.make_async_copy(stage.at[:, cols], squares[n], sem.at[n]))

    for n in range(3):
        for block in range(4 * n, 4 * n + 4):
            stage[:, 128 * block:128 * block + 128] = half_ref[512 * block:512 * block + 512, :].astype(F32)
        copies(n, lambda copy: copy.start())
    return lambda: [copies(n, lambda copy: copy.wait()) for n in range(3)]


def unpack_mine_kernel(core_ref, mine_ref, qkv_hbm, proj_hbm, key_hbm, value_hbm, stage, sem):
    finish = spread_half(core_ref[0, 0] == 0, mine_ref, (qkv_hbm, proj_hbm, key_hbm, value_hbm), stage, sem)
    finish()


def unpack_other_kernel(
    core_ref, level_ref, mine_hbm, other_ref, qkv_in, proj_in, key_in, value_in,
    qkv_hbm, proj_hbm, key_hbm, value_hbm, out_ref, gain_ref, table_ref, stage, tail_ref, mine_ref, sem, mine_sem,
):
    first = core_ref[0, 0] == 0
    fetch_tail = pltpu.make_async_copy(mine_hbm.at[6144:6400], mine_ref, mine_sem)
    fetch_tail.start()
    finish = spread_half(
        jnp.logical_not(first), other_ref, (qkv_hbm, proj_hbm, key_hbm, value_hbm), stage, sem
    )
    fetch_tail.wait()
    for hp in range(4):
        at_row = 128 * (hp % 2)
        mine, other = mine_ref[at_row:at_row + 128, :], other_ref[6144 + at_row:6144 + at_row + 128, :]
        chosen = jnp.where(first, mine, other) if hp < 2 else jnp.where(first, other, mine)
        tail_ref[:, 128 * hp:128 * hp + 128] = chosen.astype(F32).T
    out_ref[...] = tail_ref[0:80, :]
    gain_ref[...] = tail_ref[96:97, :]
    row = lax.broadcasted_iota(jnp.int32, (37, 512), 0)
    table = jnp.zeros((37, 512), F32)
    for p in range(13):
        table = table + jnp.where(row == level_ref[p], tail_ref[80 + p:81 + p, :], 0.0)
    table_ref[...] = table
    finish()


def unpack(core, level_ids, mine, other):
    shape = lambda *dims: jax.ShapeDtypeStruct(dims, F32)
    smem, vmem = pl.BlockSpec(memory_space=pltpu.SMEM), pl.BlockSpec(memory_space=pltpu.VMEM)
    hbm = pl.BlockSpec(memory_space=pl.ANY)
    matrices = (shape(512, 1536), shape(512, 512), shape(512, 512), shape(512, 512))
    cost = pl.CostEstimate(flops=3_000_000, bytes_accessed=6_000_000, transcendentals=0)
    params = pltpu.CompilerParams(vmem_limit_bytes=24 * 1024 * 1024)
    sem, stage = pltpu.SemaphoreType.DMA((3,)), pltpu.VMEM((512, 1536), F32)
    halves = pl.pallas_call(
        unpack_mine_kernel,
        out_shape=matrices,
        in_specs=[smem, vmem],
        out_specs=[hbm] * 4,
        scratch_shapes=[stage, sem],
        compiler_params=params,
        cost_estimate=cost,
        name="unpack_mine",
    )(core, mine)
    return pl.pallas_call(
        unpack_other_kernel,
        out_shape=matrices + (shape(80, 512), shape(1, 512), shape(37, 512)),
        in_specs=[smem, smem, hbm, vmem] + [hbm] * 4,
        out_specs=[hbm] * 4 + [vmem] * 3,
        scratch_shapes=[
            stage, pltpu.VMEM((128, 512), F32), pltpu.VMEM((256, 128), BF16), sem, pltpu.SemaphoreType.DMA,
        ],
        input_output_aliases={4: 0, 5: 1, 6: 2, 7: 3},
        compiler_params=params,
        cost_estimate=cost,
        name="unpack_other",
    )(core, level_ids, mine, other, *halves)


def shards(
    latent, grad_fields, region_ids, level_ids, w_qkv, w_proj, gain, level_table, w_key, w_value, w_out
):
    core = lax.axis_index("core")
    tokens = latent.reshape(576, 512)
    fields = grad_fields.transpose(0, 2, 1, 3)
    out, keep, send = section(
        core.reshape(1, 1), level_ids, tokens, fields, fetch(tokens, fields), region_ids, level_table, w_qkv, w_proj,
        gain, w_key, w_value, w_out.T,
    )
    tile = out.reshape(12, 24, 2, 512)
    mine, other, d_latent = sum_all(keep, send, tile, send_back(tile))
    grad_qkv, grad_proj, grad_key, grad_value, out_t, grad_gain, table = unpack(core.reshape(1, 1), level_ids, mine, other)
    return d_latent, grad_qkv, grad_proj, grad_gain[0], table, grad_key, grad_value, out_t.T


def solution(mesh):
    fine = Mesh(mesh.devices.reshape(2, 2, 4, 4, 2), LAT + LON)
    tile = P(LAT, LON, None, None)
    return jax.shard_map(
        shards,
        mesh=fine,
        in_specs=(tile, tile, P(LAT, LON)) + (P(),) * 8,
        out_specs=(tile,) + (P(),) * 7,
        check_vma=False,
    )
```

```python
import functools
import jax
import jax.numpy as jnp
from jax import lax
from jax.experimental import pallas as pl
from jax.experimental.pallas import tpu as pltpu

HEADS = 8
WH = 6
WW = 12
LV = 2
SH = 3
SW = 6
EPS = 1e-05
MASKED = -1e30
F32 = jnp.float32
BF16 = jnp.bfloat16


def dot_nn(a, b):
    return lax.dot_general(a, b, (((1,), (0,)), ((), ())), preferred_element_type=F32)


def dot_nt(a, b):
    return lax.dot_general(a, b, (((1,), (1,)), ((), ())), preferred_element_type=F32)


def dot_tn(a, b):
    return lax.dot_general(a, b, (((0,), (0,)), ((), ())), preferred_element_type=F32)


def swap_rows(a):
    rows, lanes = a.shape
    blocks = a.reshape(rows // 8, 8, lanes)
    later = pltpu.roll(blocks, 7, 1)
    earlier = pltpu.roll(blocks, 1, 1)
    even = lax.broadcasted_iota(jnp.int32, blocks.shape, 1) % 2 == 0
    return jnp.where(even, later, earlier).reshape(rows, lanes)


def nine_tiles(levels):
    lane = lax.broadcasted_iota(jnp.int32, levels.shape[1:], 1)
    tiles = [levels[p] for p in range(9)]
    for m in range(4):
        extra = levels[9 + m]
        tiles[2 * m] = jnp.where(lane < 80, tiles[2 * m], pltpu.roll(extra, 80, 1))
        tiles[2 * m + 1] = jnp.where(lane < 80, tiles[2 * m + 1], pltpu.roll(extra, 32, 1))
    return jnp.stack(tiles, axis=0)


def all_levels(tiles):
    lane = lax.broadcasted_iota(jnp.int32, tiles.shape[1:], 1)
    levels = [tiles[p] for p in range(9)]
    for m in range(4):
        levels.append(
            jnp.where(lane < 48, pltpu.roll(tiles[2 * m], 48, 1), pltpu.roll(tiles[2 * m + 1], 96, 1))
        )
    return jnp.stack(levels, axis=0)[:, :, :80]


def row_of_tile():
    return lax.broadcasted_iota(jnp.int32, (8, 128), 0)


def side_tiles(line, levels):
    row = row_of_tile()
    tiles = [line[0:8, 128 * c:128 * c + 128] for c in range(4)]
    for m in range(2):
        left, right = (line[8:16, 128 * c:128 * c + 128] for c in (2 * m, 2 * m + 1))
        tiles.append(jnp.where(row < 4, left, pltpu.roll(right, 4, 0)))
    places = []
    for m in range(2):
        for i in range(3):
            places.append(jnp.where(row < 6, levels[4 * m + i], pltpu.roll(levels[4 * m + 3], 6 - 2 * i, 0)))
    return tiles, places + [levels[8]]


def side_levels(places):
    row = row_of_tile()
    out = []
    for m in range(2):
        first, second, third = places[3 * m:3 * m + 3]
        last = jnp.where(
            row < 2, pltpu.roll(first, 2, 0), jnp.where(row < 4, pltpu.roll(second, 4, 0), pltpu.roll(third, 6, 0))
        )
        out += [first, second, third, last]
    return jnp.stack(out + [places[6]], axis=0)


def pack_kernel(x_ref, f_ref, below_ref, right_ref, corner_ref, wide):
    row = row_of_tile()
    full, halves, lines, sides = [], [], [], ([], [])
    for h in range(12):
        wide[h, :, :, 0:80] = f_ref[h].astype(F32)
        line = x_ref[48 * h:48 * h + 48, :].astype(F32)
        tiles, places = side_tiles(line[0:16], nine_tiles(wide[h, :, 0:8, :]))
        sides[0].append(tiles)
        sides[1].append(places)
        if h < 3:
            for c in range(4):
                full += [line[8 * n:8 * n + 8, 128 * c:128 * c + 128] for n in range(2, 6)]
            for m in range(2):
                left, right = (line[8:16, 128 * c:128 * c + 128] for c in (2 * m, 2 * m + 1))
                halves.append(jnp.where(row < 4, pltpu.roll(right, 4, 0), left))
            levels = nine_tiles(wide[h])
            for k in range(9):
                lines += [levels[k, 8:16], levels[k, 16:24]]
            for q in range(2):
                four = [pltpu.roll(levels[4 * q + i, 0:8], (8 - 2 * i) % 8, 0) for i in range(4)]
                low = jnp.where(row < 2, four[3], four[2])
                lines.append(jnp.where(row < 4, low, jnp.where(row < 6, four[1], four[0])))
            lines.append(levels[8, 0:8])
    below_ref[...] = jnp.concatenate(full + halves + lines, axis=0).astype(BF16)
    right_ref[...] = jnp.concatenate(sum(sides[0][3:], []) + sum(sides[1][3:], []), axis=0).astype(BF16)
    corner_ref[...] = jnp.concatenate(sum(sides[0][:3], []) + sum(sides[1][:3], []), axis=0).astype(BF16)


def pack(x, fields):
    vmem = pl.BlockSpec(memory_space=pltpu.VMEM)
    return pl.pallas_call(
        pack_kernel,
        out_shape=tuple(jax.ShapeDtypeStruct((rows, 128), BF16) for rows in (936, 936, 312)),
        in_specs=[vmem, vmem],
        out_specs=[vmem] * 3,
        scratch_shapes=[pltpu.VMEM((12, 13, 24, 128), F32)],
        compiler_params=pltpu.CompilerParams(vmem_limit_bytes=16 * 1024 * 1024),
        cost_estimate=pl.CostEstimate(flops=2_000_000, bytes_accessed=3_000_000, transcendentals=0),
        name="pack",
    )(x, fields)


def section_kernel(
    core_ref, level_ref, x_ref, below_ref, right_ref, corner_ref, ids_ref, table_ref, gain_ref, wout_ref,
    wqkv_hbm, wproj_hbm, wkey_hbm, wval_hbm, f_hbm,
    out_hbm, keep_hbm, send_hbm,
    xw32, xw, pk, probs, at, nrm, inv, mix32, mixb, kk, vv, uu, ww, cc, ds, gg, dkd, dvd, dm32, dp32, dpb, dat, dpk, hs, at_t, x_t, hot, q32, qs, wo128, f_below, f_right, f_corner,
    wqkv_ref, wproj_ref, wkey_ref, wval_ref, f_ref, out_ref, grads_ref, in_sem, out_sem,
):
    n_win = 4
    tok = 144
    rows = 576
    core = core_ref[0, 0]
    loads = [
        pltpu.make_async_copy(source, target, in_sem.at[n])
        for n, (source, target) in enumerate(
            (
                (wqkv_hbm, wqkv_ref), (wproj_hbm, wproj_ref), (wkey_hbm, wkey_ref), (wval_hbm, wval_ref),
                (f_hbm, f_ref),
            )
        )
    ]
    for load in loads:
        load.start()

    def put(half_no, block, matrix):
        for c in range(matrix.shape[1] // 128):
            at_row = 512 * (block + c)
            piece = matrix[:, 128 * c:128 * c + 128].astype(BF16)
            grads_ref[half_no ^ core, at_row:at_row + 512, :] = piece

    lane = lax.broadcasted_iota(jnp.int32, (1, 128), 1)
    half = ((lane < 64).astype(BF16), (lane >= 64).astype(BF16))
    eighth = (half[0] * jnp.asarray(0.125, BF16), half[1] * jnp.asarray(0.125, BF16))
    low = lax.broadcasted_iota(jnp.int32, (tok, 128), 1) < 64
    gain = gain_ref[...]

    wide = table_ref[...].astype(F32)
    table_row = lax.broadcasted_iota(jnp.int32, wide.shape, 0)
    for p in range(13):
        q32[8 * p:8 * p + 8, :] = jnp.broadcast_to(
            jnp.sum(jnp.where(table_row == level_ref[p], wide, 0.0), axis=0, keepdims=True), (8, 512)
        )
    q32[104:128, :] = jnp.zeros((24, 512), F32)
    qs[...] = q32[...].astype(BF16)
    wo128[...] = jnp.zeros((512, 128), BF16)
    wo128[:, 0:80] = wout_ref[...].T

    ids = ids_ref[...].astype(F32)
    token = lax.broadcasted_iota(jnp.int32, (tok, 24), 0)
    spot = lax.broadcasted_iota(jnp.int32, (tok, 24), 1)
    tok12 = lax.broadcasted_iota(jnp.int32, (tok, 12), 0)
    row12 = lax.broadcasted_iota(jnp.int32, (tok, 12), 1)
    kind = lax.broadcasted_iota(jnp.int32, (tok, 128), 1).astype(F32)
    for w in range(n_win):
        pick = (tok12 // 24 + 6 * (w // 2) == row12).astype(F32)
        line = dot_nn(pick, ids)
        own_id = jnp.sum(
            jnp.where(spot == 12 * (w % 2) + (token % 24) // 2, line, 0.0), axis=1, keepdims=True
        )
        hot[w] = (own_id == kind).astype(BF16)

    row8 = row_of_tile()
    below = below_ref[...].astype(F32).reshape(117, 8, 128)
    right = right_ref[...].astype(F32).reshape(117, 8, 128)
    corner = corner_ref[...].astype(F32).reshape(39, 8, 128)
    for h in range(9):
        f_right[h] = side_levels([right[54 + 7 * h + n] for n in range(7)])
    for h in range(3):
        f_corner[h] = side_levels([corner[18 + 7 * h + n] for n in range(7)])
        for k in range(9):
            at_tile = 54 + 21 * h
            f_below[h, k, 0:8, :] = pltpu.roll(below[at_tile + 18 + k // 4], 2 * (k % 4), 0)
            f_below[h, k, 8:16, :] = below[at_tile + 2 * k]
            f_below[h, k, 16:24, :] = below[at_tile + 2 * k + 1]
    for h in range(12):
        side = right[6 * h:6 * h + 6] if h < 9 else corner[6 * (h - 9):6 * (h - 9) + 6]
        for c in range(4):
            cols = slice(128 * c, 128 * c + 128)
            if h < 9:
                main = x_ref[48 * (h + 3):48 * (h + 3) + 48, cols].astype(F32)
                line = [main[8 * n:8 * n + 8] for n in range(1, 6)]
            else:
                half_tile = below[48 + 2 * (h - 9) + c // 2]
                line = [half_tile if c % 2 == 0 else pltpu.roll(half_tile, 4, 0)]
                line += [below[16 * (h - 9) + 4 * c + n] for n in range(4)]
            half_tile = side[4 + c // 2]
            line += [side[c], half_tile if c % 2 == 0 else pltpu.roll(half_tile, 4, 0)]
            turned = [pltpu.roll(tile, 4, 0) for tile in line]
            piece = [jnp.where(row8 < 4, turned[n], turned[n + 1]) for n in range(6)]
            for b in range(2):
                xw32[(h // 6) * 2 + b, 24 * (h % 6):24 * (h % 6) + 24, cols] = jnp.concatenate(
                    piece[3 * b:3 * b + 3], axis=0
                )
    for w in range(n_win):
        xw[w] = xw32[w].astype(BF16)
    flat_x = xw[...].reshape(rows, 512)
    loads[0].wait()
    x_t[...] = flat_x.T
    for n in range(6):
        part = dot_nn(flat_x, wqkv_ref[:, 256 * n:256 * n + 256]).astype(BF16)
        pk[:, :, 256 * n:256 * n + 256] = part.reshape(n_win, tok, 256)

    def attend(w, carry):
        same = dot_nt(hot[w], hot[w])
        bias = (same - 1.0) * -MASKED
        for hp in range(4):
            cols = slice(128 * hp, 128 * hp + 128)
            q = pk[w, :, 128 * hp:128 * hp + 128]
            k = pk[w, :, 512 + 128 * hp:512 + 128 * hp + 128]
            v_t = pk[w, :, 1024 + 128 * hp:1024 + 128 * hp + 128].T
            outs = []
            both = dot_nt(jnp.concatenate([k * eighth[0], k * eighth[1]], axis=0), q)
            for e in range(2):
                s = both[tok * e:tok * e + tok] + bias
                p = jnp.exp(s - jnp.max(s, axis=0, keepdims=True))
                p = p * (1.0 / jnp.sum(p, axis=0, keepdims=True))
                probs[w, 2 * hp + e] = p
                outs.append(dot_nn(v_t[64 * e:64 * e + 64], p.astype(BF16)))
            o_t = jnp.concatenate(outs, axis=0).astype(BF16)
            at_t[w, cols, :] = o_t
            at[w, :, cols] = o_t.T
        return carry

    lax.fori_loop(0, n_win, attend, 0)

    flat_at = at[...].reshape(rows, 512)
    loads[1].wait()
    nrm[...] = dot_nn(flat_at, wproj_ref[...]).reshape(n_win, tok, 512)
    for w in range(n_win):
        for i in range(6):
            at_row = 48 * (6 * (w // 2) + i) + 24 * (w % 2)
            p = nrm[w, 24 * i:24 * i + 24, :]
            c = p - jnp.mean(p, axis=-1, keepdims=True)
            r = lax.rsqrt(jnp.mean(c * c, axis=-1, keepdims=True) + EPS)
            n = c * r
            nrm[w, 24 * i:24 * i + 24, :] = n
            inv[w, 24 * i:24 * i + 24, :] = jnp.broadcast_to(r, (24, 128))
            mix32[at_row:at_row + 24, :] = xw32[w, 24 * i:24 * i + 24, :] + n * gain
    mixb[...] = mix32[...].astype(BF16)

    mixed = mixb[...]
    for load in loads[2:]:
        load.wait()
    for hp in range(4):
        cols = slice(128 * hp, 128 * hp + 128)
        for w_ref, pair in ((wkey_ref, kk), (wval_ref, vv)):
            part = dot_nn(mixed, w_ref[:, cols]).astype(BF16)
            other = swap_rows(part.astype(F32))
            pair[hp, :, 0:128] = part
            pair[hp, :, 128:256] = (-other).astype(BF16)

    row16 = lax.broadcasted_iota(jnp.int32, (16, 128), 0)
    lane16 = lax.broadcasted_iota(jnp.int32, (16, 128), 1)
    own = (row16 // 2 == lane16 % 8).astype(F32)[None]
    zero64 = jnp.zeros((64, 128), BF16)
    for hp in range(4):
        cols = slice(128 * hp, 128 * hp + 128)
        q = qs[:, cols] * jnp.asarray(0.125, BF16)
        q_e, q_o = q * half[0], q * half[1]
        rhs = jnp.concatenate(
            [jnp.concatenate([q_e, q_e], axis=1), jnp.concatenate([q_o, q_o], axis=1)], axis=0
        )
        diff = dot_nt(kk[hp], rhs)
        wo = wo128[cols, :]
        top = jnp.concatenate(
            [jnp.concatenate([wo[:64], zero64], axis=0), jnp.concatenate([zero64, wo[64:]], axis=0)], axis=1
        )
        u = dot_nn(vv[hp], jnp.concatenate([top, top], axis=0)).astype(BF16)
        for e in range(2):
            d = diff[:, 128 * e:128 * e + 128].reshape(36, 16, 128)
            small = jnp.exp(-jnp.abs(d))
            big = 1.0 / (1.0 + small)
            small = small * big
            weight = jnp.where(d >= 0, big, small)
            ww[2 * hp + e] = (weight * own).astype(BF16).reshape(rows, 128)
            cc[2 * hp + e] = (small * big * (own * 0.125)).reshape(rows, 128)
            uu[2 * hp + e] = u[:, 128 * e:128 * e + 128]

    gg[...] = jnp.zeros((8, rows, 128), BF16)

    edge = lax.broadcasted_iota(jnp.int32, (13, 8, 80), 1) < 2

    def groups(h, tiles):
        turned = [pltpu.roll(tile, 2, 1) for tile in tiles]
        for o in range(3):
            g16 = pl.ds(pl.multiple_of(48 * h + 16 * o, 16), 16)
            f = jnp.where(edge, turned[o], turned[o + 1]).reshape(104, 80)
            f = jnp.concatenate([f, jnp.zeros((24, 80), F32)], axis=0).astype(BF16)
            dw = dot_nt(uu[:, g16, 0:80].reshape(128, 80), f)
            d = (dw * cc[:, g16, :].reshape(128, 128)).astype(BF16)
            ds[:, g16, :] = d.reshape(8, 16, 128)
            g = dot_nn(ww[:, g16, :].reshape(128, 128), f).astype(BF16)
            gg[:, g16, 0:80] = g.reshape(8, 16, 80)

    def near(h, carry):
        own = f_ref[h + 3].astype(F32)
        groups(h, [own[:, 0:8], own[:, 8:16], own[:, 16:24], all_levels(f_right[h])])
        return carry

    def far(h, carry):
        own = all_levels(f_below[h])
        groups(h + 9, [own[:, 0:8], own[:, 8:16], own[:, 16:24], all_levels(f_corner[h])])
        return carry

    lax.fori_loop(0, 9, near, 0, unroll=9)
    lax.fori_loop(0, 3, far, 0, unroll=3)

    fold_row = lax.broadcasted_iota(jnp.int32, (128, 128), 0)
    fold_lane = lax.broadcasted_iota(jnp.int32, (128, 128), 1)
    fold = (fold_row // 8 == fold_lane - 80).astype(BF16)
    for hp in range(4):
        cols = slice(128 * hp, 128 * hp + 128)
        q = qs[:, cols]
        d = jnp.concatenate([ds[2 * hp], ds[2 * hp + 1]], axis=1)
        g = jnp.concatenate([gg[2 * hp], gg[2 * hp + 1]], axis=1)
        dkd[:, cols] = dot_nn(d, jnp.concatenate([q * half[0], q * half[1]], axis=0)).astype(BF16)
        wo = wo128[cols, :]
        top = jnp.concatenate(
            [jnp.concatenate([wo[:64], zero64], axis=0), jnp.concatenate([zero64, wo[64:]], axis=0)], axis=1
        )
        dvd[:, cols] = dot_nt(g, top).astype(BF16)
        dq = dot_tn(kk[hp, :, 0:128], d)
        dq = jnp.concatenate([dq[:64, :128], dq[64:, 128:]], axis=0)
        go = dot_tn(vv[hp, :, 0:128], g)
        go = jnp.concatenate([go[:64, :128], go[64:, 128:]], axis=0)
        dq_hi = dq.astype(BF16)
        dq_lo = (dq - dq_hi.astype(F32)).astype(BF16)
        hs[:, cols] = go + dot_nn(dq_hi, fold) + dot_nn(dq_lo, fold)

    d_mix = dot_nt(dkd[...], wkey_ref[...]) + dot_nt(dvd[...], wval_ref[...])
    dm32[...] = d_mix.astype(BF16).astype(F32)
    mixed_t = mixed.T
    put(1, 4, dot_nn(mixed_t, dkd[...]))
    put(1, 8, dot_nn(mixed_t, dvd[...]))

    total_gain = jnp.zeros((8, 512), F32)
    for w in range(n_win):
        for i in range(6):
            at_row = 48 * (6 * (w // 2) + i) + 24 * (w % 2)
            g = dm32[at_row:at_row + 24, :]
            n = nrm[w, 24 * i:24 * i + 24, :]
            total_gain = total_gain + jnp.sum((g * n).reshape(3, 8, 512), axis=0)
            gn = g * gain
            m1 = jnp.mean(gn, axis=-1, keepdims=True)
            m2 = jnp.mean(gn * n, axis=-1, keepdims=True)
            r = inv[w, 24 * i:24 * i + 24, 0:1]
            dp32[w, 24 * i:24 * i + 24, :] = r * (gn - m1 - n * m2)
    row_gain = jnp.broadcast_to(jnp.sum(total_gain, axis=0, keepdims=True), (128, 512))
    for hp in range(4):
        cols = slice(128 * hp, 128 * hp + 128)
        column = row_gain[:, cols].T
        lanes = lax.broadcasted_iota(jnp.int32, (128, 128), 1)
        tail = jnp.where(lanes == 96, column, hs[:, cols]).astype(BF16)
        at_row = 6144 + 128 * (hp % 2)
        grads_ref[(hp // 2) ^ core, at_row:at_row + 128, :] = tail
    for half_no in range(2):
        grads_ref[half_no, 6400:6656, :] = jnp.zeros((256, 128), BF16)
    for w in range(n_win):
        dpb[w] = dp32[w].astype(BF16)
    flat_dp = dpb[...].reshape(rows, 512)
    total = dot_nn(at_t[0], dpb[0])
    for w in range(1, n_win):
        total = total + dot_nn(at_t[w], dpb[w])
    put(1, 0, total)
    dat[...] = dot_nt(flat_dp, wproj_ref[...]).astype(BF16).reshape(n_win, tok, 512)

    early_keep = pltpu.make_async_copy(grads_ref.at[0], keep_hbm, out_sem.at[0])
    early_send = pltpu.make_async_copy(grads_ref.at[1], send_hbm, out_sem.at[1])
    late_keep = pltpu.make_async_copy(grads_ref.at[0], keep_hbm, out_sem.at[2])
    late_send = pltpu.make_async_copy(grads_ref.at[1], send_hbm, out_sem.at[3])

    @pl.when(core == 1)
    def _():
        early_keep.start()

    @pl.when(core == 0)
    def _():
        early_send.start()

    def unattend(w, carry):
        for hp in range(4):
            cols = slice(128 * hp, 128 * hp + 128)
            q = pk[w, :, 128 * hp:128 * hp + 128]
            k_t = pk[w, :, 512 + 128 * hp:512 + 128 * hp + 128].T
            v = pk[w, :, 1024 + 128 * hp:1024 + 128 * hp + 128]
            da = dat[w, :, cols]
            both = dot_nt(jnp.concatenate([v * eighth[0], v * eighth[1]], axis=0), da)
            ps, ss, dqs = [], [], []
            for e in range(2):
                p = probs[w, 2 * hp + e]
                dw = both[tok * e:tok * e + tok]
                s = (p * (dw - jnp.sum(p * dw, axis=0, keepdims=True))).astype(BF16)
                ps.append(p.astype(BF16))
                ss.append(s)
                dqs.append(dot_nn(k_t[64 * e:64 * e + 64], s))
            dv = dot_nn(jnp.concatenate(ps, axis=0), da)
            dk = dot_nn(jnp.concatenate(ss, axis=0), q)
            dpk[w, :, cols] = jnp.concatenate(dqs, axis=0).astype(BF16).T
            dpk[w, :, 512 + 128 * hp:512 + 128 * hp + 128] = jnp.where(low, dk[:tok], dk[tok:]).astype(BF16)
            dpk[w, :, 1024 + 128 * hp:1024 + 128 * hp + 128] = jnp.where(low, dv[:tok], dv[tok:]).astype(BF16)
        return carry

    lax.fori_loop(0, n_win, unattend, 0)

    flat_d = dpk[...].reshape(rows, 1536)
    for n in range(3):
        put(0, 4 * n, dot_nn(x_t[...], flat_d[:, 512 * n:512 * n + 512]))

    @pl.when(core == 0)
    def _():
        late_keep.start()

    @pl.when(core == 1)
    def _():
        late_send.start()

    dp32[...] = dot_nt(flat_d, wqkv_ref[...]).reshape(n_win, tok, 512)
    for h in range(12):
        parts = []
        for b in range(2):
            at_row = 48 * h + 24 * b
            parts.append(
                dp32[(h // 6) * 2 + b, 24 * (h % 6):24 * (h % 6) + 24, :] + dm32[at_row:at_row + 24, :]
            )
        out_ref[48 * h:48 * h + 48, :] = jnp.concatenate(parts, axis=0).astype(BF16)
    result = pltpu.make_async_copy(out_ref, out_hbm, out_sem.at[4])
    result.start()

    @pl.when(core == 0)
    def _():
        early_send.wait()
        late_keep.wait()

    @pl.when(core == 1)
    def _():
        early_keep.wait()
        late_send.wait()

    result.wait()


def section(core, level_ids, x, fields, halo, ids, table, w_qkv, w_proj, gain, w_key, w_value, w_out):
    vm = lambda shape, kind: pltpu.VMEM(shape, kind)
    scratch = [
        vm((4, 144, 512), F32), vm((4, 144, 512), BF16), vm((4, 144, 1536), BF16), vm((4, 8, 144, 144), F32),
        vm((4, 144, 512), BF16), vm((4, 144, 512), F32), vm((4, 144, 128), F32), vm((576, 512), F32),
        vm((576, 512), BF16), vm((4, 576, 256), BF16), vm((4, 576, 256), BF16), vm((8, 576, 128), BF16),
        vm((8, 576, 128), BF16), vm((8, 576, 128), F32), vm((8, 576, 128), BF16), vm((8, 576, 128), BF16),
        vm((576, 512), BF16), vm((576, 512), BF16), vm((576, 512), F32), vm((4, 144, 512), F32),
        vm((4, 144, 512), BF16), vm((4, 144, 512), BF16), vm((4, 144, 1536), BF16), vm((128, 512), F32),
        vm((4, 512, 144), BF16), vm((512, 576), BF16), vm((4, 144, 128), BF16), vm((128, 512), F32),
        vm((128, 512), BF16), vm((512, 128), BF16), vm((3, 9, 24, 128), F32), vm((9, 9, 8, 128), F32),
        vm((3, 9, 8, 128), F32),
        vm((512, 1536), BF16), vm((512, 512), BF16), vm((512, 512), BF16), vm((512, 512), BF16),
        vm((12, 13, 24, 80), BF16), vm((576, 512), BF16), vm((2, 6656, 128), BF16),
        pltpu.SemaphoreType.DMA((5,)), pltpu.SemaphoreType.DMA((5,)),
    ]
    smem, vmem = pl.BlockSpec(memory_space=pltpu.SMEM), pl.BlockSpec(memory_space=pltpu.VMEM)
    hbm = pl.BlockSpec(memory_space=pl.ANY)
    half = jax.ShapeDtypeStruct((6656, 128), BF16)
    return pl.pallas_call(
        section_kernel,
        out_shape=(jax.ShapeDtypeStruct((576, 512), BF16), half, half),
        in_specs=[smem, smem] + [vmem] * 8 + [hbm] * 5,
        out_specs=[hbm] * 3,
        scratch_shapes=scratch,
        compiler_params=pltpu.CompilerParams(vmem_limit_bytes=52 * 1024 * 1024),
        cost_estimate=pl.CostEstimate(flops=15_000_000_000, bytes_accessed=12_000_000, transcendentals=2_000_000),
        name="section",
    )(core, level_ids, x, *halo, ids, table, gain[None], w_out, w_qkv, w_proj, w_key, w_value, fields)


from jax.sharding import Mesh, PartitionSpec as P

LAT = ("z_hi", "core")
LON = ("x", "y", "z_lo")
CHIPS = ("x", "y", "z_hi", "z_lo")


def neighbours(axes, by):
    count = 1
    for axis in axes:
        count *= lax.axis_size(axis)
    return [(i, (i + by) % count) for i in range(count)]


def corner_pairs(by):
    n_lat, n_lon = 4, 32
    return [
        (a * n_lon + b, ((a + by) % n_lat) * n_lon + (b + by) % n_lon) for a in range(n_lat) for b in range(n_lon)
    ]


def fetch(tokens, fields):
    below, right, corner = pack(tokens, fields)
    return (
        lax.ppermute(below, LAT, neighbours(LAT, -1)),
        lax.ppermute(right, LON, neighbours(LON, -1)),
        lax.ppermute(corner, LAT + LON, corner_pairs(-1)),
    )


def send_back(tile):
    h, w = tile.shape[0], tile.shape[1]
    above = lax.ppermute(tile[h - SH:, :w - SW], LAT, neighbours(LAT, 1))
    left = lax.ppermute(tile[:h - SH, w - SW:], LON, neighbours(LON, 1))
    corner = lax.ppermute(tile[h - SH:, w - SW:], LAT + LON, corner_pairs(1))
    return above, left, corner


def place_back(tile, above, left, corner):
    h, w = tile.shape[0], tile.shape[1]
    top = jnp.concatenate([corner, above], axis=1)
    bottom = jnp.concatenate([left, tile[:h - SH, :w - SW]], axis=1)
    return jnp.concatenate([top, bottom], axis=0)


def sum_all(keep, send, tile, sent):
    swap = [(0, 1), (1, 0)]
    other = lax.ppermute(send, "core", swap)
    mine = (keep.astype(F32) + other.astype(F32)).astype(BF16)
    pieces = lax.all_to_all(mine.reshape(64, 104, 128), CHIPS, split_axis=0, concat_axis=0, tiled=True)
    piece = jnp.sum(pieces.astype(F32), axis=0).astype(BF16)
    spread = jnp.broadcast_to(piece[None], (64, 104, 128))
    mine = lax.all_to_all(spread, CHIPS, split_axis=0, concat_axis=0, tiled=True).reshape(6656, 128)
    mine, d_latent = lax.optimization_barrier((mine, place_back(tile, *sent)))
    other = lax.ppermute(mine, "core", swap)
    return mine, other, d_latent


def spread_half(is_first, half_ref, targets, stage, sem):
    qkv_hbm, squares = targets[0], targets[1:]

    def copies(n, act):
        cols = slice(512 * n, 512 * n + 512)

        @pl.when(is_first)
        def _():
            act(pltpu.make_async_copy(stage.at[:, cols], qkv_hbm.at[:, cols], sem.at[n]))

        @pl.when(jnp.logical_not(is_first))
        def _():
            act(pltpu.make_async_copy(stage.at[:, cols], squares[n], sem.at[n]))

    for n in range(3):
        for block in range(4 * n, 4 * n + 4):
            stage[:, 128 * block:128 * block + 128] = half_ref[512 * block:512 * block + 512, :].astype(F32)
        copies(n, lambda copy: copy.start())
    return lambda: [copies(n, lambda copy: copy.wait()) for n in range(3)]


def unpack_mine_kernel(core_ref, mine_ref, qkv_hbm, proj_hbm, key_hbm, value_hbm, stage, sem):
    finish = spread_half(core_ref[0, 0] == 0, mine_ref, (qkv_hbm, proj_hbm, key_hbm, value_hbm), stage, sem)
    finish()


def unpack_other_kernel(
    core_ref, level_ref, mine_hbm, other_ref, qkv_in, proj_in, key_in, value_in,
    qkv_hbm, proj_hbm, key_hbm, value_hbm, out_ref, gain_ref, table_ref, stage, tail_ref, mine_ref, sem, mine_sem,
):
    first = core_ref[0, 0] == 0
    fetch_tail = pltpu.make_async_copy(mine_hbm.at[6144:6400], mine_ref, mine_sem)
    fetch_tail.start()
    finish = spread_half(
        jnp.logical_not(first), other_ref, (qkv_hbm, proj_hbm, key_hbm, value_hbm), stage, sem
    )
    fetch_tail.wait()
    for hp in range(4):
        at_row = 128 * (hp % 2)
        mine, other = mine_ref[at_row:at_row + 128, :], other_ref[6144 + at_row:6144 + at_row + 128, :]
        chosen = jnp.where(first, mine, other) if hp < 2 else jnp.where(first, other, mine)
        tail_ref[:, 128 * hp:128 * hp + 128] = chosen.astype(F32).T
    out_ref[...] = tail_ref[0:80, :]
    gain_ref[...] = tail_ref[96:97, :]
    row = lax.broadcasted_iota(jnp.int32, (37, 512), 0)
    table = jnp.zeros((37, 512), F32)
    for p in range(13):
        table = table + jnp.where(row == level_ref[p], tail_ref[80 + p:81 + p, :], 0.0)
    table_ref[...] = table
    finish()


def unpack(core, level_ids, mine, other):
    shape = lambda *dims: jax.ShapeDtypeStruct(dims, F32)
    smem, vmem = pl.BlockSpec(memory_space=pltpu.SMEM), pl.BlockSpec(memory_space=pltpu.VMEM)
    hbm = pl.BlockSpec(memory_space=pl.ANY)
    matrices = (shape(512, 1536), shape(512, 512), shape(512, 512), shape(512, 512))
    cost = pl.CostEstimate(flops=3_000_000, bytes_accessed=6_000_000, transcendentals=0)
    params = pltpu.CompilerParams(vmem_limit_bytes=24 * 1024 * 1024)
    sem, stage = pltpu.SemaphoreType.DMA((3,)), pltpu.VMEM((512, 1536), F32)
    halves = pl.pallas_call(
        unpack_mine_kernel,
        out_shape=matrices,
        in_specs=[smem, vmem],
        out_specs=[hbm] * 4,
        scratch_shapes=[stage, sem],
        compiler_params=params,
        cost_estimate=cost,
        name="unpack_mine",
    )(core, mine)
    return pl.pallas_call(
        unpack_other_kernel,
        out_shape=matrices + (shape(80, 512), shape(1, 512), shape(37, 512)),
        in_specs=[smem, smem, hbm, vmem] + [hbm] * 4,
        out_specs=[hbm] * 4 + [vmem] * 3,
        scratch_shapes=[
            stage, pltpu.VMEM((128, 512), F32), pltpu.VMEM((256, 128), BF16), sem, pltpu.SemaphoreType.DMA,
        ],
        input_output_aliases={4: 0, 5: 1, 6: 2, 7: 3},
        compiler_params=params,
        cost_estimate=cost,
        name="unpack_other",
    )(core, level_ids, mine, other, *halves)


def shards(
    latent, grad_fields, region_ids, level_ids, w_qkv, w_proj, gain, level_table, w_key, w_value, w_out
):
    core = lax.axis_index("core")
    tokens = latent.reshape(576, 512)
    fields = grad_fields.transpose(0, 2, 1, 3)
    out, keep, send = section(
        core.reshape(1, 1), level_ids, tokens, fields, fetch(tokens, fields), region_ids, level_table, w_qkv, w_proj,
        gain, w_key, w_value, w_out.T,
    )
    tile = out.reshape(12, 24, 2, 512)
    mine, other, d_latent = sum_all(keep, send, tile, send_back(tile))
    grad_qkv, grad_proj, grad_key, grad_value, out_t, grad_gain, table = unpack(core.reshape(1, 1), level_ids, mine, other)
    return d_latent, grad_qkv, grad_proj, grad_gain[0], table, grad_key, grad_value, out_t.T


def solution(mesh):
    fine = Mesh(mesh.devices.reshape(2, 2, 4, 4, 2), LAT + LON)
    tile = P(LAT, LON, None, None)
    return jax.shard_map(
        shards,
        mesh=fine,
        in_specs=(tile, tile, P(LAT, LON)) + (P(),) * 8,
        out_specs=(tile,) + (P(),) * 7,
        check_vma=False,
    )
```

```python
import functools
import jax
import jax.numpy as jnp
from jax import lax
from jax.experimental import pallas as pl
from jax.experimental.pallas import tpu as pltpu

HEADS = 8
WH = 6
WW = 12
LV = 2
SH = 3
SW = 6
EPS = 1e-05
MASKED = -1e30
F32 = jnp.float32
BF16 = jnp.bfloat16


def dot_nn(a, b):
    return lax.dot_general(a, b, (((1,), (0,)), ((), ())), preferred_element_type=F32)


def dot_nt(a, b):
    return lax.dot_general(a, b, (((1,), (1,)), ((), ())), preferred_element_type=F32)


def dot_tn(a, b):
    return lax.dot_general(a, b, (((0,), (0,)), ((), ())), preferred_element_type=F32)


def swap_rows(a):
    rows, lanes = a.shape
    blocks = a.reshape(rows // 8, 8, lanes)
    later = pltpu.roll(blocks, 7, 1)
    earlier = pltpu.roll(blocks, 1, 1)
    even = lax.broadcasted_iota(jnp.int32, blocks.shape, 1) % 2 == 0
    return jnp.where(even, later, earlier).reshape(rows, lanes)


def nine_tiles(levels):
    lane = lax.broadcasted_iota(jnp.int32, levels.shape[1:], 1)
    tiles = [levels[p] for p in range(9)]
    for m in range(4):
        extra = levels[9 + m]
        tiles[2 * m] = jnp.where(lane < 80, tiles[2 * m], pltpu.roll(extra, 80, 1))
        tiles[2 * m + 1] = jnp.where(lane < 80, tiles[2 * m + 1], pltpu.roll(extra, 32, 1))
    return jnp.stack(tiles, axis=0)


def all_levels(tiles):
    lane = lax.broadcasted_iota(jnp.int32, tiles.shape[1:], 1)
    levels = [tiles[p] for p in range(9)]
    for m in range(4):
        levels.append(
            jnp.where(lane < 48, pltpu.roll(tiles[2 * m], 48, 1), pltpu.roll(tiles[2 * m + 1], 96, 1))
        )
    return jnp.stack(levels, axis=0)[:, :, :80]


def row_of_tile():
    return lax.broadcasted_iota(jnp.int32, (8, 128), 0)


def side_tiles(line, levels):
    row = row_of_tile()
    tiles = [line[0:8, 128 * c:128 * c + 128] for c in range(4)]
    for m in range(2):
        left, right = (line[8:16, 128 * c:128 * c + 128] for c in (2 * m, 2 * m + 1))
        tiles.append(jnp.where(row < 4, left, pltpu.roll(right, 4, 0)))
    places = []
    for m in range(2):
        for i in range(3):
            places.append(jnp.where(row < 6, levels[4 * m + i], pltpu.roll(levels[4 * m + 3], 6 - 2 * i, 0)))
    return tiles, places + [levels[8]]


def side_levels(places):
    row = row_of_tile()
    out = []
    for m in range(2):
        first, second, third = places[3 * m:3 * m + 3]
        last = jnp.where(
            row < 2, pltpu.roll(first, 2, 0), jnp.where(row < 4, pltpu.roll(second, 4, 0), pltpu.roll(third, 6, 0))
        )
        out += [first, second, third, last]
    return jnp.stack(out + [places[6]], axis=0)


def pack_kernel(x_ref, f_ref, below_ref, right_ref, corner_ref, wide):
    row = row_of_tile()
    full, halves, lines, sides = [], [], [], ([], [])
    for h in range(12):
        wide[h, :, :, 0:80] = f_ref[h].astype(F32)
        line = x_ref[48 * h:48 * h + 48, :].astype(F32)
        tiles, places = side_tiles(line[0:16], nine_tiles(wide[h, :, 0:8, :]))
        sides[0].append(tiles)
        sides[1].append(places)
        if h < 3:
            for c in range(4):
                full += [line[8 * n:8 * n + 8, 128 * c:128 * c + 128] for n in range(2, 6)]
            for m in range(2):
                left, right = (line[8:16, 128 * c:128 * c + 128] for c in (2 * m, 2 * m + 1))
                halves.append(jnp.where(row < 4, pltpu.roll(right, 4, 0), left))
            levels = nine_tiles(wide[h])
            for k in range(9):
                lines += [levels[k, 8:16], levels[k, 16:24]]
            for q in range(2):
                four = [pltpu.roll(levels[4 * q + i, 0:8], (8 - 2 * i) % 8, 0) for i in range(4)]
                low = jnp.where(row < 2, four[3], four[2])
                lines.append(jnp.where(row < 4, low, jnp.where(row < 6, four[1], four[0])))
            lines.append(levels[8, 0:8])
    below_ref[...] = jnp.concatenate(full + halves + lines, axis=0).astype(BF16)
    right_ref[...] = jnp.concatenate(sum(sides[0][3:], []) + sum(sides[1][3:], []), axis=0).astype(BF16)
    corner_ref[...] = jnp.concatenate(sum(sides[0][:3], []) + sum(sides[1][:3], []), axis=0).astype(BF16)


def pack(x, fields):
    vmem = pl.BlockSpec(memory_space=pltpu.VMEM)
    return pl.pallas_call(
        pack_kernel,
        out_shape=tuple(jax.ShapeDtypeStruct((rows, 128), BF16) for rows in (936, 936, 312)),
        in_specs=[vmem, vmem],
        out_specs=[vmem] * 3,
        scratch_shapes=[pltpu.VMEM((12, 13, 24, 128), F32)],
        compiler_params=pltpu.CompilerParams(vmem_limit_bytes=16 * 1024 * 1024),
        cost_estimate=pl.CostEstimate(flops=2_000_000, bytes_accessed=3_000_000, transcendentals=0),
        name="pack",
    )(x, fields)


def section_kernel(
    core_ref, level_ref, x_ref, below_ref, right_ref, corner_ref, ids_ref, table_ref, gain_ref, wout_ref,
    wqkv_hbm, wproj_hbm, wkey_hbm, wval_hbm, f_hbm,
    out_hbm, keep_hbm, send_hbm,
    xw32, xw, pk, probs, at, nrm, inv, mix32, mixb, kk, vv, uu, ww, cc, ds, gg, dkd, dvd, dm32, dp32, dpb, dat, dpk, hs, at_t, x_t, hot, q32, qs, wo128, f_below, f_right, f_corner,
    wqkv_ref, wproj_ref, wkey_ref, wval_ref, f_ref, out_ref, grads_ref, in_sem, out_sem,
):
    n_win = 4
    tok = 144
    rows = 576
    core = core_ref[0, 0]
    loads = [
        pltpu.make_async_copy(source, target, in_sem.at[n])
        for n, (source, target) in enumerate(
            (
                (wqkv_hbm, wqkv_ref), (wproj_hbm, wproj_ref), (wkey_hbm, wkey_ref), (wval_hbm, wval_ref),
                (f_hbm, f_ref),
            )
        )
    ]
    for load in loads:
        load.start()

    def put(half_no, block, matrix):
        for c in range(matrix.shape[1] // 128):
            at_row = 512 * (block + c)
            piece = matrix[:, 128 * c:128 * c + 128].astype(BF16)
            grads_ref[half_no ^ core, at_row:at_row + 512, :] = piece

    lane = lax.broadcasted_iota(jnp.int32, (1, 128), 1)
    half = ((lane < 64).astype(BF16), (lane >= 64).astype(BF16))
    eighth = (half[0] * jnp.asarray(0.125, BF16), half[1] * jnp.asarray(0.125, BF16))
    low = lax.broadcasted_iota(jnp.int32, (tok, 128), 1) < 64
    gain = gain_ref[...]

    wide = table_ref[...].astype(F32)
    table_row = lax.broadcasted_iota(jnp.int32, wide.shape, 0)
    for p in range(13):
        q32[8 * p:8 * p + 8, :] = jnp.broadcast_to(
            jnp.sum(jnp.where(table_row == level_ref[p], wide, 0.0), axis=0, keepdims=True), (8, 512)
        )
    q32[104:128, :] = jnp.zeros((24, 512), F32)
    qs[...] = q32[...].astype(BF16)
    wo128[...] = jnp.zeros((512, 128), BF16)
    wo128[:, 0:80] = wout_ref[...].T

    ids = ids_ref[...].astype(F32)
    token = lax.broadcasted_iota(jnp.int32, (tok, 24), 0)
    spot = lax.broadcasted_iota(jnp.int32, (tok, 24), 1)
    tok12 = lax.broadcasted_iota(jnp.int32, (tok, 12), 0)
    row12 = lax.broadcasted_iota(jnp.int32, (tok, 12), 1)
    kind = lax.broadcasted_iota(jnp.int32, (tok, 128), 1).astype(F32)
    for w in range(n_win):
        pick = (tok12 // 24 + 6 * (w // 2) == row12).astype(F32)
        line = dot_nn(pick, ids)
        own_id = jnp.sum(
            jnp.where(spot == 12 * (w % 2) + (token % 24) // 2, line, 0.0), axis=1, keepdims=True
        )
        hot[w] = (own_id == kind).astype(BF16)

    row8 = row_of_tile()
    below = below_ref[...].astype(F32).reshape(117, 8, 128)
    right = right_ref[...].astype(F32).reshape(117, 8, 128)
    corner = corner_ref[...].astype(F32).reshape(39, 8, 128)
    for h in range(9):
        f_right[h] = side_levels([right[54 + 7 * h + n] for n in range(7)])
    for h in range(3):
        f_corner[h] = side_levels([corner[18 + 7 * h + n] for n in range(7)])
        for k in range(9):
            at_tile = 54 + 21 * h
            f_below[h, k, 0:8, :] = pltpu.roll(below[at_tile + 18 + k // 4], 2 * (k % 4), 0)
            f_below[h, k, 8:16, :] = below[at_tile + 2 * k]
            f_below[h, k, 16:24, :] = below[at_tile + 2 * k + 1]
    for h in range(12):
        side = right[6 * h:6 * h + 6] if h < 9 else corner[6 * (h - 9):6 * (h - 9) + 6]
        for c in range(4):
            cols = slice(128 * c, 128 * c + 128)
            if h < 9:
                main = x_ref[48 * (h + 3):48 * (h + 3) + 48, cols].astype(F32)
                line = [main[8 * n:8 * n + 8] for n in range(1, 6)]
            else:
                half_tile = below[48 + 2 * (h - 9) + c // 2]
                line = [half_tile if c % 2 == 0 else pltpu.roll(half_tile, 4, 0)]
                line += [below[16 * (h - 9) + 4 * c + n] for n in range(4)]
            half_tile = side[4 + c // 2]
            line += [side[c], half_tile if c % 2 == 0 else pltpu.roll(half_tile, 4, 0)]
            turned = [pltpu.roll(tile, 4, 0) for tile in line]
            piece = [jnp.where(row8 < 4, turned[n], turned[n + 1]) for n in range(6)]
            for b in range(2):
                xw32[(h // 6) * 2 + b, 24 * (h % 6):24 * (h % 6) + 24, cols] = jnp.concatenate(
                    piece[3 * b:3 * b + 3], axis=0
                )
    for w in range(n_win):
        xw[w] = xw32[w].astype(BF16)
    flat_x = xw[...].reshape(rows, 512)
    loads[0].wait()
    x_t[...] = flat_x.T
    for n in range(6):
        part = dot_nn(flat_x, wqkv_ref[:, 256 * n:256 * n + 256]).astype(BF16)
        pk[:, :, 256 * n:256 * n + 256] = part.reshape(n_win, tok, 256)

    def attend(w, carry):
        same = dot_nt(hot[w], hot[w])
        bias = (same - 1.0) * -MASKED
        for hp in range(4):
            cols = slice(128 * hp, 128 * hp + 128)
            q = pk[w, :, 128 * hp:128 * hp + 128]
            k = pk[w, :, 512 + 128 * hp:512 + 128 * hp + 128]
            v_t = pk[w, :, 1024 + 128 * hp:1024 + 128 * hp + 128].T
            outs = []
            both = dot_nt(jnp.concatenate([k * eighth[0], k * eighth[1]], axis=0), q)
            for e in range(2):
                s = both[tok * e:tok * e + tok] + bias
                p = jnp.exp(s - jnp.max(s, axis=0, keepdims=True))
                p = p * (1.0 / jnp.sum(p, axis=0, keepdims=True))
                probs[w, 2 * hp + e] = p
                outs.append(dot_nn(v_t[64 * e:64 * e + 64], p.astype(BF16)))
            o_t = jnp.concatenate(outs, axis=0).astype(BF16)
            at_t[w, cols, :] = o_t
            at[w, :, cols] = o_t.T
        return carry

    lax.fori_loop(0, n_win, attend, 0)

    flat_at = at[...].reshape(rows, 512)
    loads[1].wait()
    nrm[...] = dot_nn(flat_at, wproj_ref[...]).reshape(n_win, tok, 512)
    for w in range(n_win):
        for i in range(6):
            at_row = 48 * (6 * (w // 2) + i) + 24 * (w % 2)
            p = nrm[w, 24 * i:24 * i + 24, :]
            c = p - jnp.mean(p, axis=-1, keepdims=True)
            r = lax.rsqrt(jnp.mean(c * c, axis=-1, keepdims=True) + EPS)
            n = c * r
            nrm[w, 24 * i:24 * i + 24, :] = n
            inv[w, 24 * i:24 * i + 24, :] = jnp.broadcast_to(r, (24, 128))
            mix32[at_row:at_row + 24, :] = xw32[w, 24 * i:24 * i + 24, :] + n * gain
    mixb[...] = mix32[...].astype(BF16)

    mixed = mixb[...]
    for load in loads[2:]:
        load.wait()
    for hp in range(4):
        cols = slice(128 * hp, 128 * hp + 128)
        for w_ref, pair in ((wkey_ref, kk), (wval_ref, vv)):
            part = dot_nn(mixed, w_ref[:, cols]).astype(BF16)
            other = swap_rows(part.astype(F32))
            pair[hp, :, 0:128] = part
            pair[hp, :, 128:256] = (-other).astype(BF16)

    row16 = lax.broadcasted_iota(jnp.int32, (16, 128), 0)
    lane16 = lax.broadcasted_iota(jnp.int32, (16, 128), 1)
    own = (row16 // 2 == lane16 % 8).astype(F32)[None]
    zero64 = jnp.zeros((64, 128), BF16)
    for hp in range(4):
        cols = slice(128 * hp, 128 * hp + 128)
        q = qs[:, cols] * jnp.asarray(0.125, BF16)
        q_e, q_o = q * half[0], q * half[1]
        rhs = jnp.concatenate(
            [jnp.concatenate([q_e, q_e], axis=1), jnp.concatenate([q_o, q_o], axis=1)], axis=0
        )
        diff = dot_nt(kk[hp], rhs)
        wo = wo128[cols, :]
        top = jnp.concatenate(
            [jnp.concatenate([wo[:64], zero64], axis=0), jnp.concatenate([zero64, wo[64:]], axis=0)], axis=1
        )
        u = dot_nn(vv[hp], jnp.concatenate([top, top], axis=0)).astype(BF16)
        for e in range(2):
            d = diff[:, 128 * e:128 * e + 128].reshape(36, 16, 128)
            small = jnp.exp(-jnp.abs(d))
            big = 1.0 / (1.0 + small)
            small = small * big
            weight = jnp.where(d >= 0, big, small)
            ww[2 * hp + e] = (weight * own).astype(BF16).reshape(rows, 128)
            cc[2 * hp + e] = (small * big * (own * 0.125)).reshape(rows, 128)
            uu[2 * hp + e] = u[:, 128 * e:128 * e + 128]

    gg[...] = jnp.zeros((8, rows, 128), BF16)

    edge = lax.broadcasted_iota(jnp.int32, (13, 8, 80), 1) < 2

    def groups(h, tiles):
        turned = [pltpu.roll(tile, 2, 1) for tile in tiles]
        for o in range(3):
            g16 = pl.ds(pl.multiple_of(48 * h + 16 * o, 16), 16)
            f = jnp.where(edge, turned[o], turned[o + 1]).reshape(104, 80)
            f = jnp.concatenate([f, jnp.zeros((24, 80), F32)], axis=0).astype(BF16)
            dw = dot_nt(uu[:, g16, 0:80].reshape(128, 80), f)
            d = (dw * cc[:, g16, :].reshape(128, 128)).astype(BF16)
            ds[:, g16, :] = d.reshape(8, 16, 128)
            g = dot_nn(ww[:, g16, :].reshape(128, 128), f).astype(BF16)
            gg[:, g16, 0:80] = g.reshape(8, 16, 80)

    def near(h, carry):
        own = f_ref[h + 3].astype(F32)
        groups(h, [own[:, 0:8], own[:, 8:16], own[:, 16:24], all_levels(f_right[h])])
        return carry

    def far(h, carry):
        own = all_levels(f_below[h])
        groups(h + 9, [own[:, 0:8], own[:, 8:16], own[:, 16:24], all_levels(f_corner[h])])
        return carry

    lax.fori_loop(0, 9, near, 0, unroll=9)
    lax.fori_loop(0, 3, far, 0, unroll=3)

    fold_row = lax.broadcasted_iota(jnp.int32, (128, 128), 0)
    fold_lane = lax.broadcasted_iota(jnp.int32, (128, 128), 1)
    fold = (fold_row // 8 == fold_lane - 80).astype(BF16)
    for hp in range(4):
        cols = slice(128 * hp, 128 * hp + 128)
        q = qs[:, cols]
        d = jnp.concatenate([ds[2 * hp], ds[2 * hp + 1]], axis=1)
        g = jnp.concatenate([gg[2 * hp], gg[2 * hp + 1]], axis=1)
        dkd[:, cols] = dot_nn(d, jnp.concatenate([q * half[0], q * half[1]], axis=0)).astype(BF16)
        wo = wo128[cols, :]
        top = jnp.concatenate(
            [jnp.concatenate([wo[:64], zero64], axis=0), jnp.concatenate([zero64, wo[64:]], axis=0)], axis=1
        )
        dvd[:, cols] = dot_nt(g, top).astype(BF16)
        dq = dot_tn(kk[hp, :, 0:128], d)
        dq = jnp.concatenate([dq[:64, :128], dq[64:, 128:]], axis=0)
        go = dot_tn(vv[hp, :, 0:128], g)
        go = jnp.concatenate([go[:64, :128], go[64:, 128:]], axis=0)
        dq_hi = dq.astype(BF16)
        dq_lo = (dq - dq_hi.astype(F32)).astype(BF16)
        hs[:, cols] = go + dot_nn(dq_hi, fold) + dot_nn(dq_lo, fold)

    d_mix = dot_nt(dkd[...], wkey_ref[...]) + dot_nt(dvd[...], wval_ref[...])
    dm32[...] = d_mix.astype(BF16).astype(F32)
    mixed_t = mixed.T
    put(1, 4, dot_nn(mixed_t, dkd[...]))
    put(1, 8, dot_nn(mixed_t, dvd[...]))

    total_gain = jnp.zeros((8, 512), F32)
    for w in range(n_win):
        for i in range(6):
            at_row = 48 * (6 * (w // 2) + i) + 24 * (w % 2)
            g = dm32[at_row:at_row + 24, :]
            n = nrm[w, 24 * i:24 * i + 24, :]
            total_gain = total_gain + jnp.sum((g * n).reshape(3, 8, 512), axis=0)
            gn = g * gain
            m1 = jnp.mean(gn, axis=-1, keepdims=True)
            m2 = jnp.mean(gn * n, axis=-1, keepdims=True)
            r = inv[w, 24 * i:24 * i + 24, 0:1]
            dp32[w, 24 * i:24 * i + 24, :] = r * (gn - m1 - n * m2)
    row_gain = jnp.broadcast_to(jnp.sum(total_gain, axis=0, keepdims=True), (128, 512))
    for hp in range(4):
        cols = slice(128 * hp, 128 * hp + 128)
        column = row_gain[:, cols].T
        lanes = lax.broadcasted_iota(jnp.int32, (128, 128), 1)
        tail = jnp.where(lanes == 96, column, hs[:, cols]).astype(BF16)
        at_row = 6144 + 128 * (hp % 2)
        grads_ref[(hp // 2) ^ core, at_row:at_row + 128, :] = tail
    for half_no in range(2):
        grads_ref[half_no, 6400:6656, :] = jnp.zeros((256, 128), BF16)
    for w in range(n_win):
        dpb[w] = dp32[w].astype(BF16)
    flat_dp = dpb[...].reshape(rows, 512)
    total = dot_nn(at_t[0], dpb[0])
    for w in range(1, n_win):
        total = total + dot_nn(at_t[w], dpb[w])
    put(1, 0, total)
    dat[...] = dot_nt(flat_dp, wproj_ref[...]).astype(BF16).reshape(n_win, tok, 512)

    early_keep = pltpu.make_async_copy(grads_ref.at[0], keep_hbm, out_sem.at[0])
    early_send = pltpu.make_async_copy(grads_ref.at[1], send_hbm, out_sem.at[1])
    late_keep = pltpu.make_async_copy(grads_ref.at[0], keep_hbm, out_sem.at[2])
    late_send = pltpu.make_async_copy(grads_ref.at[1], send_hbm, out_sem.at[3])

    @pl.when(core == 1)
    def _():
        early_keep.start()

    @pl.when(core == 0)
    def _():
        early_send.start()

    def unattend(w, carry):
        for hp in range(4):
            cols = slice(128 * hp, 128 * hp + 128)
            q = pk[w, :, 128 * hp:128 * hp + 128]
            k_t = pk[w, :, 512 + 128 * hp:512 + 128 * hp + 128].T
            v = pk[w, :, 1024 + 128 * hp:1024 + 128 * hp + 128]
            da = dat[w, :, cols]
            both = dot_nt(jnp.concatenate([v * eighth[0], v * eighth[1]], axis=0), da)
            ps, ss, dqs = [], [], []
            for e in range(2):
                p = probs[w, 2 * hp + e]
                dw = both[tok * e:tok * e + tok]
                s = (p * (dw - jnp.sum(p * dw, axis=0, keepdims=True))).astype(BF16)
                ps.append(p.astype(BF16))
                ss.append(s)
                dqs.append(dot_nn(k_t[64 * e:64 * e + 64], s))
            dv = dot_nn(jnp.concatenate(ps, axis=0), da)
            dk = dot_nn(jnp.concatenate(ss, axis=0), q)
            dpk[w, :, cols] = jnp.concatenate(dqs, axis=0).astype(BF16).T
            dpk[w, :, 512 + 128 * hp:512 + 128 * hp + 128] = jnp.where(low, dk[:tok], dk[tok:]).astype(BF16)
            dpk[w, :, 1024 + 128 * hp:1024 + 128 * hp + 128] = jnp.where(low, dv[:tok], dv[tok:]).astype(BF16)
        return carry

    lax.fori_loop(0, n_win, unattend, 0)

    flat_d = dpk[...].reshape(rows, 1536)
    for n in range(3):
        put(0, 4 * n, dot_nn(x_t[...], flat_d[:, 512 * n:512 * n + 512]))

    @pl.when(core == 0)
    def _():
        late_keep.start()

    @pl.when(core == 1)
    def _():
        late_send.start()

    dp32[...] = dot_nt(flat_d, wqkv_ref[...]).reshape(n_win, tok, 512)
    for h in range(12):
        parts = []
        for b in range(2):
            at_row = 48 * h + 24 * b
            parts.append(
                dp32[(h // 6) * 2 + b, 24 * (h % 6):24 * (h % 6) + 24, :] + dm32[at_row:at_row + 24, :]
            )
        out_ref[48 * h:48 * h + 48, :] = jnp.concatenate(parts, axis=0).astype(BF16)
    result = pltpu.make_async_copy(out_ref, out_hbm, out_sem.at[4])
    result.start()

    @pl.when(core == 0)
    def _():
        early_send.wait()
        late_keep.wait()

    @pl.when(core == 1)
    def _():
        early_keep.wait()
        late_send.wait()

    result.wait()


def section(core, level_ids, x, fields, halo, ids, table, w_qkv, w_proj, gain, w_key, w_value, w_out):
    vm = lambda shape, kind: pltpu.VMEM(shape, kind)
    scratch = [
        vm((4, 144, 512), F32), vm((4, 144, 512), BF16), vm((4, 144, 1536), BF16), vm((4, 8, 144, 144), F32),
        vm((4, 144, 512), BF16), vm((4, 144, 512), F32), vm((4, 144, 128), F32), vm((576, 512), F32),
        vm((576, 512), BF16), vm((4, 576, 256), BF16), vm((4, 576, 256), BF16), vm((8, 576, 128), BF16),
        vm((8, 576, 128), BF16), vm((8, 576, 128), F32), vm((8, 576, 128), BF16), vm((8, 576, 128), BF16),
        vm((576, 512), BF16), vm((576, 512), BF16), vm((576, 512), F32), vm((4, 144, 512), F32),
        vm((4, 144, 512), BF16), vm((4, 144, 512), BF16), vm((4, 144, 1536), BF16), vm((128, 512), F32),
        vm((4, 512, 144), BF16), vm((512, 576), BF16), vm((4, 144, 128), BF16), vm((128, 512), F32),
        vm((128, 512), BF16), vm((512, 128), BF16), vm((3, 9, 24, 128), F32), vm((9, 9, 8, 128), F32),
        vm((3, 9, 8, 128), F32),
        vm((512, 1536), BF16), vm((512, 512), BF16), vm((512, 512), BF16), vm((512, 512), BF16),
        vm((12, 13, 24, 80), BF16), vm((576, 512), BF16), vm((2, 6656, 128), BF16),
        pltpu.SemaphoreType.DMA((5,)), pltpu.SemaphoreType.DMA((5,)),
    ]
    smem, vmem = pl.BlockSpec(memory_space=pltpu.SMEM), pl.BlockSpec(memory_space=pltpu.VMEM)
    hbm = pl.BlockSpec(memory_space=pl.ANY)
    half = jax.ShapeDtypeStruct((6656, 128), BF16)
    return pl.pallas_call(
        section_kernel,
        out_shape=(jax.ShapeDtypeStruct((576, 512), BF16), half, half),
        in_specs=[smem, smem] + [vmem] * 8 + [hbm] * 5,
        out_specs=[hbm] * 3,
        scratch_shapes=scratch,
        compiler_params=pltpu.CompilerParams(vmem_limit_bytes=52 * 1024 * 1024),
        cost_estimate=pl.CostEstimate(flops=15_000_000_000, bytes_accessed=12_000_000, transcendentals=2_000_000),
        name="section",
    )(core, level_ids, x, *halo, ids, table, gain[None], w_out, w_qkv, w_proj, w_key, w_value, fields)


from jax.sharding import Mesh, PartitionSpec as P

LAT = ("z_hi", "core")
LON = ("x", "y", "z_lo")
CHIPS = ("z_hi", "x", "y", "z_lo")


def neighbours(axes, by):
    count = 1
    for axis in axes:
        count *= lax.axis_size(axis)
    return [(i, (i + by) % count) for i in range(count)]


def corner_pairs(by):
    n_lat, n_lon = 4, 32
    return [
        (a * n_lon + b, ((a + by) % n_lat) * n_lon + (b + by) % n_lon) for a in range(n_lat) for b in range(n_lon)
    ]


def fetch(tokens, fields):
    below, right, corner = pack(tokens, fields)
    return (
        lax.ppermute(below, LAT, neighbours(LAT, -1)),
        lax.ppermute(right, LON, neighbours(LON, -1)),
        lax.ppermute(corner, LAT + LON, corner_pairs(-1)),
    )


def send_back(tile):
    h, w = tile.shape[0], tile.shape[1]
    above = lax.ppermute(tile[h - SH:, :w - SW], LAT, neighbours(LAT, 1))
    left = lax.ppermute(tile[:h - SH, w - SW:], LON, neighbours(LON, 1))
    corner = lax.ppermute(tile[h - SH:, w - SW:], LAT + LON, corner_pairs(1))
    return above, left, corner


def place_back(tile, above, left, corner):
    h, w = tile.shape[0], tile.shape[1]
    top = jnp.concatenate([corner, above], axis=1)
    bottom = jnp.concatenate([left, tile[:h - SH, :w - SW]], axis=1)
    return jnp.concatenate([top, bottom], axis=0)


def sum_all(keep, send, tile, sent):
    swap = [(0, 1), (1, 0)]
    other = lax.ppermute(send, "core", swap)
    mine = (keep.astype(F32) + other.astype(F32)).astype(BF16)
    pieces = lax.all_to_all(mine.reshape(64, 104, 128), CHIPS, split_axis=0, concat_axis=0, tiled=True)
    piece = jnp.sum(pieces.astype(F32), axis=0).astype(BF16)
    spread = jnp.broadcast_to(piece[None], (64, 104, 128))
    mine = lax.all_to_all(spread, CHIPS, split_axis=0, concat_axis=0, tiled=True).reshape(6656, 128)
    other = lax.ppermute(mine, "core", swap)
    return mine, other, place_back(tile, *sent)


def spread_half(is_first, half_ref, targets, stage, sem):
    qkv_hbm, squares = targets[0], targets[1:]

    def copies(n, act):
        cols = slice(512 * n, 512 * n + 512)

        @pl.when(is_first)
        def _():
            act(pltpu.make_async_copy(stage.at[:, cols], qkv_hbm.at[:, cols], sem.at[n]))

        @pl.when(jnp.logical_not(is_first))
        def _():
            act(pltpu.make_async_copy(stage.at[:, cols], squares[n], sem.at[n]))

    for n in range(3):
        for block in range(4 * n, 4 * n + 4):
            stage[:, 128 * block:128 * block + 128] = half_ref[512 * block:512 * block + 512, :].astype(F32)
        copies(n, lambda copy: copy.start())
    return lambda: [copies(n, lambda copy: copy.wait()) for n in range(3)]


def unpack_mine_kernel(core_ref, mine_ref, qkv_hbm, proj_hbm, key_hbm, value_hbm, stage, sem):
    finish = spread_half(core_ref[0, 0] == 0, mine_ref, (qkv_hbm, proj_hbm, key_hbm, value_hbm), stage, sem)
    finish()


def unpack_other_kernel(
    core_ref, level_ref, mine_hbm, other_ref, qkv_in, proj_in, key_in, value_in,
    qkv_hbm, proj_hbm, key_hbm, value_hbm, out_ref, gain_ref, table_ref, stage, tail_ref, mine_ref, sem, mine_sem,
):
    first = core_ref[0, 0] == 0
    fetch_tail = pltpu.make_async_copy(mine_hbm.at[6144:6400], mine_ref, mine_sem)
    fetch_tail.start()
    finish = spread_half(
        jnp.logical_not(first), other_ref, (qkv_hbm, proj_hbm, key_hbm, value_hbm), stage, sem
    )
    fetch_tail.wait()
    for hp in range(4):
        at_row = 128 * (hp % 2)
        mine, other = mine_ref[at_row:at_row + 128, :], other_ref[6144 + at_row:6144 + at_row + 128, :]
        chosen = jnp.where(first, mine, other) if hp < 2 else jnp.where(first, other, mine)
        tail_ref[:, 128 * hp:128 * hp + 128] = chosen.astype(F32).T
    out_ref[...] = tail_ref[0:80, :]
    gain_ref[...] = tail_ref[96:97, :]
    row = lax.broadcasted_iota(jnp.int32, (37, 512), 0)
    table = jnp.zeros((37, 512), F32)
    for p in range(13):
        table = table + jnp.where(row == level_ref[p], tail_ref[80 + p:81 + p, :], 0.0)
    table_ref[...] = table
    finish()


def unpack(core, level_ids, mine, other):
    shape = lambda *dims: jax.ShapeDtypeStruct(dims, F32)
    smem, vmem = pl.BlockSpec(memory_space=pltpu.SMEM), pl.BlockSpec(memory_space=pltpu.VMEM)
    hbm = pl.BlockSpec(memory_space=pl.ANY)
    matrices = (shape(512, 1536), shape(512, 512), shape(512, 512), shape(512, 512))
    cost = pl.CostEstimate(flops=3_000_000, bytes_accessed=6_000_000, transcendentals=0)
    params = pltpu.CompilerParams(vmem_limit_bytes=24 * 1024 * 1024)
    sem, stage = pltpu.SemaphoreType.DMA((3,)), pltpu.VMEM((512, 1536), F32)
    halves = pl.pallas_call(
        unpack_mine_kernel,
        out_shape=matrices,
        in_specs=[smem, vmem],
        out_specs=[hbm] * 4,
        scratch_shapes=[stage, sem],
        compiler_params=params,
        cost_estimate=cost,
        name="unpack_mine",
    )(core, mine)
    return pl.pallas_call(
        unpack_other_kernel,
        out_shape=matrices + (shape(80, 512), shape(1, 512), shape(37, 512)),
        in_specs=[smem, smem, hbm, vmem] + [hbm] * 4,
        out_specs=[hbm] * 4 + [vmem] * 3,
        scratch_shapes=[
            stage, pltpu.VMEM((128, 512), F32), pltpu.VMEM((256, 128), BF16), sem, pltpu.SemaphoreType.DMA,
        ],
        input_output_aliases={4: 0, 5: 1, 6: 2, 7: 3},
        compiler_params=params,
        cost_estimate=cost,
        name="unpack_other",
    )(core, level_ids, mine, other, *halves)


def shards(
    latent, grad_fields, region_ids, level_ids, w_qkv, w_proj, gain, level_table, w_key, w_value, w_out
):
    core = lax.axis_index("core")
    tokens = latent.reshape(576, 512)
    fields = grad_fields.transpose(0, 2, 1, 3)
    out, keep, send = section(
        core.reshape(1, 1), level_ids, tokens, fields, fetch(tokens, fields), region_ids, level_table, w_qkv, w_proj,
        gain, w_key, w_value, w_out.T,
    )
    tile = out.reshape(12, 24, 2, 512)
    mine, other, d_latent = sum_all(keep, send, tile, send_back(tile))
    grad_qkv, grad_proj, grad_key, grad_value, out_t, grad_gain, table = unpack(core.reshape(1, 1), level_ids, mine, other)
    return d_latent, grad_qkv, grad_proj, grad_gain[0], table, grad_key, grad_value, out_t.T


def solution(mesh):
    fine = Mesh(mesh.devices.reshape(2, 2, 4, 4, 2), LAT + LON)
    tile = P(LAT, LON, None, None)
    return jax.shard_map(
        shards,
        mesh=fine,
        in_specs=(tile, tile, P(LAT, LON)) + (P(),) * 8,
        out_specs=(tile,) + (P(),) * 7,
        check_vma=False,
    )
```
